32 devices in a mesh: dp: 4 (over y, core), fsdp: 8 (over z, x).
Axes of the slice: x: 2, y: 2, z: 4, core: 2. Of those that a mesh axis runs over, the one named last changes fastest.
Arguments:
- tokens: bfloat16 [16384, 768], P(('dp', 'fsdp')), may hold values from -8 to 8
- doc_lengths: int32 [32], P(('dp', 'fsdp')), may hold values from 128 to 512, as said below
- w_query: bfloat16 [768, 768], P('dp', 'fsdp'), may hold values from -0.21875 to 0.21875
- w_key: bfloat16 [768, 768], P('dp', 'fsdp'), may hold values from -0.21875 to 0.21875
- w_value: bfloat16 [768, 768], P('dp', 'fsdp'), may hold values from -0.21875 to 0.21875
- w_query2: bfloat16 [768, 768], P('dp', 'fsdp'), may hold values from -1.75 to 1.75
- w_key2: bfloat16 [768, 768], P('dp', 'fsdp'), may hold values from -0.21875 to 0.21875
- w_value2: bfloat16 [768, 768], P('dp', 'fsdp'), may hold values from -0.21875 to 0.21875
- w_out: bfloat16 [768, 768], P('dp', 'fsdp'), may hold values from -1.25 to 1.25
- w_up: bfloat16 [768, 3072], P('dp', 'fsdp'), may hold values from -0.21875 to 0.21875
- w_down: bfloat16 [3072, 768], P('dp', 'fsdp'), may hold values from -0.109375 to 0.109375
- norm_gains: float32 [2, 768], replicated, may hold values from 0.5 to 1.5
- norm_shifts: float32 [2, 768], replicated, may hold values from -3 to 3
- pool_kernels: float32 [2, 5, 768], replicated, may hold values from -2.5 to 2.5
- out_grad: bfloat16 [16384, 768], P(('dp', 'fsdp')), may hold values from -8 to 8
Outputs:
- activations: bfloat16 [16384, 768], P(('dp', 'fsdp'))
- input_grad: bfloat16 [16384, 768], P(('dp', 'fsdp'))
- grad_w_query: float32 [768, 768], P('dp', 'fsdp')
- grad_w_key: float32 [768, 768], P('dp', 'fsdp')
- grad_w_value: float32 [768, 768], P('dp', 'fsdp')
- grad_w_query2: float32 [768, 768], P('dp', 'fsdp')
- grad_w_key2: float32 [768, 768], P('dp', 'fsdp')
- grad_w_value2: float32 [768, 768], P('dp', 'fsdp')
- grad_w_out: float32 [768, 768], P('dp', 'fsdp')
- grad_w_up: float32 [768, 3072], P('dp', 'fsdp')
- grad_w_down: float32 [3072, 768], P('dp', 'fsdp')
- grad_gains: float32 [2, 768], replicated
- grad_shifts: float32 [2, 768], replicated
- grad_pools: float32 [2, 5, 768], replicated
The draws below stay inside these ranges and needn't reach their ends.
Inputs may be any that keep to these rules, and one draw needn't show every extreme that they name: `doc_lengths`: every entry is a multiple of 128; some entry equals 512.
All inputs are finite; a program needn't handle non-finite values.
Results may differ from the reference program's by a relative error of at most 0.038.
The reference program's roundings to bfloat16 on the way count: a program that leaves them out, or rounds other values in their place, can miss the bound.
Values may be sent and summed in bfloat16 or wider, within the bound.
A program may use at most 192 MiB of HBM per device.

```python
import math
import jax
import jax.numpy as jnp
from jax import lax

D = 768
HEADS = 12
HD = 64
FF = 3072
WIN = 128
PWIN = 512
POOLK = 5
STRIDE = 4
PAD_UNIT = 128
SEQ = 512
DOCS = 32
TOKENS = 16384


def draw_doc_lengths(key, part):
    units_key, full_key = jax.random.split(key)
    blocks = jax.random.randint(units_key, (DOCS,), 1, SEQ // PAD_UNIT + 1)
    chosen = jax.random.randint(full_key, (), 0, DOCS)
    blocks = jnp.where(jnp.arange(DOCS) == chosen, SEQ // PAD_UNIT, blocks)
    return (blocks * PAD_UNIT).astype(jnp.int32)


def drawn_rows(key):
    value_key, scale_key = jax.random.split(key)
    values = jnp.clip(jax.random.normal(value_key, (TOKENS, D), jnp.float32), -4.0, 4.0)
    seq_scale = jnp.exp(jax.random.uniform(scale_key, (DOCS, 1, 1), jnp.float32, math.log(0.5), math.log(2.0)))
    values = (values.reshape(DOCS, SEQ, D) * seq_scale).reshape(TOKENS, D)
    return values.astype(jnp.bfloat16)


def draw_tokens(key, part):
    return drawn_rows(jax.random.fold_in(key, 11))


def draw_out_grad(key, part):
    return drawn_rows(jax.random.fold_in(key, 23))


def shard_levels(rng, extent, cuts, least, high):
    factor_of = 1.0
    for axis_at, parts in cuts:
        draws = jax.random.uniform(jax.random.fold_in(jax.random.fold_in(rng, 6), axis_at), (parts,), jnp.float32, least / len(cuts), high / len(cuts))
        factor_of = factor_of * jnp.repeat(jnp.exp(draws), extent[axis_at] // parts).reshape((-1,) + (1,) * (len(extent) - 1 - axis_at))
    return factor_of


def noise(stream_key, dims, width, most, cuts=(), kind=jnp.bfloat16):
    values = width * jax.random.normal(stream_key, dims, jnp.float32)
    if cuts:
        values = values * shard_levels(stream_key, dims, cuts, -0.22, 0.18)
    return jnp.clip(values, -most, most).astype(kind)


def setup_inputs(seed: int = 0) -> dict:
    splits = jax.random.split(jax.random.key(seed), 16)
    tokens = draw_tokens(jax.random.fold_in(splits[15], 71), 0)
    doc_lengths = draw_doc_lengths(jax.random.fold_in(splits[15], 71), 0)
    w_query = noise(splits[2], (D, D), D ** -0.5, 0.21875, ((0, 4), (1, 8)))
    w_key = noise(splits[3], (D, D), D ** -0.5, 0.21875, ((0, 4), (1, 8)))
    w_value = noise(splits[4], (D, D), D ** -0.5, 0.21875, ((0, 4), (1, 8)))
    w_query2 = noise(splits[5], (D, D), (max(D // 64, 1)) ** -0.5, 1.75, ((0, 4), (1, 8)))
    w_key2 = noise(splits[6], (D, D), D ** -0.5, 0.21875, ((0, 4), (1, 8)))
    w_value2 = noise(splits[7], (D, D), D ** -0.5, 0.21875, ((0, 4), (1, 8)))
    w_out = noise(splits[8], (D, D), (max(D // 32, 1)) ** -0.5, 1.25, ((0, 4), (1, 8)))
    w_up = noise(splits[9], (D, FF), D ** -0.5, 0.21875, ((0, 4), (1, 8)))
    w_down = noise(splits[10], (FF, D), FF ** -0.5, 0.109375, ((0, 4), (1, 8)))
    norm_gains = jnp.clip(1.0 + 0.1 * jax.random.normal(splits[11], (2, D), jnp.float32), 0.5, 1.5)
    norm_shifts = noise(splits[12], (2, D), 0.5, 3.0, (), jnp.float32)
    pool_kernels = noise(splits[13], (2, POOLK, D), POOLK ** -0.5, 2.5, (), jnp.float32)
    out_grad = draw_out_grad(jax.random.fold_in(splits[15], 71), 0)
    return dict(tokens=tokens, doc_lengths=doc_lengths, w_query=w_query, w_key=w_key, w_value=w_value, w_query2=w_query2, w_key2=w_key2, w_value2=w_value2, w_out=w_out, w_up=w_up, w_down=w_down, norm_gains=norm_gains, norm_shifts=norm_shifts, pool_kernels=pool_kernels, out_grad=out_grad)


@jax.custom_vjp
def low(v):
    return lax.optimization_barrier(v.astype(jnp.bfloat16)).astype(jnp.float32)

@jax.custom_vjp
def low_back(v):
    return v

def low_keep(v):
    return (low(v), None)

def low_pass(kept, grad):
    return (grad,)

def back_keep(v):
    return (v, None)

def back_low(kept, grad):
    return (low(grad),)
low.defvjp(low_keep, low_pass)
low_back.defvjp(back_keep, back_low)

def matmul(left_mat, right_mat):
    return jnp.dot(left_mat, right_mat, precision=lax.Precision.HIGHEST, preferred_element_type=jnp.float32)

def layer_norm(inputs, norm_gain, norm_shift):
    average = lax.optimization_barrier(jnp.mean(inputs, axis=-1, keepdims=True))
    centred = inputs - average
    variance = lax.optimization_barrier(jnp.mean(centred * centred, axis=-1, keepdims=True))
    return centred * lax.rsqrt(variance + 1e-05) * norm_gain + norm_shift

def pool_rows(inputs, kernel):
    side_rows = (kernel.shape[0] - 1) // 2
    pooled_rows = inputs.shape[0] // STRIDE
    padded = jnp.pad(inputs, ((side_rows, side_rows), (0, 0)))
    summed = jnp.zeros((pooled_rows, inputs.shape[1]), inputs.dtype)
    for offset in range(kernel.shape[0]):
        summed = summed + kernel[offset] * padded[offset:offset + inputs.shape[0]:STRIDE]
    return summed

def attend(query, keys, values, allowed):
    raw_scores = jnp.einsum('ihd,jhd->hij', query, keys, precision=lax.Precision.HIGHEST) * (1.0 / math.sqrt(HD))
    scores = low_back(jnp.where(allowed[None], raw_scores, -1e+30))
    highest = lax.optimization_barrier(jnp.max(scores, axis=-1, keepdims=True))
    expo_terms = jnp.exp(scores - highest)
    soft_weights = expo_terms / lax.optimization_barrier(jnp.sum(expo_terms, axis=-1, keepdims=True))
    return jnp.einsum('hij,jhd->ihd', low(soft_weights), values, precision=lax.Precision.HIGHEST)

def by_heads(matrix):
    return matrix.reshape(matrix.shape[0], HEADS, HD)

def forward(inputs, length, w_query, w_key, w_value, w_query2, w_key2, w_value2, w_out, w_up, w_down, norm_gains, norm_shifts, pool_kernels):
    positions = jnp.arange(SEQ, dtype=jnp.int32)
    padding = positions >= length
    allowed_one = (jnp.abs(positions[:, None] - positions[None, :]) <= WIN) & (padding[:, None] == padding[None, :])
    pooled_at = positions[:SEQ // STRIDE] * STRIDE
    allowed_two = (jnp.abs(positions[:, None] - pooled_at[None, :]) <= PWIN // 2) & (padding[:, None] == (pooled_at >= length)[None, :])
    query = low_back(low(matmul(inputs, w_query)))
    keys = low_back(low(matmul(inputs, w_key)))
    values = low_back(low(matmul(inputs, w_value)))
    key_two = low_back(matmul(inputs, w_key2))
    value_two = low_back(matmul(inputs, w_value2))
    key_pool = low_back(low(pool_rows(key_two, pool_kernels[0])))
    value_pool = low_back(low(pool_rows(value_two, pool_kernels[1])))
    first = low_back(low(attend(by_heads(query), by_heads(keys), by_heads(values), allowed_one).reshape(SEQ, D)))
    query_two = low_back(low(matmul(first, w_query2)))
    second = low_back(attend(by_heads(query_two), by_heads(key_pool), by_heads(value_pool), allowed_two).reshape(SEQ, D))
    mixed = low(first + second)
    branch = low_back(matmul(mixed, w_out))
    hidden = layer_norm(inputs + branch, norm_gains[0], norm_shifts[0])
    upper = low_back(matmul(low(hidden), w_up))
    activated = low(jax.nn.gelu(upper, approximate=True))
    ffn_out = low_back(matmul(activated, w_down))
    return layer_norm(hidden + ffn_out, norm_gains[1], norm_shifts[1])

def reference(tokens, doc_lengths, w_query, w_key, w_value, w_query2, w_key2, w_value2, w_out, w_up, w_down, norm_gains, norm_shifts, pool_kernels, out_grad):
    params = tuple((param.astype(jnp.float32) for param in (w_query, w_key, w_value, w_query2, w_key2, w_value2, w_out, w_up, w_down, norm_gains, norm_shifts, pool_kernels)))
    sequences = tokens.astype(jnp.float32).reshape(DOCS, SEQ, D)
    cotangents = out_grad.astype(jnp.float32).reshape(DOCS, SEQ, D)

    def one_sequence(running, inputs_now):
        seq_inputs, length, cotangent = inputs_now

        def closed(layer_inputs, *weights):
            return forward(layer_inputs, length, *weights)
        result, pullback = jax.vjp(closed, seq_inputs, *params)
        gradients = pullback(cotangent)
        running = tuple((running_sum + gradient for running_sum, gradient in zip(running, gradients[1:])))
        return (running, (result.astype(jnp.bfloat16), gradients[0].astype(jnp.bfloat16)))
    initial = tuple((jnp.zeros_like(param) for param in params))
    totals, outputs = lax.scan(one_sequence, initial, (sequences, doc_lengths.astype(jnp.int32), cotangents))
    return (outputs[0].reshape(TOKENS, D), outputs[1].reshape(TOKENS, D), totals[0], totals[1], totals[2], totals[3], totals[4], totals[5], totals[6], totals[7], totals[8], totals[9], totals[10], totals[11])
```

```python
import math

import jax
import jax.numpy as jnp
from jax import lax
from jax.experimental import pallas as pl
from jax.experimental.pallas import tpu as pltpu
from jax.sharding import PartitionSpec as P

HEADS = 12
HD = 64
WIN = 128
PWIN = 512
STRIDE = 4


def matmul(left_mat, right_mat):
    return jnp.dot(left_mat, right_mat, preferred_element_type=jnp.float32)


def inner_rows(left_mat, right_mat):
    return lax.dot_general(
        left_mat, right_mat, (((0,), (0,)), ((), ())), preferred_element_type=jnp.float32
    )


def outer_cols(left_mat, right_mat):
    return lax.dot_general(
        left_mat, right_mat, (((1,), (1,)), ((), ())), preferred_element_type=jnp.float32
    )


def layer_norm(inputs, norm_gain, norm_shift):
    average = jnp.mean(inputs, axis=-1, keepdims=True)
    centred = inputs - average
    variance = jnp.mean(centred * centred, axis=-1, keepdims=True)
    return centred * lax.rsqrt(variance + 1e-05) * norm_gain + norm_shift


def gelu_tanh(inputs):
    return jax.nn.gelu(inputs, approximate=True)


def pool_rows(inputs, kernel):
    side_rows = (kernel.shape[0] - 1) // 2
    pooled_rows = inputs.shape[0] // STRIDE
    padded = jnp.pad(inputs, ((side_rows, side_rows), (0, 0)))
    summed = jnp.zeros((pooled_rows, inputs.shape[1]), jnp.float32)
    for offset in range(kernel.shape[0]):
        summed = summed + kernel[offset] * padded[offset : offset + inputs.shape[0] : STRIDE]
    return summed


def split_heads(matrix):
    return matrix.reshape(matrix.shape[0], HEADS // 2, 2, HD).transpose(1, 0, 2, 3)


def join_heads(groups):
    return groups.transpose(1, 0, 2, 3).reshape(groups.shape[1], HEADS * HD)


def masked_scores(query, keys, allowed, score_scale):
    raw_scores = (
        jnp.einsum("ihd,jhd->hij", query, keys, preferred_element_type=jnp.float32) * score_scale
    )
    return jnp.where(allowed[None], raw_scores, -1e30)


def attend_forward(query, keys, values, allowed, score_scale):
    scores = masked_scores(query, keys, allowed, score_scale)
    highest = jnp.max(scores, axis=-1, keepdims=True)
    expo_terms = jnp.exp(scores - highest)
    summed = jnp.sum(expo_terms, axis=-1, keepdims=True)
    soft_weights = (expo_terms / summed).astype(jnp.bfloat16)
    result = jnp.einsum("hij,jhd->ihd", soft_weights, values, preferred_element_type=jnp.float32)
    return (result, (highest + jnp.log(summed))[..., 0])


def attend_backward(query, keys, values, allowed, score_scale, log_total, grad_result):
    scores = masked_scores(query, keys, allowed, score_scale)
    soft_weights = jnp.exp(scores - log_total[..., None])
    grad_soft = jnp.einsum("ihd,jhd->hij", grad_result, values, preferred_element_type=jnp.float32)
    grad_values = jnp.einsum(
        "hij,ihd->jhd",
        soft_weights.astype(jnp.bfloat16),
        grad_result,
        preferred_element_type=jnp.float32,
    )
    row_terms = jnp.sum(soft_weights * grad_soft, axis=-1, keepdims=True)
    grad_scores = (soft_weights * (grad_soft - row_terms)).astype(jnp.bfloat16)
    grad_query = (
        jnp.einsum("hij,jhd->ihd", grad_scores, keys, preferred_element_type=jnp.float32)
        * score_scale
    )
    grad_keys = (
        jnp.einsum("hij,ihd->jhd", grad_scores, query, preferred_element_type=jnp.float32)
        * score_scale
    )
    return (grad_query, grad_keys, grad_values)


def level_forward(query, keys, values, allowed, score_scale):

    def one_group(group_parts):
        return attend_forward(group_parts[0], group_parts[1], group_parts[2], allowed, score_scale)

    results, log_totals = lax.map(
        one_group, (split_heads(query), split_heads(keys), split_heads(values))
    )
    return (join_heads(results), log_totals)


def level_backward(query, keys, values, allowed, score_scale, log_totals, grad_result):

    def one_group(group_parts):
        return attend_backward(
            group_parts[0],
            group_parts[1],
            group_parts[2],
            allowed,
            score_scale,
            group_parts[3],
            group_parts[4],
        )

    grad_query, grad_keys, grad_values = lax.map(
        one_group,
        (
            split_heads(query),
            split_heads(keys),
            split_heads(values),
            log_totals,
            split_heads(grad_result),
        ),
    )
    return (join_heads(grad_query), join_heads(grad_keys), join_heads(grad_values))


def gather_first(shards):
    column_parts = (
        lax.all_gather(shards[0], "fsdp", axis=1, tiled=True),
        lax.all_gather(shards[1], "fsdp", axis=1, tiled=True),
        lax.all_gather(shards[2], "fsdp", axis=1, tiled=True),
        lax.all_gather(shards[3], "fsdp", axis=1, tiled=True),
        lax.all_gather(shards[4], "fsdp", axis=1, tiled=True),
        lax.all_gather(shards[5], "fsdp", axis=1, tiled=True),
        lax.all_gather(shards[6], "fsdp", axis=1, tiled=True),
        lax.all_gather(shards[7], "fsdp", axis=1, tiled=True),
        lax.all_gather(shards[8], "fsdp", axis=1, tiled=True),
    )
    return (
        lax.all_gather(column_parts[0], "dp", axis=0, tiled=True),
        lax.all_gather(column_parts[1], "dp", axis=0, tiled=True),
        lax.all_gather(column_parts[2], "dp", axis=0, tiled=True),
        lax.all_gather(column_parts[3], "dp", axis=0, tiled=True),
        lax.all_gather(column_parts[4], "dp", axis=0, tiled=True),
        lax.all_gather(column_parts[5], "dp", axis=0, tiled=True),
        lax.all_gather(column_parts[6], "dp", axis=0, tiled=True),
        lax.all_gather(column_parts[7], "dp", axis=0, tiled=True),
        lax.all_gather(column_parts[8], "dp", axis=0, tiled=True),
    )


def gather_second(shards):
    column_parts = (
        lax.all_gather(shards[0], "fsdp", axis=1, tiled=True),
        lax.all_gather(shards[1], "fsdp", axis=1, tiled=True),
        lax.all_gather(shards[2], "fsdp", axis=1, tiled=True),
        lax.all_gather(shards[3], "fsdp", axis=1, tiled=True),
        lax.all_gather(shards[4], "fsdp", axis=1, tiled=True),
        lax.all_gather(shards[5], "fsdp", axis=1, tiled=True),
        lax.all_gather(shards[6], "fsdp", axis=1, tiled=True),
        lax.all_gather(shards[7], "fsdp", axis=1, tiled=True),
        lax.all_gather(shards[8], "fsdp", axis=1, tiled=True),
    )
    return (
        lax.all_gather(column_parts[0], "dp", axis=0, tiled=True),
        lax.all_gather(column_parts[1], "dp", axis=0, tiled=True),
        lax.all_gather(column_parts[2], "dp", axis=0, tiled=True),
        lax.all_gather(column_parts[3], "dp", axis=0, tiled=True),
        lax.all_gather(column_parts[4], "dp", axis=0, tiled=True),
        lax.all_gather(column_parts[5], "dp", axis=0, tiled=True),
        lax.all_gather(column_parts[6], "dp", axis=0, tiled=True),
        lax.all_gather(column_parts[7], "dp", axis=0, tiled=True),
        lax.all_gather(column_parts[8], "dp", axis=0, tiled=True),
    )


def reduce_columns_first(grads_all):
    column_sums = (
        lax.psum_scatter(
            grads_all[0].astype(jnp.bfloat16), "fsdp", scatter_dimension=1, tiled=True
        ).astype(jnp.float32),
        lax.psum_scatter(
            grads_all[1].astype(jnp.bfloat16), "fsdp", scatter_dimension=1, tiled=True
        ).astype(jnp.float32),
        lax.psum_scatter(
            grads_all[2].astype(jnp.bfloat16), "fsdp", scatter_dimension=1, tiled=True
        ).astype(jnp.float32),
        lax.psum_scatter(
            grads_all[3].astype(jnp.bfloat16), "fsdp", scatter_dimension=1, tiled=True
        ).astype(jnp.float32),
        lax.psum_scatter(
            grads_all[4].astype(jnp.bfloat16), "fsdp", scatter_dimension=1, tiled=True
        ).astype(jnp.float32),
        lax.psum_scatter(
            grads_all[5].astype(jnp.bfloat16), "fsdp", scatter_dimension=1, tiled=True
        ).astype(jnp.float32),
        lax.psum_scatter(
            grads_all[6].astype(jnp.bfloat16), "fsdp", scatter_dimension=1, tiled=True
        ).astype(jnp.float32),
        lax.psum_scatter(
            grads_all[7].astype(jnp.bfloat16), "fsdp", scatter_dimension=1, tiled=True
        ).astype(jnp.float32),
        lax.psum_scatter(
            grads_all[8].astype(jnp.bfloat16), "fsdp", scatter_dimension=1, tiled=True
        ).astype(jnp.float32),
    )
    return (
        lax.psum_scatter(
            column_sums[0].astype(jnp.bfloat16), "dp", scatter_dimension=0, tiled=True
        ).astype(jnp.float32),
        lax.psum_scatter(
            column_sums[1].astype(jnp.bfloat16), "dp", scatter_dimension=0, tiled=True
        ).astype(jnp.float32),
        lax.psum_scatter(
            column_sums[2].astype(jnp.bfloat16), "dp", scatter_dimension=0, tiled=True
        ).astype(jnp.float32),
        lax.psum_scatter(
            column_sums[3].astype(jnp.bfloat16), "dp", scatter_dimension=0, tiled=True
        ).astype(jnp.float32),
        lax.psum_scatter(
            column_sums[4].astype(jnp.bfloat16), "dp", scatter_dimension=0, tiled=True
        ).astype(jnp.float32),
        lax.psum_scatter(
            column_sums[5].astype(jnp.bfloat16), "dp", scatter_dimension=0, tiled=True
        ).astype(jnp.float32),
        lax.psum_scatter(
            column_sums[6].astype(jnp.bfloat16), "dp", scatter_dimension=0, tiled=True
        ).astype(jnp.float32),
        lax.psum_scatter(
            column_sums[7].astype(jnp.bfloat16), "dp", scatter_dimension=0, tiled=True
        ).astype(jnp.float32),
        lax.psum_scatter(
            column_sums[8].astype(jnp.bfloat16), "dp", scatter_dimension=0, tiled=True
        ).astype(jnp.float32),
    )


MESH = pl.DeviceIdType.MESH
BF = jnp.bfloat16
F32 = jnp.float32
SQUARE = ((0, 3), (3, 5), (5, 7))
GROUPS = (0, 1, 2, 3, 4)


class Place:
    def __init__(self):
        dp = lax.axis_index("dp")
        fs = lax.axis_index("fsdp")
        self.y = lax.div(dp, 2)
        self.c = lax.rem(dp, 2)
        self.z = lax.div(fs, 2)
        self.x = lax.rem(fs, 2)
        c, x, y = self.c, self.x, self.y
        self.p1 = ((1 - c) * (1 - x) + c * x, (1 - c) * y + c * (1 - y))
        self.p2 = ((1 - c) * x + c * (1 - x), (1 - c) * (1 - y) + c * y)
        self.own = (x, y)
        self.diag = (1 - x, 1 - y)

    def dev(self, xy, z=None, c=None):
        z = self.z if z is None else z
        c = self.c if c is None else c
        return (xy[1] * 2 + c, z * 2 + xy[0])

    def peer(self, k):
        return lax.rem(self.z + k, 4)

    def everyone(self):
        return [
            self.dev(self.own, c=1 - self.c),
            self.dev(self.p1),
            self.dev(self.p2),
            self.dev(self.own, z=self.peer(1)),
            self.dev(self.own, z=self.peer(2)),
            self.dev(self.own, z=self.peer(3)),
        ]


def greet(me):
    bar = pltpu.get_barrier_semaphore()
    for d in me.everyone():
        pl.semaphore_signal(bar, inc=1, device_id=d, device_id_type=MESH)
    pl.semaphore_wait(bar, 6)


def quad(refs, g, xy, c, z=None):
    sq, up, down = refs
    x, y = xy
    zz = slice(None) if z is None else z
    if g < 3:
        lo, hi = SQUARE[g]
        return sq.at[lo:hi, zz, x, c, :, pl.ds(pl.multiple_of(y * 384, 128), 384)]
    if g == 3:
        return up.at[y, c, zz, x]
    return down.at[zz, x, :, pl.ds(pl.multiple_of((y * 2 + c) * 768, 128), 768)]


def rcopy(src, dst, ssem, rsem, dev):
    return pltpu.make_async_remote_copy(
        src_ref=src, dst_ref=dst, send_sem=ssem, recv_sem=rsem, device_id=dev, device_id_type=MESH
    )


class Gather:
    def __init__(self, me, refs, ssem, rsem):
        self.me, self.refs, self.ssem, self.rsem = me, refs, ssem, rsem

    def zcopy(self, g, k, incoming):
        me = self.me
        z = lax.rem(me.z + 4 - k, 4) if incoming else me.z
        b = quad(self.refs, g, me.own, me.c, z)
        return rcopy(b, b, self.ssem.at[g, k - 1], self.rsem.at[g, k - 1], me.dev(me.own, z=me.peer(k)))

    def qcopy(self, g, i, incoming):
        me = self.me
        what = {3: (me.own, me.p1), 4: (me.own, me.p2), 5: (me.p1, me.diag)}[i][1 if incoming else 0]
        b = quad(self.refs, g, what, me.c)
        return rcopy(b, b, self.ssem.at[g, i], self.rsem.at[g, i], me.dev(me.p1 if i == 3 else me.p2))

    def scopy(self, g, i, incoming):
        me = self.me
        what = {
            6: (me.own, me.own),
            7: (me.p1, me.p2),
            8: (me.p2, me.p1),
            9: (me.diag, me.diag),
        }[i][1 if incoming else 0]
        b = quad(self.refs, g, what, (1 - me.c) if incoming else me.c)
        return rcopy(b, b, self.ssem.at[g, i], self.rsem.at[g, i], me.dev(me.own, c=1 - me.c))

    def start(self, g):
        for k in (1, 2, 3):
            self.zcopy(g, k, False).start()

    def step1(self, g):
        for k in (1, 2, 3):
            self.zcopy(g, k, True).wait_recv()
        self.qcopy(g, 3, False).start()
        self.qcopy(g, 4, False).start()
        self.scopy(g, 6, False).start()

    def step2(self, g):
        self.qcopy(g, 3, True).wait_recv()
        self.qcopy(g, 5, False).start()
        self.scopy(g, 7, False).start()

    def step3(self, g):
        self.qcopy(g, 4, True).wait_recv()
        self.scopy(g, 8, False).start()

    def step4(self, g):
        self.qcopy(g, 5, True).wait_recv()
        self.scopy(g, 9, False).start()

    def arrived(self, g):
        for i in (6, 7, 8, 9):
            self.scopy(g, i, True).wait_recv()

    def sent(self, g):
        for k in (1, 2, 3):
            self.zcopy(g, k, False).wait_send()
        for i in (3, 4, 5):
            self.qcopy(g, i, False).wait_send()
        for i in (6, 7, 8, 9):
            self.scopy(g, i, False).wait_send()


def place_own(me, shards, sq, up, down, contrib, sib, ssem, rsem):
    rows = lax.broadcasted_iota(jnp.int32, (192, 384), 0)
    lanes = lax.broadcasted_iota(jnp.int32, (192, 384), 1)
    spot = jnp.where(lanes == rows + me.c * 192, 1.0, 0.0).astype(BF)
    for m in range(7):
        t = lax.dot_general(shards[m][...], spot, (((0,), (0,)), ((), ())), preferred_element_type=F32)
        t = t.astype(BF)
        contrib[m, 0] = t[:48]
        contrib[m, 1] = t[48:]
    swap = rcopy(contrib.at[:, 1 - me.c], sib, ssem.at[0], rsem.at[0], me.dev(me.own, c=1 - me.c))
    swap.start()
    up[me.y, me.c, me.z, me.x] = shards[7][...]
    eye_r = lax.broadcasted_iota(jnp.int32, (96, 96), 0)
    eye_c = lax.broadcasted_iota(jnp.int32, (96, 96), 1)
    eye = jnp.where(eye_r == eye_c, 1.0, 0.0).astype(BF)
    t = lax.dot_general(eye, shards[8][...], (((1,), (1,)), ((), ())), preferred_element_type=F32)
    down[me.z, me.x, :, pl.ds(pl.multiple_of((me.y * 2 + me.c) * 768, 128), 768)] = t.astype(BF)
    swap.wait()
    for m in range(7):
        both = contrib[m, me.c].astype(F32) + sib[m].astype(F32)
        sq[m, me.z, me.x, me.c, :, pl.ds(pl.multiple_of(me.y * 384, 128), 384)] = both.astype(BF)


class Scatter:
    def __init__(self, me, refs, sib, r1, r2, r3, ssem, rsem):
        self.me, self.refs, self.sib = me, refs, sib
        self.r1, self.r2, self.r3 = r1, r2, r3
        self.ssem, self.rsem = ssem, rsem

    def sib_view(self, g, xy, z=None):
        sq, up, down = self.sib
        x, y = xy
        zz = slice(None) if z is None else z
        if g < 3:
            lo, hi = SQUARE[g]
            return sq.at[lo:hi, zz, x, :, pl.ds(pl.multiple_of(y * 384, 128), 384)]
        if g == 3:
            return up.at[y, zz, x]
        return down.at[zz, x, :, pl.ds(pl.multiple_of(y * 768, 128), 768)]

    def slot(self, bufs, g, i):
        sq, up, down = bufs
        if g < 3:
            lo, hi = SQUARE[g]
            return sq.at[i, lo:hi]
        return (up if g == 3 else down).at[i]

    def copy(self, g, i):
        me = self.me
        ss, rs = self.ssem.at[g, i], self.rsem.at[g, i]
        if i < 4:
            what = (me.p1, me.diag, me.p2, me.own)[i]
            return rcopy(
                quad(self.refs, g, what, 1 - me.c), self.sib_view(g, what), ss, rs, me.dev(me.own, c=1 - me.c)
            )
        if i < 6:
            what = (me.diag, me.p2)[i - 4]
            return rcopy(quad(self.refs, g, what, me.c), self.slot(self.r1, g, i - 4), ss, rs, me.dev(me.p2))
        if i == 6:
            return rcopy(quad(self.refs, g, me.p1, me.c), self.slot(self.r2, g, 0), ss, rs, me.dev(me.p1))
        k = i - 6
        return rcopy(
            quad(self.refs, g, me.own, me.c, me.peer(k)),
            self.slot(self.r3, g, k - 1),
            ss,
            rs,
            me.dev(me.own, z=me.peer(k)),
        )

    def add(self, g, xy, other):
        here = quad(self.refs, g, xy, self.me.c)
        here[...] = (here[...].astype(F32) + other[...].astype(F32)).astype(BF)

    def start(self, g):
        for i in range(4):
            self.copy(g, i).start()

    def step1(self, g):
        me = self.me
        for i, what in ((1, me.diag), (0, me.p2)):
            self.copy(g, i).wait_recv()
            self.add(g, what, self.sib_view(g, what))
            self.copy(g, 4 if i == 1 else 5).start()

    def step2(self, g):
        me = self.me
        self.copy(g, 2).wait_recv()
        self.add(g, me.p1, self.sib_view(g, me.p1))
        self.copy(g, 4).wait_recv()
        self.add(g, me.p1, self.slot(self.r1, g, 0))
        self.copy(g, 6).start()

    def step3(self, g):
        me = self.me
        self.copy(g, 3).wait_recv()
        self.add(g, me.own, self.sib_view(g, me.own))
        self.copy(g, 5).wait_recv()
        self.add(g, me.own, self.slot(self.r1, g, 1))
        self.copy(g, 6).wait_recv()
        self.add(g, me.own, self.slot(self.r2, g, 0))
        for k in (1, 2, 3):
            self.copy(g, 6 + k).start()

    def finish(self, g):
        me = self.me
        total = quad(self.refs, g, me.own, me.c, me.z)[...].astype(F32)
        for k in (1, 2, 3):
            self.copy(g, 6 + k).wait_recv()
            total = total + self.slot(self.r3, g, k - 1)[...].astype(F32)
        return total

    def sent(self, g):
        for i in range(10):
            self.copy(g, i).wait_send()


GAIN, SHIFT, POOL = 0, 2, 4


def dg(a, b, ca, cb):
    return lax.dot_general(a, b, (((ca,), (cb,)), ((), ())), preferred_element_type=F32)


def weight(r, m):
    return r.sq[m].reshape(768, 768)


def weight_up(r, j):
    left = r.up[:, :, j, 0].reshape(768, 384)
    right = r.up[:, :, j, 1].reshape(768, 384)
    return jnp.concatenate([left, right], axis=1)


def down_lanes(j):
    return pl.ds(pl.multiple_of(j * 768, 128), 768)


def weight_down(r, j):
    return r.down[:, :, :, down_lanes(j)].reshape(768, 768)


def set_masks(r, length):
    for i in range(2):
        row = lax.broadcasted_iota(jnp.int32, (256, 384), 0) + 256 * i
        col = lax.broadcasted_iota(jnp.int32, (256, 384), 1) + 128 * i
        ok = (jnp.abs(row - col) <= WIN) & ((row >= length) == (col >= length))
        r.bias1[i] = jnp.where(ok, 0.0, -1e30)
    row = lax.broadcasted_iota(jnp.int32, (512, 128), 0)
    col = lax.broadcasted_iota(jnp.int32, (512, 128), 1) * STRIDE
    ok = (jnp.abs(row - col) <= PWIN // 2) & ((row >= length) == (col >= length))
    r.bias2[...] = jnp.where(ok, 0.0, -1e30)


def low_lanes(rows):
    return lax.broadcasted_iota(jnp.int32, (rows, 128), 1) < HD


def two_heads(pair):
    low = low_lanes(pair.shape[0])
    zero = jnp.zeros_like(pair)
    return jnp.concatenate([jnp.where(low, pair, zero), jnp.where(low, zero, pair)], axis=0)


def side_by_side(stacked):
    n = stacked.shape[0] // 2
    return jnp.where(low_lanes(n), stacked[:n], stacked[n:])


def pair_lanes(p):
    return pl.ds(pl.multiple_of(p * 128, 128), 128)


def softmax_out(scores, bias, values, lse_ref, p):
    scores = scores + jnp.concatenate([bias, bias], axis=0)
    highest = jnp.max(scores, axis=-1, keepdims=True)
    terms = jnp.exp(scores - highest)
    summed = jnp.sum(terms, axis=-1, keepdims=True)
    probs = (terms * (1.0 / summed)).astype(BF)
    lane = lax.broadcasted_iota(jnp.int32, lse_ref.shape, 1)
    lse_ref[...] = jnp.where(lane == p, highest + jnp.log(summed), lse_ref[...])
    return side_by_side(dg(probs, values, 1, 0))


def scores_of(query, keys):
    scaled = two_heads(query * jnp.asarray(0.125, BF))
    return scaled, dg(scaled, keys, 1, 1)


def softmax_back(scores, bias, lse_ref, p, grad, values):
    scores = scores + jnp.concatenate([bias, bias], axis=0)
    lane = lax.broadcasted_iota(jnp.int32, lse_ref.shape, 1)
    lse = jnp.sum(jnp.where(lane == p, lse_ref[...], 0.0), axis=-1, keepdims=True)
    probs = jnp.exp(scores - lse)
    grad_probs = dg(grad, values, 1, 1)
    row_terms = jnp.sum(probs * grad_probs, axis=-1, keepdims=True)
    return probs.astype(BF), (probs * (grad_probs - row_terms)).astype(BF)


def project(r, m):
    r.qkv[m] = dg(r.tokens[...], weight(r, m), 1, 1).astype(BF)


def project_pool(r, i):
    full = dg(r.tokens[...], weight(r, 3 + i), 1, 1)
    for l in range(6):
        lanes = slice(l * 128, l * 128 + 128)
        r.kt[i, l, 0:8] = jnp.zeros((8, 128), F32)
        r.kt[i, l, 520:528] = jnp.zeros((8, 128), F32)
        r.kt[i, l, 8:520] = full[:, lanes]
        total = None
        for t in range(5):
            term = r.pool[i, t : t + 1, lanes] * r.kt[i, l, pl.ds(6 + t, 128, stride=STRIDE), :]
            total = term if total is None else total + term
        r.kp[i, :, lanes] = total.astype(BF)


def level_one(r):
    @pl.loop(0, HEADS // 2)
    def _(p):
        lanes = pair_lanes(p)
        for i in range(2):
            rows, cols = pl.ds(256 * i, 256), pl.ds(128 * i, 384)
            _, scores = scores_of(r.qkv[0, rows, lanes], r.qkv[1, cols, lanes])
            out = softmax_out(scores, r.bias1[i], r.qkv[2, cols, lanes], r.lse1.at[i], p)
            r.first[rows, lanes] = out.astype(BF)


def level_two(r):
    r.q2[...] = dg(r.first[...], weight(r, 5), 1, 1).astype(BF)

    @pl.loop(0, HEADS // 2)
    def _(p):
        lanes = pair_lanes(p)
        _, scores = scores_of(r.q2[:, lanes], r.kp[0, :, lanes])
        out = softmax_out(scores, r.bias2[...], r.kp[1, :, lanes], r.lse2, p)
        r.mixed[:, lanes] = (r.first[:, lanes].astype(F32) + out).astype(BF)


def norm_parts(x):
    average = jnp.mean(x, axis=-1, keepdims=True)
    centred = x - average
    inverse = lax.rsqrt(jnp.mean(centred * centred, axis=-1, keepdims=True) + 1e-05)
    return centred * inverse, inverse


def norm_back(n, inverse, gain, grad):
    scaled = grad * gain
    return (
        scaled - jnp.mean(scaled, axis=-1, keepdims=True) - n * jnp.mean(scaled * n, axis=-1, keepdims=True)
    ) * inverse


def first_norm(r):
    r.acc[...] = dg(r.mixed[...], weight(r, 6), 1, 1)

    @pl.loop(0, 4)
    def _(i):
        rows = pl.ds(pl.multiple_of(i * 128, 128), 128)
        n, inverse = norm_parts(r.tokens[rows].astype(F32) + r.acc[rows])
        r.n1[rows] = n
        r.inv1[rows] = inverse
        r.hlow[rows] = (n * r.gains[0:1] + r.shifts[0:1]).astype(BF)


def ffn_up(r, j):
    u = dg(r.hlow[...], weight_up(r, j), 1, 0)
    k = math.sqrt(2.0 / math.pi)
    square = u * u
    t = jnp.tanh(k * u * (1.0 + 0.044715 * square))
    half = 0.5 * (1.0 + t)
    r.act[j] = (u * half).astype(BF)
    slope = half + (0.5 * k) * u * (1.0 - t * t) * (1.0 + (3 * 0.044715) * square)
    r.gd[j] = slope.astype(BF)


def ffn_down_norm(r):
    for i in range(2):
        rows = pl.ds(256 * i, 256)
        total = dg(r.act[0, rows], weight_down(r, 0), 1, 1)
        for j in range(1, 4):
            total = total + dg(r.act[j, rows], weight_down(r, j), 1, 1)
        r.acc[rows] = total

    r.vec[...] = jnp.zeros_like(r.vec)

    @pl.loop(0, 4)
    def _(i):
        rows = pl.ds(pl.multiple_of(i * 128, 128), 128)
        hidden = r.n1[rows] * r.gains[0:1] + r.shifts[0:1]
        n, inverse = norm_parts(hidden + r.acc[rows])
        r.out[rows] = (n * r.gains[1:2] + r.shifts[1:2]).astype(BF)
        grad = r.og[rows].astype(F32)
        r.vec[GAIN + 1 : GAIN + 2] += jnp.sum(grad * n, axis=0, keepdims=True)
        r.vec[SHIFT + 1 : SHIFT + 2] += jnp.sum(grad, axis=0, keepdims=True)
        d = norm_back(n, inverse, r.gains[1:2], grad)
        r.dr[rows] = d
        r.dlow[rows] = d.astype(BF)


def back_upper(r, j):
    t = dg(r.dlow[...], weight_down(r, j), 1, 0)
    r.gd[j] = (r.gd[j].astype(F32) * t).astype(BF)


def grad_down(r, j):
    g = dg(r.dlow[...], r.act[j], 0, 0).astype(BF)
    r.down[:, :, :, down_lanes(j)] = g.reshape(4, 2, 96, 768)


def back_first_norm(r):
    for i in range(2):
        rows = pl.ds(256 * i, 256)
        total = r.dr[rows]
        for j in range(4):
            total = total + dg(r.gd[j, rows], weight_up(r, j), 1, 1)
        r.acc[rows] = total

    @pl.loop(0, 4)
    def _(i):
        rows = pl.ds(pl.multiple_of(i * 128, 128), 128)
        grad = r.acc[rows]
        n = r.n1[rows]
        r.vec[GAIN : GAIN + 1] += jnp.sum(grad * n, axis=0, keepdims=True)
        r.vec[SHIFT : SHIFT + 1] += jnp.sum(grad, axis=0, keepdims=True)
        d = norm_back(n, r.inv1[rows], r.gains[0:1], grad)
        r.dr[rows] = d
        r.dlow[rows] = d.astype(BF)


def grad_up(r, j):
    g = dg(r.hlow[...], r.gd[j], 0, 0).astype(BF)
    for x in range(2):
        r.up[:, :, j, x] = g[:, x * 384 : (x + 1) * 384].reshape(2, 2, 192, 384)


def set_grad(r, m, left, right):
    r.sq[m] = dg(left, right, 0, 0).astype(BF).reshape(4, 2, 2, 48, 768)


def back_out(r):
    r.acc[...] = dg(r.dlow[...], weight(r, 6), 1, 0)
    set_grad(r, 6, r.dlow[...], r.mixed[...])


def back_level_two(r):
    @pl.loop(0, HEADS // 2)
    def _(p):
        lanes = pair_lanes(p)
        scaled, scores = scores_of(r.q2[:, lanes], r.kp[0, :, lanes])
        grad = two_heads(r.acc[:, lanes].astype(BF))
        probs, grad_scores = softmax_back(scores, r.bias2[...], r.lse2, p, grad, r.kp[1, :, lanes])
        r.dpool[1, 0:128, lanes] = dg(probs, grad, 0, 0).astype(BF).astype(F32)
        r.dpool[0, 0:128, lanes] = dg(grad_scores, scaled, 0, 0).astype(BF).astype(F32)
        r.dq2[:, lanes] = (side_by_side(dg(grad_scores, r.kp[0, :, lanes], 1, 0)) * 0.125).astype(BF)

    r.dfirst[...] = (r.acc[...] + dg(r.dq2[...], weight(r, 5), 1, 0)).astype(BF)
    set_grad(r, 5, r.dq2[...], r.first[...])


def back_pool(r, i):
    r.dpool[i, 128:136] = jnp.zeros((8, 768), F32)
    for l in range(6):
        lanes = slice(l * 128, l * 128 + 128)
        here = r.dpool[i, 0:128, lanes]
        after = r.dpool[i, 1:129, lanes]
        for t in range(5):
            term = here * r.kt[i, l, pl.ds(6 + t, 128, stride=STRIDE), :]
            at = POOL + 5 * i + t
            r.vec[at : at + 1, lanes] = jnp.sum(term, axis=0, keepdims=True)
        k = [r.pool[i, t : t + 1, lanes] for t in range(5)]
        r.kt[i, l, pl.ds(8, 128, stride=STRIDE), :] = k[2] * here
        r.kt[i, l, pl.ds(9, 128, stride=STRIDE), :] = k[3] * here
        r.kt[i, l, pl.ds(10, 128, stride=STRIDE), :] = k[4] * here + k[0] * after
        r.kt[i, l, pl.ds(11, 128, stride=STRIDE), :] = k[1] * after
    grad = jnp.concatenate([r.kt[i, l, 8:520].astype(BF) for l in range(6)], axis=1)
    finish_projection(r, 3 + i, grad)


def finish_projection(r, m, grad):
    r.dr[...] = r.dr[...] + dg(grad, weight(r, m), 1, 0)
    set_grad(r, m, grad, r.tokens[...])


def back_level_one(r):
    @pl.loop(0, HEADS // 2)
    def _(p):
        lanes = pair_lanes(p)
        keys, vals = [], []
        for i in range(2):
            rows, cols = pl.ds(256 * i, 256), pl.ds(128 * i, 384)
            scaled, scores = scores_of(r.qkv[0, rows, lanes], r.qkv[1, cols, lanes])
            grad = two_heads(r.dfirst[rows, lanes])
            probs, grad_scores = softmax_back(
                scores, r.bias1[i], r.lse1.at[i], p, grad, r.qkv[2, cols, lanes]
            )
            vals.append(dg(probs, grad, 0, 0))
            keys.append(dg(grad_scores, scaled, 0, 0))
            dq = side_by_side(dg(grad_scores, r.qkv[1, cols, lanes], 1, 0)) * 0.125
            r.dqkv[0, rows, lanes] = dq.astype(BF)
        for at, parts in ((1, keys), (2, vals)):
            r.dqkv[at, 0:128, lanes] = parts[0][:128].astype(BF)
            r.dqkv[at, 128:384, lanes] = (parts[0][128:] + parts[1][:256]).astype(BF)
            r.dqkv[at, 384:512, lanes] = parts[1][256:].astype(BF)


class Refs:
    pass


ACTIVE = dict(
    qkv=((3, 512, 768), BF),
    kt=((2, 6, 528, 128), F32),
    kp=((2, 128, 768), BF),
    dpool=((2, 136, 768), F32),
    first=((512, 768), BF),
    q2=((512, 768), BF),
    mixed=((512, 768), BF),
    n1=((512, 768), F32),
    inv1=((512, 1), F32),
    hlow=((512, 768), BF),
    act=((4, 512, 768), BF),
    gd=((4, 512, 768), BF),
    dr=((512, 768), F32),
    acc=((512, 768), F32),
    dlow=((512, 768), BF),
    lse1=((2, 512, 128), F32),
    lse2=((1024, 128), F32),
    bias1=((2, 256, 384), F32),
    bias2=((512, 128), F32),
)


def alias_late(r):
    r.dq2 = r.act.at[0]
    r.dfirst = r.act.at[1]
    r.dqkv = r.gd


def gather_kernel(*refs):
    shards = refs[:9]
    outs = refs[9:12]
    sq, up, down, contrib, sib, psem, qsem, ssem, rsem, osem = refs[12:]
    me = Place()
    greet(me)
    place_own(me, shards, sq, up, down, contrib, sib, psem, qsem)
    gat = Gather(me, (sq, up, down), ssem, rsem)
    for g in GROUPS:
        gat.start(g)
    for s in range(len(GROUPS) + 3):
        if s < 5:
            gat.step1(s)
        if 0 <= s - 1 < 5:
            gat.step2(s - 1)
        if 0 <= s - 2 < 5:
            gat.step3(s - 2)
        if 0 <= s - 3 < 5:
            gat.step4(s - 3)
    for g in GROUPS:
        gat.arrived(g)
    copies = [
        pltpu.make_async_copy(a, b, osem.at[i]) for i, (a, b) in enumerate(zip((sq, up, down), outs))
    ]
    for cp in copies:
        cp.start()
    for g in GROUPS:
        gat.sent(g)
    for cp in copies:
        cp.wait()


SQ = (7, 4, 2, 2, 48, 768)
UP = (2, 2, 4, 2, 192, 384)
DOWN = (4, 2, 96, 3072)


def gather(shards):
    return pl.pallas_call(
        gather_kernel,
        out_shape=[jax.ShapeDtypeStruct(s, BF) for s in (SQ, UP, DOWN)],
        in_specs=[pl.BlockSpec(memory_space=pltpu.VMEM)] * 9,
        out_specs=[pl.BlockSpec(memory_space=pl.ANY)] * 3,
        scratch_shapes=[
            pltpu.VMEM(SQ, BF),
            pltpu.VMEM(UP, BF),
            pltpu.VMEM(DOWN, BF),
            pltpu.VMEM((7, 2, 48, 384), BF),
            pltpu.VMEM((7, 48, 384), BF),
            pltpu.SemaphoreType.DMA((1,)),
            pltpu.SemaphoreType.DMA((1,)),
            pltpu.SemaphoreType.DMA((5, 10)),
            pltpu.SemaphoreType.DMA((5, 10)),
            pltpu.SemaphoreType.DMA((3,)),
        ],
        compiler_params=pltpu.CompilerParams(
            collective_id=0, has_side_effects=True, vmem_limit_bytes=56 * 2**20
        ),
    )(*shards)


def vector_sum(me, vec, vbuf, vsem, wsem):
    hops = [me.dev(me.own, c=1 - me.c), me.dev((1 - me.x, me.y)), me.dev((me.x, 1 - me.y))]
    for i, d in enumerate(hops):
        vbuf[i] = vec[...]
        cp = rcopy(vbuf.at[i], vbuf.at[3 + i], vsem.at[i], wsem.at[i], d)
        cp.start()
        cp.wait()
        vec[...] = vec[...] + vbuf[3 + i]
    vbuf[6 + me.z] = vec[...]
    cps = [
        rcopy(
            vbuf.at[6 + me.z], vbuf.at[6 + me.z], vsem.at[2 + k], wsem.at[2 + k], me.dev(me.own, z=me.peer(k))
        )
        for k in (1, 2, 3)
    ]
    for cp in cps:
        cp.start()
    for k in (1, 2, 3):
        zz = lax.rem(me.z + 4 - k, 4)
        rcopy(
            vbuf.at[6 + zz], vbuf.at[6 + zz], vsem.at[2 + k], wsem.at[2 + k], me.dev(me.own, z=me.peer(k))
        ).wait_recv()
    for cp in cps:
        cp.wait_send()
    vec[...] = (vbuf[6] + vbuf[7]) + (vbuf[8] + vbuf[9])


def scatter_kernel(*refs):
    sq, up, down, vec_in = refs[:4]
    o_sq, o_up, o_down, o_vec = refs[4:8]
    s_sq, s_up, s_down = refs[8:11]
    r1 = refs[11:14]
    r2 = refs[14:17]
    r3 = refs[17:20]
    ssem, rsem, esem, vbuf, vsem, wsem, half = refs[20:]
    me = Place()
    greet(me)
    sca = Scatter(me, (sq, up, down), (s_sq, s_up, s_down), r1, r2, r3, ssem, rsem)
    order = (4, 3, 2, 1, 0)
    for g in order:
        sca.start(g)
    for s in range(8):
        if s < 5:
            sca.step1(order[s])
        if 0 <= s - 1 < 5:
            sca.step2(order[s - 1])
        if 0 <= s - 2 < 5:
            sca.step3(order[s - 2])
        if 0 <= s - 3 < 5:
            g = order[s - 3]
            total = sca.finish(g)
            if g == 3:
                o_up[...] = total
            elif g == 4:
                o_down[...] = total
            else:
                lo, hi = SQUARE[g]
                half[lo:hi] = total
    o_vec[...] = vec_in[...]
    vector_sum(me, o_vec, vbuf, vsem, wsem)
    swap = rcopy(half, o_sq.at[:, me.c], esem.at[0], esem.at[1], me.dev(me.own, c=1 - me.c))
    swap.start()
    o_sq[:, me.c] = half[...]
    swap.wait_send()
    rcopy(half, o_sq.at[:, 1 - me.c], esem.at[0], esem.at[1], me.dev(me.own, c=1 - me.c)).wait_recv()
    for g in GROUPS:
        sca.sent(g)


def scatter(sq, up, down, vec):
    def slots(n):
        return [
            pltpu.VMEM((n, 7, 4, 48, 384), BF),
            pltpu.VMEM((n, 4, 192, 384), BF),
            pltpu.VMEM((n, 4, 96, 768), BF),
        ]

    return pl.pallas_call(
        scatter_kernel,
        out_shape=[
            jax.ShapeDtypeStruct((7, 2, 48, 384), F32),
            jax.ShapeDtypeStruct((192, 384), F32),
            jax.ShapeDtypeStruct((96, 768), F32),
            jax.ShapeDtypeStruct(vec.shape, F32),
        ],
        in_specs=[pl.BlockSpec(memory_space=pltpu.VMEM)] * 4,
        out_specs=[pl.BlockSpec(memory_space=pltpu.VMEM)] * 4,
        scratch_shapes=[
            pltpu.VMEM((7, 4, 2, 48, 768), BF),
            pltpu.VMEM((2, 4, 2, 192, 384), BF),
            pltpu.VMEM((4, 2, 96, 1536), BF),
            *slots(2),
            *slots(1),
            pltpu.VMEM((3, 7, 48, 384), BF),
            pltpu.VMEM((3, 192, 384), BF),
            pltpu.VMEM((3, 96, 768), BF),
            pltpu.SemaphoreType.DMA((5, 10)),
            pltpu.SemaphoreType.DMA((5, 10)),
            pltpu.SemaphoreType.DMA((2,)),
            pltpu.VMEM((10, *vec.shape), F32),
            pltpu.SemaphoreType.DMA((6,)),
            pltpu.SemaphoreType.DMA((6,)),
            pltpu.VMEM((7, 48, 384), F32),
        ],
        compiler_params=pltpu.CompilerParams(
            collective_id=1, has_side_effects=True, vmem_limit_bytes=60 * 2**20
        ),
    )(sq, up, down, vec)


def compute_kernel(*refs):
    r = Refs()
    (length, r.tokens, r.og, r.gains, r.shifts, r.pool, sq_in, up_in, down_in) = refs[:9]
    (r.out, r.din, r.vec, sq_out, up_out, down_out) = refs[9:15]
    r.sq, r.up, r.down = refs[15:18]
    sem = refs[18]
    for name, ref in zip(ACTIVE, refs[19:]):
        setattr(r, name, ref)
    alias_late(r)
    loads = [pltpu.make_async_copy(a, b, sem.at[i]) for i, (a, b) in enumerate(((sq_in, r.sq), (up_in, r.up), (down_in, r.down)))]
    for cp in loads:
        cp.start()
    set_masks(r, length[0])
    loads[0].wait()
    for m in range(3):
        project(r, m)
    for i in range(2):
        project_pool(r, i)
    level_one(r)
    level_two(r)
    first_norm(r)
    loads[1].wait()
    for j in range(4):
        ffn_up(r, j)
    loads[2].wait()
    ffn_down_norm(r)
    for j in range(4):
        back_upper(r, j)
    for j in range(4):
        grad_down(r, j)
    outs = [pltpu.make_async_copy(b, a, sem.at[i]) for i, (a, b) in enumerate(((sq_out, r.sq), (up_out, r.up), (down_out, r.down)))]
    outs[2].start()
    back_first_norm(r)
    for j in range(4):
        grad_up(r, j)
    outs[1].start()
    back_out(r)
    back_level_two(r)
    for i in range(2):
        back_pool(r, i)
    back_level_one(r)
    for m in range(3):
        finish_projection(r, m, r.dqkv[m])
    outs[0].start()
    r.din[...] = r.dr[...].astype(BF)
    for cp in outs:
        cp.wait()


def compute(length, tokens, og, gains, shifts, pool, sq, up, down):
    vmem = pl.BlockSpec(memory_space=pltpu.VMEM)
    hbm = pl.BlockSpec(memory_space=pl.ANY)
    return pl.pallas_call(
        compute_kernel,
        out_shape=[
            jax.ShapeDtypeStruct((512, 768), BF),
            jax.ShapeDtypeStruct((512, 768), BF),
            jax.ShapeDtypeStruct((16, 768), F32),
            jax.ShapeDtypeStruct(SQ, BF),
            jax.ShapeDtypeStruct(UP, BF),
            jax.ShapeDtypeStruct(DOWN, BF),
        ],
        in_specs=[pl.BlockSpec(memory_space=pltpu.SMEM)] + [vmem] * 5 + [hbm] * 3,
        out_specs=[vmem] * 3 + [hbm] * 3,
        scratch_shapes=[pltpu.VMEM(SQ, BF), pltpu.VMEM(UP, BF), pltpu.VMEM(DOWN, BF), pltpu.SemaphoreType.DMA((3,))]
        + [pltpu.VMEM(*s) for s in ACTIVE.values()],
        compiler_params=pltpu.CompilerParams(vmem_limit_bytes=58 * 2**20),
    )(length, tokens, og, gains, shifts, pool, sq, up, down)


def local_kernels(
    tokens,
    doc_lengths,
    w_query,
    w_key,
    w_value,
    w_query2,
    w_key2,
    w_value2,
    w_out,
    w_up,
    w_down,
    norm_gains,
    norm_shifts,
    pool_kernels,
    out_grad,
):
    shards = (w_query, w_key, w_value, w_key2, w_value2, w_query2, w_out, w_up, w_down)
    sq, up, down = gather(shards)
    activations, d_tokens, vec, g_sq, g_up, g_down = compute(
        doc_lengths, tokens, out_grad, norm_gains, norm_shifts, pool_kernels, sq, up, down
    )
    o_sq, o_up, o_down, o_vec = scatter(g_sq, g_up, g_down, vec)
    core = lax.rem(lax.axis_index("dp"), 2)
    mine = lax.dynamic_slice_in_dim(o_sq.reshape(7, 96, 384), core * 192, 192, 2).transpose(0, 2, 1)
    return (
        activations,
        d_tokens,
        *[mine[i] for i in (0, 1, 2, 5, 3, 4, 6)],
        o_up,
        o_down.T,
        o_vec[0:2],
        o_vec[2:4],
        o_vec[4:14].reshape(2, 5, 768),
    )


def local(
    tokens,
    doc_lengths,
    w_query,
    w_key,
    w_value,
    w_query2,
    w_key2,
    w_value2,
    w_out,
    w_up,
    w_down,
    norm_gains,
    norm_shifts,
    pool_kernels,
    out_grad,
):
    shards = (w_query, w_key, w_value, w_query2, w_key2, w_value2, w_out, w_up, w_down)
    forward_weights = gather_first(shards)
    (
        full_query,
        full_key,
        full_value,
        full_query2,
        full_key2,
        full_value2,
        full_out,
        full_up,
        full_down,
    ) = forward_weights
    seq_rows = tokens.shape[0]
    length = doc_lengths[0]
    positions = jnp.arange(seq_rows, dtype=jnp.int32)
    padding = positions >= length
    allowed_one = (jnp.abs(positions[:, None] - positions[None, :]) <= WIN) & (
        padding[:, None] == padding[None, :]
    )
    pooled_at = positions[: seq_rows // STRIDE] * STRIDE
    allowed_two = (jnp.abs(positions[:, None] - pooled_at[None, :]) <= PWIN // 2) & (
        padding[:, None] == (pooled_at >= length)[None, :]
    )
    score_scale = 1.0 / math.sqrt(HD)
    query = matmul(tokens, full_query).astype(jnp.bfloat16)
    keys = matmul(tokens, full_key).astype(jnp.bfloat16)
    values = matmul(tokens, full_value).astype(jnp.bfloat16)
    key_two = matmul(tokens, full_key2)
    value_two = matmul(tokens, full_value2)
    key_pool_f, pool_key_back = jax.vjp(pool_rows, key_two, pool_kernels[0])
    value_pool_f, pool_value_back = jax.vjp(pool_rows, value_two, pool_kernels[1])
    key_pool = key_pool_f.astype(jnp.bfloat16)
    value_pool = value_pool_f.astype(jnp.bfloat16)
    first_f, log_one = level_forward(query, keys, values, allowed_one, score_scale)
    first = first_f.astype(jnp.bfloat16)
    query_two = matmul(first, full_query2).astype(jnp.bfloat16)
    second, log_two = level_forward(query_two, key_pool, value_pool, allowed_two, score_scale)
    mixed = (first.astype(jnp.float32) + second).astype(jnp.bfloat16)
    branch = matmul(mixed, full_out)
    hidden, norm_one_back = jax.vjp(
        layer_norm, tokens.astype(jnp.float32) + branch, norm_gains[0], norm_shifts[0]
    )
    hidden_low = hidden.astype(jnp.bfloat16)
    upper = matmul(hidden_low, full_up)
    activated_f, gelu_back = jax.vjp(gelu_tanh, upper)
    activated = activated_f.astype(jnp.bfloat16)
    resid_two = hidden + matmul(activated, full_down)
    result, norm_two_back = jax.vjp(layer_norm, resid_two, norm_gains[1], norm_shifts[1])
    activations = result.astype(jnp.bfloat16)
    back_weights = gather_second(shards)
    (
        back_query,
        back_key,
        back_value,
        back_query2,
        back_key2,
        back_value2,
        back_out,
        back_up,
        back_down,
    ) = back_weights
    d_resid_two, d_gain_two, d_shift_two = norm_two_back(out_grad.astype(jnp.float32))
    d_ffn = d_resid_two.astype(jnp.bfloat16)
    grad_down = inner_rows(activated, d_ffn)
    d_upper = gelu_back(outer_cols(d_ffn, back_down))[0].astype(jnp.bfloat16)
    grad_up = inner_rows(hidden_low, d_upper)
    d_hidden = d_resid_two + outer_cols(d_upper, back_up)
    d_resid_one, d_gain_one, d_shift_one = norm_one_back(d_hidden)
    d_branch = d_resid_one.astype(jnp.bfloat16)
    grad_out = inner_rows(mixed, d_branch)
    d_mixed = outer_cols(d_branch, back_out)
    d_query_two_f, d_key_pool_f, d_value_pool_f = level_backward(
        query_two,
        key_pool,
        value_pool,
        allowed_two,
        score_scale,
        log_two,
        d_mixed.astype(jnp.bfloat16),
    )
    d_query_two = d_query_two_f.astype(jnp.bfloat16)
    d_key_pool = d_key_pool_f.astype(jnp.bfloat16)
    d_value_pool = d_value_pool_f.astype(jnp.bfloat16)
    grad_query2 = inner_rows(first, d_query_two)
    d_first = (d_mixed + outer_cols(d_query_two, back_query2)).astype(jnp.bfloat16)
    d_query_f, d_keys_f, d_values_f = level_backward(
        query, keys, values, allowed_one, score_scale, log_one, d_first
    )
    d_query = d_query_f.astype(jnp.bfloat16)
    d_keys = d_keys_f.astype(jnp.bfloat16)
    d_values = d_values_f.astype(jnp.bfloat16)
    d_key_two_f, d_pool_key = pool_key_back(d_key_pool.astype(jnp.float32))
    d_value_two_f, d_pool_value = pool_value_back(d_value_pool.astype(jnp.float32))
    d_key_two = d_key_two_f.astype(jnp.bfloat16)
    d_value_two = d_value_two_f.astype(jnp.bfloat16)
    grad_query = inner_rows(tokens, d_query)
    grad_key = inner_rows(tokens, d_keys)
    grad_value = inner_rows(tokens, d_values)
    grad_key2 = inner_rows(tokens, d_key_two)
    grad_value2 = inner_rows(tokens, d_value_two)
    d_tokens = (
        d_resid_one
        + outer_cols(d_query, back_query)
        + outer_cols(d_keys, back_key)
        + outer_cols(d_values, back_value)
    )
    d_tokens = d_tokens + outer_cols(d_key_two, back_key2) + outer_cols(d_value_two, back_value2)
    grads_all = (
        grad_query,
        grad_key,
        grad_value,
        grad_query2,
        grad_key2,
        grad_value2,
        grad_out,
        grad_up,
        grad_down,
    )
    owned = reduce_columns_first(grads_all)
    gain_stack = jnp.stack([d_gain_one, d_gain_two])
    shift_stack = jnp.stack([d_shift_one, d_shift_two])
    pool_stack = jnp.stack([d_pool_key, d_pool_value])
    vector_sums = lax.psum((gain_stack, shift_stack, pool_stack), ("dp", "fsdp"))
    return (
        activations,
        d_tokens.astype(jnp.bfloat16),
        owned[0],
        owned[1],
        owned[2],
        owned[3],
        owned[4],
        owned[5],
        owned[6],
        owned[7],
        owned[8],
        vector_sums[0],
        vector_sums[1],
        vector_sums[2],
    )


def solution(mesh):
    fits = mesh.shape["dp"] == 4 and mesh.shape["fsdp"] == 8
    return jax.shard_map(
        local_kernels if fits else local,
        mesh=mesh,
        in_specs=(
            P(("dp", "fsdp"), None),
            P(("dp", "fsdp")),
            P("dp", "fsdp"),
            P("dp", "fsdp"),
            P("dp", "fsdp"),
            P("dp", "fsdp"),
            P("dp", "fsdp"),
            P("dp", "fsdp"),
            P("dp", "fsdp"),
            P("dp", "fsdp"),
            P("dp", "fsdp"),
            P(),
            P(),
            P(),
            P(("dp", "fsdp"), None),
        ),
        out_specs=(
            P(("dp", "fsdp"), None),
            P(("dp", "fsdp"), None),
            P("dp", "fsdp"),
            P("dp", "fsdp"),
            P("dp", "fsdp"),
            P("dp", "fsdp"),
            P("dp", "fsdp"),
            P("dp", "fsdp"),
            P("dp", "fsdp"),
            P("dp", "fsdp"),
            P("dp", "fsdp"),
            P(),
            P(),
            P(),
        ),
        check_vma=False,
    )
```

```python
import math

import jax
import jax.numpy as jnp
from jax import lax
from jax.experimental import pallas as pl
from jax.experimental.pallas import tpu as pltpu
from jax.sharding import PartitionSpec as P

HEADS = 12
HD = 64
WIN = 128
PWIN = 512
STRIDE = 4


def matmul(left_mat, right_mat):
    return jnp.dot(left_mat, right_mat, preferred_element_type=jnp.float32)


def inner_rows(left_mat, right_mat):
    return lax.dot_general(
        left_mat, right_mat, (((0,), (0,)), ((), ())), preferred_element_type=jnp.float32
    )


def outer_cols(left_mat, right_mat):
    return lax.dot_general(
        left_mat, right_mat, (((1,), (1,)), ((), ())), preferred_element_type=jnp.float32
    )


def layer_norm(inputs, norm_gain, norm_shift):
    average = jnp.mean(inputs, axis=-1, keepdims=True)
    centred = inputs - average
    variance = jnp.mean(centred * centred, axis=-1, keepdims=True)
    return centred * lax.rsqrt(variance + 1e-05) * norm_gain + norm_shift


def gelu_tanh(inputs):
    return jax.nn.gelu(inputs, approximate=True)


def pool_rows(inputs, kernel):
    side_rows = (kernel.shape[0] - 1) // 2
    pooled_rows = inputs.shape[0] // STRIDE
    padded = jnp.pad(inputs, ((side_rows, side_rows), (0, 0)))
    summed = jnp.zeros((pooled_rows, inputs.shape[1]), jnp.float32)
    for offset in range(kernel.shape[0]):
        summed = summed + kernel[offset] * padded[offset : offset + inputs.shape[0] : STRIDE]
    return summed


def split_heads(matrix):
    return matrix.reshape(matrix.shape[0], HEADS // 2, 2, HD).transpose(1, 0, 2, 3)


def join_heads(groups):
    return groups.transpose(1, 0, 2, 3).reshape(groups.shape[1], HEADS * HD)


def masked_scores(query, keys, allowed, score_scale):
    raw_scores = (
        jnp.einsum("ihd,jhd->hij", query, keys, preferred_element_type=jnp.float32) * score_scale
    )
    return jnp.where(allowed[None], raw_scores, -1e30)


def attend_forward(query, keys, values, allowed, score_scale):
    scores = masked_scores(query, keys, allowed, score_scale)
    highest = jnp.max(scores, axis=-1, keepdims=True)
    expo_terms = jnp.exp(scores - highest)
    summed = jnp.sum(expo_terms, axis=-1, keepdims=True)
    soft_weights = (expo_terms / summed).astype(jnp.bfloat16)
    result = jnp.einsum("hij,jhd->ihd", soft_weights, values, preferred_element_type=jnp.float32)
    return (result, (highest + jnp.log(summed))[..., 0])


def attend_backward(query, keys, values, allowed, score_scale, log_total, grad_result):
    scores = masked_scores(query, keys, allowed, score_scale)
    soft_weights = jnp.exp(scores - log_total[..., None])
    grad_soft = jnp.einsum("ihd,jhd->hij", grad_result, values, preferred_element_type=jnp.float32)
    grad_values = jnp.einsum(
        "hij,ihd->jhd",
        soft_weights.astype(jnp.bfloat16),
        grad_result,
        preferred_element_type=jnp.float32,
    )
    row_terms = jnp.sum(soft_weights * grad_soft, axis=-1, keepdims=True)
    grad_scores = (soft_weights * (grad_soft - row_terms)).astype(jnp.bfloat16)
    grad_query = (
        jnp.einsum("hij,jhd->ihd", grad_scores, keys, preferred_element_type=jnp.float32)
        * score_scale
    )
    grad_keys = (
        jnp.einsum("hij,ihd->jhd", grad_scores, query, preferred_element_type=jnp.float32)
        * score_scale
    )
    return (grad_query, grad_keys, grad_values)


def level_forward(query, keys, values, allowed, score_scale):

    def one_group(group_parts):
        return attend_forward(group_parts[0], group_parts[1], group_parts[2], allowed, score_scale)

    results, log_totals = lax.map(
        one_group, (split_heads(query), split_heads(keys), split_heads(values))
    )
    return (join_heads(results), log_totals)


def level_backward(query, keys, values, allowed, score_scale, log_totals, grad_result):

    def one_group(group_parts):
        return attend_backward(
            group_parts[0],
            group_parts[1],
            group_parts[2],
            allowed,
            score_scale,
            group_parts[3],
            group_parts[4],
        )

    grad_query, grad_keys, grad_values = lax.map(
        one_group,
        (
            split_heads(query),
            split_heads(keys),
            split_heads(values),
            log_totals,
            split_heads(grad_result),
        ),
    )
    return (join_heads(grad_query), join_heads(grad_keys), join_heads(grad_values))


def gather_first(shards):
    column_parts = (
        lax.all_gather(shards[0], "fsdp", axis=1, tiled=True),
        lax.all_gather(shards[1], "fsdp", axis=1, tiled=True),
        lax.all_gather(shards[2], "fsdp", axis=1, tiled=True),
        lax.all_gather(shards[3], "fsdp", axis=1, tiled=True),
        lax.all_gather(shards[4], "fsdp", axis=1, tiled=True),
        lax.all_gather(shards[5], "fsdp", axis=1, tiled=True),
        lax.all_gather(shards[6], "fsdp", axis=1, tiled=True),
        lax.all_gather(shards[7], "fsdp", axis=1, tiled=True),
        lax.all_gather(shards[8], "fsdp", axis=1, tiled=True),
    )
    return (
        lax.all_gather(column_parts[0], "dp", axis=0, tiled=True),
        lax.all_gather(column_parts[1], "dp", axis=0, tiled=True),
        lax.all_gather(column_parts[2], "dp", axis=0, tiled=True),
        lax.all_gather(column_parts[3], "dp", axis=0, tiled=True),
        lax.all_gather(column_parts[4], "dp", axis=0, tiled=True),
        lax.all_gather(column_parts[5], "dp", axis=0, tiled=True),
        lax.all_gather(column_parts[6], "dp", axis=0, tiled=True),
        lax.all_gather(column_parts[7], "dp", axis=0, tiled=True),
        lax.all_gather(column_parts[8], "dp", axis=0, tiled=True),
    )


def gather_second(shards):
    column_parts = (
        lax.all_gather(shards[0], "fsdp", axis=1, tiled=True),
        lax.all_gather(shards[1], "fsdp", axis=1, tiled=True),
        lax.all_gather(shards[2], "fsdp", axis=1, tiled=True),
        lax.all_gather(shards[3], "fsdp", axis=1, tiled=True),
        lax.all_gather(shards[4], "fsdp", axis=1, tiled=True),
        lax.all_gather(shards[5], "fsdp", axis=1, tiled=True),
        lax.all_gather(shards[6], "fsdp", axis=1, tiled=True),
        lax.all_gather(shards[7], "fsdp", axis=1, tiled=True),
        lax.all_gather(shards[8], "fsdp", axis=1, tiled=True),
    )
    return (
        lax.all_gather(column_parts[0], "dp", axis=0, tiled=True),
        lax.all_gather(column_parts[1], "dp", axis=0, tiled=True),
        lax.all_gather(column_parts[2], "dp", axis=0, tiled=True),
        lax.all_gather(column_parts[3], "dp", axis=0, tiled=True),
        lax.all_gather(column_parts[4], "dp", axis=0, tiled=True),
        lax.all_gather(column_parts[5], "dp", axis=0, tiled=True),
        lax.all_gather(column_parts[6], "dp", axis=0, tiled=True),
        lax.all_gather(column_parts[7], "dp", axis=0, tiled=True),
        lax.all_gather(column_parts[8], "dp", axis=0, tiled=True),
    )


def reduce_columns_first(grads_all):
    column_sums = (
        lax.psum_scatter(
            grads_all[0].astype(jnp.bfloat16), "fsdp", scatter_dimension=1, tiled=True
        ).astype(jnp.float32),
        lax.psum_scatter(
            grads_all[1].astype(jnp.bfloat16), "fsdp", scatter_dimension=1, tiled=True
        ).astype(jnp.float32),
        lax.psum_scatter(
            grads_all[2].astype(jnp.bfloat16), "fsdp", scatter_dimension=1, tiled=True
        ).astype(jnp.float32),
        lax.psum_scatter(
            grads_all[3].astype(jnp.bfloat16), "fsdp", scatter_dimension=1, tiled=True
        ).astype(jnp.float32),
        lax.psum_scatter(
            grads_all[4].astype(jnp.bfloat16), "fsdp", scatter_dimension=1, tiled=True
        ).astype(jnp.float32),
        lax.psum_scatter(
            grads_all[5].astype(jnp.bfloat16), "fsdp", scatter_dimension=1, tiled=True
        ).astype(jnp.float32),
        lax.psum_scatter(
            grads_all[6].astype(jnp.bfloat16), "fsdp", scatter_dimension=1, tiled=True
        ).astype(jnp.float32),
        lax.psum_scatter(
            grads_all[7].astype(jnp.bfloat16), "fsdp", scatter_dimension=1, tiled=True
        ).astype(jnp.float32),
        lax.psum_scatter(
            grads_all[8].astype(jnp.bfloat16), "fsdp", scatter_dimension=1, tiled=True
        ).astype(jnp.float32),
    )
    return (
        lax.psum_scatter(
            column_sums[0].astype(jnp.bfloat16), "dp", scatter_dimension=0, tiled=True
        ).astype(jnp.float32),
        lax.psum_scatter(
            column_sums[1].astype(jnp.bfloat16), "dp", scatter_dimension=0, tiled=True
        ).astype(jnp.float32),
        lax.psum_scatter(
            column_sums[2].astype(jnp.bfloat16), "dp", scatter_dimension=0, tiled=True
        ).astype(jnp.float32),
        lax.psum_scatter(
            column_sums[3].astype(jnp.bfloat16), "dp", scatter_dimension=0, tiled=True
        ).astype(jnp.float32),
        lax.psum_scatter(
            column_sums[4].astype(jnp.bfloat16), "dp", scatter_dimension=0, tiled=True
        ).astype(jnp.float32),
        lax.psum_scatter(
            column_sums[5].astype(jnp.bfloat16), "dp", scatter_dimension=0, tiled=True
        ).astype(jnp.float32),
        lax.psum_scatter(
            column_sums[6].astype(jnp.bfloat16), "dp", scatter_dimension=0, tiled=True
        ).astype(jnp.float32),
        lax.psum_scatter(
            column_sums[7].astype(jnp.bfloat16), "dp", scatter_dimension=0, tiled=True
        ).astype(jnp.float32),
        lax.psum_scatter(
            column_sums[8].astype(jnp.bfloat16), "dp", scatter_dimension=0, tiled=True
        ).astype(jnp.float32),
    )


MESH = pl.DeviceIdType.MESH
BF = jnp.bfloat16
F32 = jnp.float32

GROUPS = (
    ("s", 0, 1),
    ("s", 1, 3),
    ("s", 3, 5),
    ("s", 5, 7),
    ("u", 0, 96),
    ("u", 96, 192),
    ("d", 0, 48),
    ("d", 48, 96),
)
N_GROUPS = len(GROUPS)
SQ = (7, 4, 2, 2, 48, 768)
UP = (2, 2, 4, 2, 192, 384)
DOWN = (4, 2, 2, 2, 96, 768)


class Place:
    def __init__(self):
        dp = lax.axis_index("dp")
        fs = lax.axis_index("fsdp")
        self.y = lax.div(dp, 2)
        self.c = lax.rem(dp, 2)
        self.z = lax.div(fs, 2)
        self.x = lax.rem(fs, 2)
        c, x, y = self.c, self.x, self.y
        self.p1 = ((1 - c) * (1 - x) + c * x, (1 - c) * y + c * (1 - y))
        self.p2 = ((1 - c) * x + c * (1 - x), (1 - c) * (1 - y) + c * y)
        self.own = (x, y)
        self.diag = (1 - x, 1 - y)

    def dev(self, xy, z=None, c=None):
        z = self.z if z is None else z
        c = self.c if c is None else c
        return (xy[1] * 2 + c, z * 2 + xy[0])

    def sibling(self):
        return self.dev(self.own, c=1 - self.c)

    def peer(self, k):
        return lax.rem(self.z + k, 4)

    def everyone(self):
        return [self.sibling(), self.dev(self.p1), self.dev(self.p2)] + [
            self.dev(self.own, z=self.peer(k)) for k in (1, 2, 3)
        ]


def greet(me):
    bar = pltpu.get_barrier_semaphore()
    for d in me.everyone():
        pl.semaphore_signal(bar, inc=1, device_id=d, device_id_type=MESH)
    pl.semaphore_wait(bar, 6)


def square_lanes(y):
    return pl.ds(pl.multiple_of(y * 384, 128), 384)


def blocks(refs, g, xy, c, z=slice(None)):
    sq, up, down = refs
    x, y = xy
    kind, lo, hi = GROUPS[g]
    if kind == "s":
        return sq.at[lo:hi, z, x, c, :, square_lanes(y)]
    if kind == "u":
        return up.at[y, c, z, x, lo:hi]
    return down.at[z, x, y, c, lo:hi]


def rcopy(src, dst, ssem, rsem, dev):
    return pltpu.make_async_remote_copy(
        src_ref=src, dst_ref=dst, send_sem=ssem, recv_sem=rsem, device_id=dev, device_id_type=MESH
    )


class Gather:
    def __init__(self, me, refs, ssem, rsem):
        self.me, self.refs, self.ssem, self.rsem = me, refs, ssem, rsem

    def copy(self, g, i, incoming=False):
        me = self.me
        ss, rs = self.ssem.at[g, i], self.rsem.at[g, i]
        side = 1 if incoming else 0
        c = me.c
        ways = ((me.own, me.p1), (me.own, me.p2), (me.p1, me.diag))
        if i < 3:
            b = blocks(self.refs, g, ways[i][side], c, me.z)
            return rcopy(b, b, ss, rs, me.dev(me.p1 if i == 0 else me.p2))
        if i < 6:
            k = i - 2
            z = lax.rem(me.z + 4 - k, 4) if incoming else me.z
            b = blocks(self.refs, g, me.own, c, z)
            return rcopy(b, b, ss, rs, me.dev(me.own, z=me.peer(k)))
        if i < 10:
            cc = 1 - c if incoming else c
            what = ((me.own, me.own), (me.p1, me.p2), (me.p2, me.p1), (me.diag, me.diag))[i - 6][side]
            b = blocks(self.refs, g, what, cc)
            return rcopy(b, b, ss, rs, me.sibling())
        way, k = (i - 10) // 3, (i - 10) % 3 + 1
        b = blocks(self.refs, g, ways[way][side], c, lax.rem(me.z + 4 - k, 4))
        return rcopy(b, b, ss, rs, me.dev(me.p1 if way == 0 else me.p2))

    def go(self, g, *which):
        for i in which:
            self.copy(g, i).start()

    def got(self, g, *which):
        for i in which:
            self.copy(g, i, True).wait_recv()

    def start(self, g):
        self.go(g, 0, 1, 3, 4, 5)

    def step0(self, g):
        self.got(g, 0)
        self.go(g, 2)

    def step1(self, g):
        for k in range(3):
            self.got(g, 3 + k)
            self.go(g, 13 + k, 10 + k)
        self.go(g, 6)

    def step2(self, g):
        for k in range(3):
            self.got(g, 10 + k)
            self.go(g, 16 + k)
        self.go(g, 7)

    def step3(self, g):
        self.got(g, 1, 13, 14, 15)
        self.go(g, 8)

    def step4(self, g):
        self.got(g, 2, 16, 17, 18)
        self.go(g, 9)

    def arrived(self, g):
        self.got(g, 6, 7, 8, 9)

    def sent(self, g):
        for i in range(19):
            self.copy(g, i).wait_send()


class Scatter:
    def __init__(self, me, refs, sib, r1, r2, r3, ssem, rsem):
        self.me, self.refs, self.sib = me, refs, sib
        self.r1, self.r2, self.r3 = r1, r2, r3
        self.ssem, self.rsem = ssem, rsem

    def sib_view(self, g, xy, z=slice(None)):
        sq, up, down = self.sib
        x, y = xy
        kind, lo, hi = GROUPS[g]
        if kind == "s":
            return sq.at[lo:hi, z, x, :, square_lanes(y)]
        if kind == "u":
            return up.at[y, z, x, lo:hi]
        return down.at[z, x, y, lo:hi]

    def slot(self, bufs, g, i):
        kind, lo, hi = GROUPS[g]
        if kind == "s":
            return bufs[0].at[i, lo:hi]
        buf = bufs[1 if kind == "u" else 2]
        return buf.at[i, :, lo:hi] if len(buf.shape) == 4 else buf.at[i, lo:hi]

    def copy(self, g, i):
        me = self.me
        c = me.c
        ss, rs = self.ssem.at[g, i], self.rsem.at[g, i]
        if i < 4:
            what = (me.p1, me.diag, me.p2, me.own)[i]
            return rcopy(blocks(self.refs, g, what, 1 - c), self.sib_view(g, what), ss, rs, me.sibling())
        if i < 6:
            src = blocks(self.refs, g, (me.diag, me.p2)[i - 4], c)
            return rcopy(src, self.slot(self.r1, g, i - 4), ss, rs, me.dev(me.p2))
        if i == 6:
            return rcopy(blocks(self.refs, g, me.p1, c), self.slot(self.r2, g, 0), ss, rs, me.dev(me.p1))
        k = i - 6
        src = blocks(self.refs, g, me.own, c, me.peer(k))
        return rcopy(src, self.slot(self.r3, g, k - 1), ss, rs, me.dev(me.own, z=me.peer(k)))

    def go(self, g, *which):
        for i in which:
            self.copy(g, i).start()

    def got(self, g, i):
        self.copy(g, i).wait_recv()

    def add(self, here, *others):
        total = here[...].astype(F32)
        for other in others:
            total = total + other[...].astype(F32)
        here[...] = total.astype(BF)

    def start(self, g):
        self.go(g, 0, 1, 2, 3)

    def step1(self, g):
        me = self.me
        for i, what, out in ((1, me.diag, 4), (0, me.p2, 5)):
            self.got(g, i)
            self.add(blocks(self.refs, g, what, me.c), self.sib_view(g, what))
            self.go(g, out)

    def step2(self, g):
        me = self.me
        self.got(g, 2)
        self.got(g, 4)
        here = blocks(self.refs, g, me.p1, me.c)
        self.add(here, self.sib_view(g, me.p1), self.slot(self.r1, g, 0))
        self.go(g, 6)

    def step3(self, g):
        me = self.me
        self.got(g, 3)
        self.got(g, 5)
        self.got(g, 6)
        here = blocks(self.refs, g, me.own, me.c)
        self.add(here, self.sib_view(g, me.own), self.slot(self.r1, g, 1), self.slot(self.r2, g, 0))
        self.go(g, 7, 8, 9)

    def finish(self, g):
        me = self.me
        total = blocks(self.refs, g, me.own, me.c, me.z)[...].astype(F32)
        for k in (1, 2, 3):
            self.got(g, 6 + k)
            total = total + self.slot(self.r3, g, k - 1)[...].astype(F32)
        return total

    def sent(self, g):
        for i in range(10):
            self.copy(g, i).wait_send()


class VectorSum:
    def __init__(self, me, vec, buf, ssem, rsem):
        self.me, self.vec, self.buf, self.ssem, self.rsem = me, vec, buf, ssem, rsem
        self.hops = [me.sibling(), me.dev((1 - me.x, me.y)), me.dev((me.x, 1 - me.y))]

    def hop(self, i):
        b = self.buf
        return rcopy(b.at[i], b.at[3 + i], self.ssem.at[i], self.rsem.at[i], self.hops[i])

    def send(self, i):
        self.buf[i] = self.vec[...]
        self.hop(i).start()

    def take(self, i):
        self.hop(i).wait()
        self.vec[...] = self.vec[...] + self.buf[3 + i]

    def zcopy(self, k, incoming):
        me = self.me
        b = self.buf.at[6 + (lax.rem(me.z + 4 - k, 4) if incoming else me.z)]
        return rcopy(b, b, self.ssem.at[2 + k], self.rsem.at[2 + k], me.dev(me.own, z=me.peer(k)))

    def send_z(self):
        self.buf[6 + self.me.z] = self.vec[...]
        for k in (1, 2, 3):
            self.zcopy(k, False).start()

    def take_z(self):
        for k in (1, 2, 3):
            self.zcopy(k, True).wait_recv()
        for k in (1, 2, 3):
            self.zcopy(k, False).wait_send()
        b = self.buf
        self.vec[...] = (b[6] + b[7]) + (b[8] + b[9])


def place_squares(me, shards, sq, room, ssem, rsem):
    rows = lax.broadcasted_iota(jnp.int32, (192, 384), 0)
    lanes = lax.broadcasted_iota(jnp.int32, (192, 384), 1)
    spot = jnp.where(lanes == rows + me.c * 192, 1.0, 0.0).astype(BF)
    for m in range(7):
        t = dg(shards[m][...], spot, 0, 0).astype(BF)
        for half in range(2):
            room[half, 48 * m : 48 * m + 48, 0:384] = t[48 * half : 48 * half + 48]
    area = (pl.ds(0, 336), pl.ds(0, 384))
    swap = rcopy(room.at[(1 - me.c, *area)], room.at[(2, *area)], ssem, rsem, me.sibling())
    swap.start()
    swap.wait()
    for m in range(7):
        rows = slice(48 * m, 48 * m + 48)
        both = room[me.c, rows, 0:384].astype(F32) + room[2, rows, 0:384].astype(F32)
        sq[m, me.z, me.x, me.c, :, square_lanes(me.y)] = both.astype(BF)


GAIN, SHIFT, POOL = 0, 2, 4


def dg(a, b, ca, cb):
    return lax.dot_general(a, b, (((ca,), (cb,)), ((), ())), preferred_element_type=F32)


def weight(r, m):
    return r.sq[m].reshape(768, 768)


def weight_up(r, j):
    left = r.up[:, :, j, 0].reshape(768, 384)
    right = r.up[:, :, j, 1].reshape(768, 384)
    return jnp.concatenate([left, right], axis=1)


def weight_down(r, y, c):
    return r.down[:, :, y, c].reshape(768, 768)


def set_masks(r, length):
    for i in range(2):
        row = lax.broadcasted_iota(jnp.int32, (256, 384), 0) + 256 * i
        col = lax.broadcasted_iota(jnp.int32, (256, 384), 1) + 128 * i
        ok = (jnp.abs(row - col) <= WIN) & ((row >= length) == (col >= length))
        r.bias1[i] = jnp.where(ok, 0.0, -1e30)
    row = lax.broadcasted_iota(jnp.int32, (512, 128), 0)
    col = lax.broadcasted_iota(jnp.int32, (512, 128), 1) * STRIDE
    ok = (jnp.abs(row - col) <= PWIN // 2) & ((row >= length) == (col >= length))
    r.bias2[...] = jnp.where(ok, 0.0, -1e30)


def low_lanes(rows):
    return lax.broadcasted_iota(jnp.int32, (rows, 128), 1) < HD


def two_heads(pair):
    low = low_lanes(pair.shape[0])
    zero = jnp.zeros_like(pair)
    return jnp.concatenate([jnp.where(low, pair, zero), jnp.where(low, zero, pair)], axis=0)


def side_by_side(stacked):
    n = stacked.shape[0] // 2
    return jnp.where(low_lanes(n), stacked[:n], stacked[n:])


def pair_lanes(p):
    return pl.ds(pl.multiple_of(p * 128, 128), 128)


def softmax_out(scores, bias, values, lse_ref, p):
    scores = scores + jnp.concatenate([bias, bias], axis=0)
    highest = jnp.max(scores, axis=-1, keepdims=True)
    terms = jnp.exp(scores - highest)
    summed = jnp.sum(terms, axis=-1, keepdims=True)
    probs = (terms * (1.0 / summed)).astype(BF)
    lane = lax.broadcasted_iota(jnp.int32, lse_ref.shape, 1)
    lse_ref[...] = jnp.where(lane == p, highest + jnp.log(summed), lse_ref[...])
    return side_by_side(dg(probs, values, 1, 0))


def scores_of(query, keys):
    scaled = two_heads(query * jnp.asarray(0.125, BF))
    return scaled, dg(scaled, keys, 1, 1)


def softmax_back(scores, bias, lse_ref, p, grad, values):
    scores = scores + jnp.concatenate([bias, bias], axis=0)
    lane = lax.broadcasted_iota(jnp.int32, lse_ref.shape, 1)
    lse = jnp.sum(jnp.where(lane == p, lse_ref[...], 0.0), axis=-1, keepdims=True)
    probs = jnp.exp(scores - lse)
    grad_probs = dg(grad, values, 1, 1)
    row_terms = jnp.sum(probs * grad_probs, axis=-1, keepdims=True)
    return probs.astype(BF), (probs * (grad_probs - row_terms)).astype(BF)


def project(r, lo, hi):
    @pl.loop(lo, hi)
    def _(m):
        r.qkv[m] = dg(r.tokens[...], weight(r, m), 1, 1).astype(BF)


def project_pool(r, i):
    full = None
    for l in range(6):
        lanes = slice(l * 128, l * 128 + 128)
        if l % 3 == 0:
            full = dg(r.tokens[...], r.sq[3 + i, 2 * (l // 3) : 2 * (l // 3) + 2].reshape(384, 768), 1, 1)
        r.kt[i, l, 0:8] = jnp.zeros((8, 128), F32)
        r.kt[i, l, 520:528] = jnp.zeros((8, 128), F32)
        r.kt[i, l, 8:520] = full[:, (l % 3) * 128 : (l % 3) * 128 + 128]
        total = None
        for t in range(5):
            term = r.pool[t, i : i + 1, lanes] * r.kt[i, l, pl.ds(6 + t, 128, stride=STRIDE), :]
            total = term if total is None else total + term
        r.kp[i, :, lanes] = total.astype(BF)


def at_steps(p, hooks):
    for at, hook in (hooks or {}).items():
        pl.when(p == at)(hook)


def level_one(r, hooks=None):
    @pl.loop(0, HEADS // 2)
    def _(p):
        at_steps(p, hooks)
        lanes = pair_lanes(p)
        for i in range(2):
            rows, cols = pl.ds(256 * i, 256), pl.ds(128 * i, 384)
            _, scores = scores_of(r.qkv[0, rows, lanes], r.qkv[1, cols, lanes])
            out = softmax_out(scores, r.bias1[i], r.qkv[2, cols, lanes], r.lse.at[pl.ds(512 * i, 512)], p)
            r.first[rows, lanes] = out.astype(BF)


def level_two(r):
    r.q2[...] = dg(r.first[...], weight(r, 5), 1, 1).astype(BF)

    @pl.loop(0, HEADS // 2)
    def _(p):
        lanes = pair_lanes(p)
        _, scores = scores_of(r.q2[:, lanes], r.kp[0, :, lanes])
        out = softmax_out(scores, r.bias2[...], r.kp[1, :, lanes], r.lse, p + HEADS // 2)
        r.mixed[:, lanes] = (r.first[:, lanes].astype(F32) + out).astype(BF)


def norm_parts(x):
    average = jnp.mean(x, axis=-1, keepdims=True)
    centred = x - average
    inverse = lax.rsqrt(jnp.mean(centred * centred, axis=-1, keepdims=True) + 1e-05)
    return centred * inverse, inverse


def norm_back(n, inverse, gain, grad):
    scaled = grad * gain
    return (
        scaled - jnp.mean(scaled, axis=-1, keepdims=True) - n * jnp.mean(scaled * n, axis=-1, keepdims=True)
    ) * inverse


def first_norm(r):
    r.acc[...] = dg(r.mixed[...], weight(r, 6), 1, 1)

    @pl.loop(0, 4)
    def _(i):
        rows = pl.ds(pl.multiple_of(i * 128, 128), 128)
        n, inverse = norm_parts(r.tokens[rows].astype(F32) + r.acc[rows])
        r.n1[rows] = n
        r.inv1[rows] = inverse
        r.hlow[rows] = (n * r.gains[0:1] + r.shifts[0:1]).astype(BF)


def ffn_up(r):
    k = math.sqrt(2.0 / math.pi)

    @pl.loop(0, 4)
    def _(j):
        for i in range(2):
            rows = pl.ds(256 * i, 256)
            u = dg(r.hlow[rows], weight_up(r, j), 1, 0)
            square = u * u
            t = jnp.tanh(k * u * (1.0 + 0.044715 * square))
            half = 0.5 * (1.0 + t)
            r.act[j, rows] = (u * half).astype(BF)
            slope = half + (0.5 * k) * u * (1.0 - t * t) * (1.0 + (3 * 0.044715) * square)
            r.gd[j, rows] = slope.astype(BF)


def ffn_down_norm(r):
    @pl.loop(0, 2)
    def _(i):
        rows = pl.ds(pl.multiple_of(256 * i, 256), 256)
        total = dg(r.act[0, rows], weight_down(r, 0, 0), 1, 1)
        for j in range(1, 4):
            total = total + dg(r.act[j, rows], weight_down(r, j // 2, j % 2), 1, 1)
        r.acc[rows] = total

    r.vec[...] = jnp.zeros_like(r.vec)

    @pl.loop(0, 4)
    def _(i):
        rows = pl.ds(pl.multiple_of(i * 128, 128), 128)
        hidden = r.n1[rows] * r.gains[0:1] + r.shifts[0:1]
        n, inverse = norm_parts(hidden + r.acc[rows])
        grad = r.og[rows].astype(F32)
        r.og[rows] = (n * r.gains[1:2] + r.shifts[1:2]).astype(BF)
        r.vec[GAIN + 1 : GAIN + 2] += jnp.sum(grad * n, axis=0, keepdims=True)
        r.vec[SHIFT + 1 : SHIFT + 2] += jnp.sum(grad, axis=0, keepdims=True)
        d = norm_back(n, inverse, r.gains[1:2], grad)
        r.dr[rows] = d
        r.dlow[rows] = d.astype(BF)


def back_down(r, c):
    @pl.loop(0, 2)
    def _(y):
        j = y * 2 + c
        t = dg(r.dlow[...], weight_down(r, y, c), 1, 0)
        r.gd[j] = (r.gd[j].astype(F32) * t).astype(BF)
        for i in range(2):
            g = dg(r.dlow[:, 384 * i : 384 * i + 384], r.act[j], 0, 0).astype(BF)
            r.down[2 * i : 2 * i + 2, :, y, c] = g.reshape(2, 2, 96, 768)


def back_first_norm(r):
    @pl.loop(0, 2)
    def _(i):
        rows = pl.ds(pl.multiple_of(256 * i, 256), 256)
        total = r.dr[rows]
        for j in range(4):
            total = total + dg(r.gd[j, rows], weight_up(r, j), 1, 1)
        r.acc[rows] = total

    @pl.loop(0, 4)
    def _(i):
        rows = pl.ds(pl.multiple_of(i * 128, 128), 128)
        grad = r.acc[rows]
        n = r.n1[rows]
        r.vec[GAIN : GAIN + 1] += jnp.sum(grad * n, axis=0, keepdims=True)
        r.vec[SHIFT : SHIFT + 1] += jnp.sum(grad, axis=0, keepdims=True)
        d = norm_back(n, r.inv1[rows], r.gains[0:1], grad)
        r.dr[rows] = d
        r.dlow[rows] = d.astype(BF)


def grad_up(r):
    @pl.loop(0, 4)
    def _(j):
        for i in range(2):
            g = dg(r.hlow[:, 384 * i : 384 * i + 384], r.gd[j], 0, 0).astype(BF)
            for x in range(2):
                r.up[i, :, j, x] = g[:, x * 384 : (x + 1) * 384].reshape(2, 192, 384)


def set_grad(r, m, left, right):
    for i in range(2):
        g = dg(left[:, 384 * i : 384 * i + 384], right, 0, 0).astype(BF)
        r.sq[m, 2 * i : 2 * i + 2] = g.reshape(2, 2, 2, 48, 768)


def back_out(r):
    r.acc[...] = dg(r.dlow[...], weight(r, 6), 1, 0)
    set_grad(r, 6, r.dlow[...], r.mixed[...])


def back_level_two(r, hooks=None):
    @pl.loop(0, HEADS // 2)
    def _(p):
        at_steps(p, hooks)
        lanes = pair_lanes(p)
        scaled, scores = scores_of(r.q2[:, lanes], r.kp[0, :, lanes])
        grad = two_heads(r.acc[:, lanes].astype(BF))
        probs, grad_scores = softmax_back(
            scores, r.bias2[...], r.lse, p + HEADS // 2, grad, r.kp[1, :, lanes]
        )
        r.dpool[1][0:128, lanes] = dg(probs, grad, 0, 0).astype(BF).astype(F32)
        r.dpool[0][0:128, lanes] = dg(grad_scores, scaled, 0, 0).astype(BF).astype(F32)
        r.dq2[:, lanes] = (side_by_side(dg(grad_scores, r.kp[0, :, lanes], 1, 0)) * 0.125).astype(BF)

    r.dfirst[...] = (r.acc[...] + dg(r.dq2[...], weight(r, 5), 1, 0)).astype(BF)
    set_grad(r, 5, r.dq2[...], r.first[...])


def back_pool(r, i):
    r.dpool[i][128:136] = jnp.zeros((8, 768), F32)
    for l in range(6):
        lanes = slice(l * 128, l * 128 + 128)
        here = r.dpool[i][0:128, lanes]
        after = r.dpool[i][1:129, lanes]
        for t in range(5):
            term = here * r.kt[i, l, pl.ds(6 + t, 128, stride=STRIDE), :]
            at = POOL + 2 * t + i
            r.vec[at : at + 1, lanes] = jnp.sum(term, axis=0, keepdims=True)
        k = [r.pool[t, i : i + 1, lanes] for t in range(5)]
        r.kt[i, l, pl.ds(8, 128, stride=STRIDE), :] = k[2] * here
        r.kt[i, l, pl.ds(9, 128, stride=STRIDE), :] = k[3] * here
        r.kt[i, l, pl.ds(10, 128, stride=STRIDE), :] = k[4] * here + k[0] * after
        r.kt[i, l, pl.ds(11, 128, stride=STRIDE), :] = k[1] * after
    grad = jnp.concatenate([r.kt[i, l, 8:520].astype(BF) for l in range(6)], axis=1)
    finish_projection(r, 3 + i, grad)


def finish_projection(r, m, grad):
    r.dr[...] = r.dr[...] + dg(grad, weight(r, m), 1, 0)
    set_grad(r, m, grad, r.tokens[...])


def back_level_one(r, hooks=None):
    @pl.loop(0, HEADS)
    def _(step):
        at_steps(step, hooks)
        p, i = lax.div(step, 2), lax.rem(step, 2)
        lanes = pair_lanes(p)
        rows = pl.ds(pl.multiple_of(256 * i, 256), 256)
        cols = pl.ds(pl.multiple_of(128 * i, 128), 384)
        scaled, scores = scores_of(r.qkv[0, rows, lanes], r.qkv[1, cols, lanes])
        grad = two_heads(r.dfirst[rows, lanes])
        stacked = r.lse.at[pl.ds(pl.multiple_of(512 * i, 512), 512)]
        probs, grad_scores = softmax_back(scores, r.bias1[i], stacked, p, grad, r.qkv[2, cols, lanes])

        @pl.when(i == 0)
        def _():
            r.acc[:, 0:256] = jnp.zeros((512, 256), F32)

        r.acc[cols, 0:128] += dg(grad_scores, scaled, 0, 0)
        r.acc[cols, 128:256] += dg(probs, grad, 0, 0)
        dq = side_by_side(dg(grad_scores, r.qkv[1, cols, lanes], 1, 0)) * 0.125
        r.dqkv[0, rows, lanes] = dq.astype(BF)

        @pl.when(i == 1)
        def _():
            r.dqkv[1, :, lanes] = r.acc[:, 0:128].astype(BF)
            r.dqkv[2, :, lanes] = r.acc[:, 128:256].astype(BF)


class Refs:
    pass


ACTIVE = dict(
    qkv=((3, 512, 768), BF),
    kt=((2, 6, 528, 128), F32),
    kp=((2, 128, 768), BF),
    first=((512, 768), BF),
    q2=((512, 768), BF),
    mixed=((512, 768), BF),
    n1=((512, 768), F32),
    inv1=((512, 1), F32),
    hlow=((512, 768), BF),
    act=((4, 512, 768), BF),
    gd=((4, 512, 768), BF),
    dr=((512, 768), F32),
    acc=((512, 768), F32),
    dlow=((512, 768), BF),
    lse=((1024, 128), F32),
    bias1=((2, 256, 384), F32),
    bias2=((512, 128), F32),
)


def alias_late(r):
    r.dq2 = r.act.at[0]
    r.dfirst = r.act.at[1]
    r.dqkv = r.gd
    r.dpool = (r.n1.at[pl.ds(0, 136)], r.n1.at[pl.ds(256, 136)])


def slots(n):
    return dict(
        sq=((n, 7, 4, 48, 384), BF),
        up=((n, 4, 192, 384), BF),
        down=((n, 4, 96, 768), BF),
    )


BUFFERS = dict(
    tokens=((512, 768), BF),
    og=((512, 768), BF),
    gains=((2, 768), F32),
    shifts=((2, 768), F32),
    pool=((5, 2, 768), F32),
    shards=((7, 192, 96), BF),
    sq=(SQ, BF),
    up=(UP, BF),
    down=(DOWN, BF),
    s_sq=((7, 4, 2, 48, 768), BF),
    s_up=((2, 4, 2, 192, 384), BF),
    s_down=((4, 2, 2, 96, 768), BF),
    **{"r1_" + k: v for k, v in slots(2).items()},
    **{"r2_" + k: v for k, v in slots(1).items()},
    r3_sq=((3, 7, 48, 384), BF),
    r3_up=((3, 192, 384), BF),
    r3_down=((3, 96, 768), BF),
    vbuf=((10, 16, 768), F32),
    **ACTIVE,
)
SEMS = dict(load=20, swap=2, ag_s=(N_GROUPS, 19), ag_r=(N_GROUPS, 19), rs_s=(N_GROUPS, 10), rs_r=(N_GROUPS, 10), vs=6, vr=6, ends=4, endr=4)


def layer_kernel(*refs):
    r = Refs()
    names = (
        ["length", "tokens_in", "og_in", "gains_in", "shifts_in", "pool_in"]
        + [f"shard{m}" for m in range(7)]
        + ["up_in", "down_in", "out", "din", "vec", "o_sq", "o_up", "o_down"]
        + list(BUFFERS)
        + list(SEMS)
    )
    for name, ref in zip(names, refs):
        setattr(r, name, ref)
    alias_late(r)
    me = Place()

    shards = [r.shards.at[m] for m in range(7)]
    pairs = [(getattr(r, f"shard{m}"), shards[m]) for m in range(7)]
    pairs += [
        (r.down_in, r.down.at[me.z, me.x, me.y, me.c]),
        (r.up_in, r.up.at[me.y, me.c, me.z, me.x]),
        (r.tokens_in, r.tokens),
        (r.pool_in, r.pool),
        (r.gains_in, r.gains),
        (r.shifts_in, r.shifts),
        (r.og_in, r.og),
    ]
    loads = [pltpu.make_async_copy(a, b, r.load.at[i]) for i, (a, b) in enumerate(pairs)]
    for cp in loads:
        cp.start()
    greet(me)
    weights = (r.sq, r.up, r.down)
    gat = Gather(me, weights, r.ag_s, r.ag_r)
    sca = Scatter(
        me,
        weights,
        (r.s_sq, r.s_up, r.s_down),
        (r.r1_sq, r.r1_up, r.r1_down),
        (r.r2_sq, r.r2_up, r.r2_down),
        (r.r3_sq, r.r3_up, r.r3_down),
        r.rs_s,
        r.rs_r,
    )

    for cp in loads[:9]:
        cp.wait()
    place_squares(me, shards, r.sq, r.act, r.swap.at[0], r.swap.at[1])
    for g in range(N_GROUPS):
        gat.start(g)
    set_masks(r, r.length[0])
    gat.step0(0)
    gat.step0(1)
    gat.step1(0)
    gat.step0(2)
    gat.step1(1)
    gat.step0(3)
    gat.step2(0)
    gat.step1(2)
    gat.step0(4)
    gat.step2(1)
    gat.step3(0)
    gat.step1(3)
    gat.step0(5)
    gat.step2(2)
    gat.step3(1)
    gat.step4(0)
    gat.step1(4)
    gat.step0(6)
    for cp in loads[9:]:
        cp.wait()
    gat.arrived(0)
    project(r, 0, 1)
    gat.step2(3)
    gat.step3(2)
    gat.step4(1)
    gat.step1(5)
    gat.step0(7)
    gat.arrived(1)
    project(r, 1, 3)
    gat.step2(4)
    gat.step3(3)
    gat.step4(2)
    gat.step1(6)
    gat.arrived(2)
    project_pool(r, 0)
    project_pool(r, 1)

    def ahead_a():
        gat.step1(7)
        gat.step2(5)

    def ahead_b():
        gat.step3(4)
        gat.step4(3)

    level_one(r, {2: ahead_a, 4: ahead_b})
    gat.step2(6)
    gat.step3(5)
    gat.step4(4)
    gat.arrived(3)
    level_two(r)
    gat.step2(7)
    gat.step3(6)
    gat.step4(5)
    first_norm(r)
    gat.step3(7)
    gat.step4(6)
    gat.arrived(4)
    gat.arrived(5)
    ffn_up(r)
    gat.step4(7)
    gat.arrived(6)
    gat.arrived(7)
    ffn_down_norm(r)
    out = pltpu.make_async_copy(r.og, r.out, r.load.at[0])
    out.start()
    for g in range(N_GROUPS):
        gat.sent(g)

    for c in (1 - me.c, me.c):
        back_down(r, c)
        if c is not me.c:
            sca.start(6)
            sca.start(7)
    sca.step1(6)
    sca.step1(7)
    back_first_norm(r)
    grad_up(r)
    sca.start(4)
    sca.start(5)
    sca.step2(6)
    back_out(r)
    sca.step1(4)
    sca.step1(5)
    sca.step2(7)

    def two_a():
        sca.step3(6)

    def two_b():
        sca.step3(7)

    back_level_two(r, {2: two_a, 5: two_b})
    sca.start(3)
    sca.step2(4)
    back_pool(r, 0)
    sca.step1(3)
    back_pool(r, 1)
    sca.start(2)
    sca.step2(5)
    sca.step3(4)
    total = VectorSum(me, r.vec, r.vbuf, r.vs, r.vr)
    total.send(0)

    def one_a():
        sca.step1(2)
        r.o_down[0:48] = sca.finish(6)
        total.take(0)
        total.send(1)

    def one_b():
        sca.step3(5)
        r.o_down[48:96] = sca.finish(7)
        total.take(1)
        total.send(2)

    def one_c():
        sca.step2(3)
        total.take(2)
        total.send_z()

    def one_d():
        r.o_up[0:96] = sca.finish(4)
        total.take_z()

    back_level_one(r, {2: one_a, 4: one_b, 8: one_c, 10: one_d})
    finish_projection(r, 1, r.dqkv[1])
    finish_projection(r, 2, r.dqkv[2])
    sca.start(1)
    sca.step2(2)
    sca.step3(3)
    finish_projection(r, 0, r.dqkv[0])
    sca.start(0)
    sca.step1(1)
    sca.step1(0)
    r.dlow[...] = r.dr[...].astype(BF)
    din = pltpu.make_async_copy(r.dlow, r.din, r.load.at[1])
    din.start()
    r.o_up[96:192] = sca.finish(5)

    def end_swap(g, incoming=False):
        _, lo, hi = GROUPS[g]
        b = r.o_sq.at[lo:hi, 1 - me.c if incoming else me.c]
        return rcopy(b, b, r.ends.at[g], r.endr.at[g], me.sibling())

    def end(g):
        _, lo, hi = GROUPS[g]
        r.o_sq[lo:hi, me.c] = sca.finish(g)
        end_swap(g).start()

    sca.step3(2)
    end(3)
    sca.step2(1)
    sca.step2(0)
    end(2)
    sca.step3(1)
    sca.step3(0)
    end(1)
    end(0)
    for g in range(N_GROUPS):
        sca.sent(g)
    for g in range(4):
        end_swap(g).wait_send()
        end_swap(g, True).wait_recv()
    out.wait()
    din.wait()


def layer(length, tokens, og, gains, shifts, pool, squares, up, down):
    vmem = pl.BlockSpec(memory_space=pltpu.VMEM)
    hbm = pl.BlockSpec(memory_space=pl.ANY)
    return pl.pallas_call(
        layer_kernel,
        out_shape=[
            jax.ShapeDtypeStruct((512, 768), BF),
            jax.ShapeDtypeStruct((512, 768), BF),
            jax.ShapeDtypeStruct((16, 768), F32),
            jax.ShapeDtypeStruct((7, 2, 48, 384), F32),
            jax.ShapeDtypeStruct((192, 384), F32),
            jax.ShapeDtypeStruct((96, 768), F32),
        ],
        in_specs=[pl.BlockSpec(memory_space=pltpu.SMEM)] + [hbm] * 14,
        out_specs=[hbm] * 2 + [vmem] * 4,
        scratch_shapes=[pltpu.VMEM(*s) for s in BUFFERS.values()]
        + [pltpu.SemaphoreType.DMA(s if isinstance(s, tuple) else (s,)) for s in SEMS.values()],
        compiler_params=pltpu.CompilerParams(
            collective_id=0, has_side_effects=True, vmem_limit_bytes=VMEM_LIMIT
        ),
    )(length, tokens, og, gains, shifts, pool, *squares, up, down)


VMEM_LIMIT = 63 * 2**20


def ending_kernel(*refs):
    act, din, vec, sq, up, down, o_act, o_din = refs[:8]
    o_sq = refs[8:15]
    o_up, o_down, o_gain, o_shift, o_pool, turned = refs[15:]
    o_act[...] = act[...]
    o_din[...] = din[...]
    o_up[...] = up[...]
    o_down[...] = down[...]
    core = lax.rem(lax.axis_index("dp"), 2)
    mine = pl.ds(pl.multiple_of(core * 192, 8), 192)
    for m in range(7):
        turned[...] = jnp.transpose(sq[m].reshape(96, 384))
        o_sq[m][...] = turned[mine, :]
    o_gain[...] = vec[GAIN : GAIN + 2]
    o_shift[...] = vec[SHIFT : SHIFT + 2]
    for t in range(5):
        o_pool[t] = vec[POOL + 2 * t : POOL + 2 * t + 2]


def ending(act, din, vec, sq, up, down):
    vmem = pl.BlockSpec(memory_space=pltpu.VMEM)
    shapes = [((512, 768), BF)] * 2 + [((192, 96), F32)] * 7 + [((192, 384), F32), ((96, 768), F32)]
    shapes += [((2, 768), F32)] * 2 + [((5, 2, 768), F32)]
    return pl.pallas_call(
        ending_kernel,
        out_shape=[jax.ShapeDtypeStruct(*s) for s in shapes],
        in_specs=[vmem] * 6,
        out_specs=[vmem] * len(shapes),
        scratch_shapes=[pltpu.VMEM((384, 96), F32)],
        compiler_params=pltpu.CompilerParams(vmem_limit_bytes=32 * 2**20),
    )(act, din, vec, sq, up, down)


def local_kernels(
    tokens,
    doc_lengths,
    w_query,
    w_key,
    w_value,
    w_query2,
    w_key2,
    w_value2,
    w_out,
    w_up,
    w_down,
    norm_gains,
    norm_shifts,
    pool_kernels,
    out_grad,
):
    squares = (w_query, w_key, w_value, w_key2, w_value2, w_query2, w_out)
    ends = layer(
        doc_lengths,
        tokens,
        out_grad,
        norm_gains,
        norm_shifts,
        pool_kernels.transpose(1, 0, 2),
        squares,
        w_up,
        w_down.T,
    )
    act, din, g_q, g_k, g_v, g_k2, g_v2, g_q2, g_out, g_up, g_down, gain, shift, pools = ending(*ends)
    return (
        act,
        din,
        g_q,
        g_k,
        g_v,
        g_q2,
        g_k2,
        g_v2,
        g_out,
        g_up,
        g_down.T,
        gain,
        shift,
        pools.transpose(1, 0, 2),
    )


def local(
    tokens,
    doc_lengths,
    w_query,
    w_key,
    w_value,
    w_query2,
    w_key2,
    w_value2,
    w_out,
    w_up,
    w_down,
    norm_gains,
    norm_shifts,
    pool_kernels,
    out_grad,
):
    shards = (w_query, w_key, w_value, w_query2, w_key2, w_value2, w_out, w_up, w_down)
    forward_weights = gather_first(shards)
    (
        full_query,
        full_key,
        full_value,
        full_query2,
        full_key2,
        full_value2,
        full_out,
        full_up,
        full_down,
    ) = forward_weights
    seq_rows = tokens.shape[0]
    length = doc_lengths[0]
    positions = jnp.arange(seq_rows, dtype=jnp.int32)
    padding = positions >= length
    allowed_one = (jnp.abs(positions[:, None] - positions[None, :]) <= WIN) & (
        padding[:, None] == padding[None, :]
    )
    pooled_at = positions[: seq_rows // STRIDE] * STRIDE
    allowed_two = (jnp.abs(positions[:, None] - pooled_at[None, :]) <= PWIN // 2) & (
        padding[:, None] == (pooled_at >= length)[None, :]
    )
    score_scale = 1.0 / math.sqrt(HD)
    query = matmul(tokens, full_query).astype(jnp.bfloat16)
    keys = matmul(tokens, full_key).astype(jnp.bfloat16)
    values = matmul(tokens, full_value).astype(jnp.bfloat16)
    key_two = matmul(tokens, full_key2)
    value_two = matmul(tokens, full_value2)
    key_pool_f, pool_key_back = jax.vjp(pool_rows, key_two, pool_kernels[0])
    value_pool_f, pool_value_back = jax.vjp(pool_rows, value_two, pool_kernels[1])
    key_pool = key_pool_f.astype(jnp.bfloat16)
    value_pool = value_pool_f.astype(jnp.bfloat16)
    first_f, log_one = level_forward(query, keys, values, allowed_one, score_scale)
    first = first_f.astype(jnp.bfloat16)
    query_two = matmul(first, full_query2).astype(jnp.bfloat16)
    second, log_two = level_forward(query_two, key_pool, value_pool, allowed_two, score_scale)
    mixed = (first.astype(jnp.float32) + second).astype(jnp.bfloat16)
    branch = matmul(mixed, full_out)
    hidden, norm_one_back = jax.vjp(
        layer_norm, tokens.astype(jnp.float32) + branch, norm_gains[0], norm_shifts[0]
    )
    hidden_low = hidden.astype(jnp.bfloat16)
    upper = matmul(hidden_low, full_up)
    activated_f, gelu_back = jax.vjp(gelu_tanh, upper)
    activated = activated_f.astype(jnp.bfloat16)
    resid_two = hidden + matmul(activated, full_down)
    result, norm_two_back = jax.vjp(layer_norm, resid_two, norm_gains[1], norm_shifts[1])
    activations = result.astype(jnp.bfloat16)
    back_weights = gather_second(shards)
    (
        back_query,
        back_key,
        back_value,
        back_query2,
        back_key2,
        back_value2,
        back_out,
        back_up,
        back_down,
    ) = back_weights
    d_resid_two, d_gain_two, d_shift_two = norm_two_back(out_grad.astype(jnp.float32))
    d_ffn = d_resid_two.astype(jnp.bfloat16)
    grad_down = inner_rows(activated, d_ffn)
    d_upper = gelu_back(outer_cols(d_ffn, back_down))[0].astype(jnp.bfloat16)
    grad_up = inner_rows(hidden_low, d_upper)
    d_hidden = d_resid_two + outer_cols(d_upper, back_up)
    d_resid_one, d_gain_one, d_shift_one = norm_one_back(d_hidden)
    d_branch = d_resid_one.astype(jnp.bfloat16)
    grad_out = inner_rows(mixed, d_branch)
    d_mixed = outer_cols(d_branch, back_out)
    d_query_two_f, d_key_pool_f, d_value_pool_f = level_backward(
        query_two,
        key_pool,
        value_pool,
        allowed_two,
        score_scale,
        log_two,
        d_mixed.astype(jnp.bfloat16),
    )
    d_query_two = d_query_two_f.astype(jnp.bfloat16)
    d_key_pool = d_key_pool_f.astype(jnp.bfloat16)
    d_value_pool = d_value_pool_f.astype(jnp.bfloat16)
    grad_query2 = inner_rows(first, d_query_two)
    d_first = (d_mixed + outer_cols(d_query_two, back_query2)).astype(jnp.bfloat16)
    d_query_f, d_keys_f, d_values_f = level_backward(
        query, keys, values, allowed_one, score_scale, log_one, d_first
    )
    d_query = d_query_f.astype(jnp.bfloat16)
    d_keys = d_keys_f.astype(jnp.bfloat16)
    d_values = d_values_f.astype(jnp.bfloat16)
    d_key_two_f, d_pool_key = pool_key_back(d_key_pool.astype(jnp.float32))
    d_value_two_f, d_pool_value = pool_value_back(d_value_pool.astype(jnp.float32))
    d_key_two = d_key_two_f.astype(jnp.bfloat16)
    d_value_two = d_value_two_f.astype(jnp.bfloat16)
    grad_query = inner_rows(tokens, d_query)
    grad_key = inner_rows(tokens, d_keys)
    grad_value = inner_rows(tokens, d_values)
    grad_key2 = inner_rows(tokens, d_key_two)
    grad_value2 = inner_rows(tokens, d_value_two)
    d_tokens = (
        d_resid_one
        + outer_cols(d_query, back_query)
        + outer_cols(d_keys, back_key)
        + outer_cols(d_values, back_value)
    )
    d_tokens = d_tokens + outer_cols(d_key_two, back_key2) + outer_cols(d_value_two, back_value2)
    grads_all = (
        grad_query,
        grad_key,
        grad_value,
        grad_query2,
        grad_key2,
        grad_value2,
        grad_out,
        grad_up,
        grad_down,
    )
    owned = reduce_columns_first(grads_all)
    gain_stack = jnp.stack([d_gain_one, d_gain_two])
    shift_stack = jnp.stack([d_shift_one, d_shift_two])
    pool_stack = jnp.stack([d_pool_key, d_pool_value])
    vector_sums = lax.psum((gain_stack, shift_stack, pool_stack), ("dp", "fsdp"))
    return (
        activations,
        d_tokens.astype(jnp.bfloat16),
        owned[0],
        owned[1],
        owned[2],
        owned[3],
        owned[4],
        owned[5],
        owned[6],
        owned[7],
        owned[8],
        vector_sums[0],
        vector_sums[1],
        vector_sums[2],
    )


def solution(mesh):
    fits = mesh.shape["dp"] == 4 and mesh.shape["fsdp"] == 8
    return jax.shard_map(
        local_kernels if fits else local,
        mesh=mesh,
        in_specs=(
            P(("dp", "fsdp"), None),
            P(("dp", "fsdp")),
            P("dp", "fsdp"),
            P("dp", "fsdp"),
            P("dp", "fsdp"),
            P("dp", "fsdp"),
            P("dp", "fsdp"),
            P("dp", "fsdp"),
            P("dp", "fsdp"),
            P("dp", "fsdp"),
            P("dp", "fsdp"),
            P(),
            P(),
            P(),
            P(("dp", "fsdp"), None),
        ),
        out_specs=(
            P(("dp", "fsdp"), None),
            P(("dp", "fsdp"), None),
            P("dp", "fsdp"),
            P("dp", "fsdp"),
            P("dp", "fsdp"),
            P("dp", "fsdp"),
            P("dp", "fsdp"),
            P("dp", "fsdp"),
            P("dp", "fsdp"),
            P("dp", "fsdp"),
            P("dp", "fsdp"),
            P(),
            P(),
            P(),
        ),
        check_vma=False,
    )
```

```python
import math

import jax
import jax.numpy as jnp
from jax import lax
from jax.experimental import pallas as pl
from jax.experimental.pallas import tpu as pltpu
from jax.sharding import PartitionSpec as P

HEADS = 12
HD = 64
WIN = 128
PWIN = 512
STRIDE = 4


def matmul(left_mat, right_mat):
    return jnp.dot(left_mat, right_mat, preferred_element_type=jnp.float32)


def inner_rows(left_mat, right_mat):
    return lax.dot_general(
        left_mat, right_mat, (((0,), (0,)), ((), ())), preferred_element_type=jnp.float32
    )


def outer_cols(left_mat, right_mat):
    return lax.dot_general(
        left_mat, right_mat, (((1,), (1,)), ((), ())), preferred_element_type=jnp.float32
    )


def layer_norm(inputs, norm_gain, norm_shift):
    average = jnp.mean(inputs, axis=-1, keepdims=True)
    centred = inputs - average
    variance = jnp.mean(centred * centred, axis=-1, keepdims=True)
    return centred * lax.rsqrt(variance + 1e-05) * norm_gain + norm_shift


def gelu_tanh(inputs):
    return jax.nn.gelu(inputs, approximate=True)


def pool_rows(inputs, kernel):
    side_rows = (kernel.shape[0] - 1) // 2
    pooled_rows = inputs.shape[0] // STRIDE
    padded = jnp.pad(inputs, ((side_rows, side_rows), (0, 0)))
    summed = jnp.zeros((pooled_rows, inputs.shape[1]), jnp.float32)
    for offset in range(kernel.shape[0]):
        summed = summed + kernel[offset] * padded[offset : offset + inputs.shape[0] : STRIDE]
    return summed


def split_heads(matrix):
    return matrix.reshape(matrix.shape[0], HEADS // 2, 2, HD).transpose(1, 0, 2, 3)


def join_heads(groups):
    return groups.transpose(1, 0, 2, 3).reshape(groups.shape[1], HEADS * HD)


def masked_scores(query, keys, allowed, score_scale):
    raw_scores = (
        jnp.einsum("ihd,jhd->hij", query, keys, preferred_element_type=jnp.float32) * score_scale
    )
    return jnp.where(allowed[None], raw_scores, -1e30)


def attend_forward(query, keys, values, allowed, score_scale):
    scores = masked_scores(query, keys, allowed, score_scale)
    highest = jnp.max(scores, axis=-1, keepdims=True)
    expo_terms = jnp.exp(scores - highest)
    summed = jnp.sum(expo_terms, axis=-1, keepdims=True)
    soft_weights = (expo_terms / summed).astype(jnp.bfloat16)
    result = jnp.einsum("hij,jhd->ihd", soft_weights, values, preferred_element_type=jnp.float32)
    return (result, (highest + jnp.log(summed))[..., 0])


def attend_backward(query, keys, values, allowed, score_scale, log_total, grad_result):
    scores = masked_scores(query, keys, allowed, score_scale)
    soft_weights = jnp.exp(scores - log_total[..., None])
    grad_soft = jnp.einsum("ihd,jhd->hij", grad_result, values, preferred_element_type=jnp.float32)
    grad_values = jnp.einsum(
        "hij,ihd->jhd",
        soft_weights.astype(jnp.bfloat16),
        grad_result,
        preferred_element_type=jnp.float32,
    )
    row_terms = jnp.sum(soft_weights * grad_soft, axis=-1, keepdims=True)
    grad_scores = (soft_weights * (grad_soft - row_terms)).astype(jnp.bfloat16)
    grad_query = (
        jnp.einsum("hij,jhd->ihd", grad_scores, keys, preferred_element_type=jnp.float32)
        * score_scale
    )
    grad_keys = (
        jnp.einsum("hij,ihd->jhd", grad_scores, query, preferred_element_type=jnp.float32)
        * score_scale
    )
    return (grad_query, grad_keys, grad_values)


def level_forward(query, keys, values, allowed, score_scale):

    def one_group(group_parts):
        return attend_forward(group_parts[0], group_parts[1], group_parts[2], allowed, score_scale)

    results, log_totals = lax.map(
        one_group, (split_heads(query), split_heads(keys), split_heads(values))
    )
    return (join_heads(results), log_totals)


def level_backward(query, keys, values, allowed, score_scale, log_totals, grad_result):

    def one_group(group_parts):
        return attend_backward(
            group_parts[0],
            group_parts[1],
            group_parts[2],
            allowed,
            score_scale,
            group_parts[3],
            group_parts[4],
        )

    grad_query, grad_keys, grad_values = lax.map(
        one_group,
        (
            split_heads(query),
            split_heads(keys),
            split_heads(values),
            log_totals,
            split_heads(grad_result),
        ),
    )
    return (join_heads(grad_query), join_heads(grad_keys), join_heads(grad_values))


def gather_first(shards):
    column_parts = (
        lax.all_gather(shards[0], "fsdp", axis=1, tiled=True),
        lax.all_gather(shards[1], "fsdp", axis=1, tiled=True),
        lax.all_gather(shards[2], "fsdp", axis=1, tiled=True),
        lax.all_gather(shards[3], "fsdp", axis=1, tiled=True),
        lax.all_gather(shards[4], "fsdp", axis=1, tiled=True),
        lax.all_gather(shards[5], "fsdp", axis=1, tiled=True),
        lax.all_gather(shards[6], "fsdp", axis=1, tiled=True),
        lax.all_gather(shards[7], "fsdp", axis=1, tiled=True),
        lax.all_gather(shards[8], "fsdp", axis=1, tiled=True),
    )
    return (
        lax.all_gather(column_parts[0], "dp", axis=0, tiled=True),
        lax.all_gather(column_parts[1], "dp", axis=0, tiled=True),
        lax.all_gather(column_parts[2], "dp", axis=0, tiled=True),
        lax.all_gather(column_parts[3], "dp", axis=0, tiled=True),
        lax.all_gather(column_parts[4], "dp", axis=0, tiled=True),
        lax.all_gather(column_parts[5], "dp", axis=0, tiled=True),
        lax.all_gather(column_parts[6], "dp", axis=0, tiled=True),
        lax.all_gather(column_parts[7], "dp", axis=0, tiled=True),
        lax.all_gather(column_parts[8], "dp", axis=0, tiled=True),
    )


def gather_second(shards):
    column_parts = (
        lax.all_gather(shards[0], "fsdp", axis=1, tiled=True),
        lax.all_gather(shards[1], "fsdp", axis=1, tiled=True),
        lax.all_gather(shards[2], "fsdp", axis=1, tiled=True),
        lax.all_gather(shards[3], "fsdp", axis=1, tiled=True),
        lax.all_gather(shards[4], "fsdp", axis=1, tiled=True),
        lax.all_gather(shards[5], "fsdp", axis=1, tiled=True),
        lax.all_gather(shards[6], "fsdp", axis=1, tiled=True),
        lax.all_gather(shards[7], "fsdp", axis=1, tiled=True),
        lax.all_gather(shards[8], "fsdp", axis=1, tiled=True),
    )
    return (
        lax.all_gather(column_parts[0], "dp", axis=0, tiled=True),
        lax.all_gather(column_parts[1], "dp", axis=0, tiled=True),
        lax.all_gather(column_parts[2], "dp", axis=0, tiled=True),
        lax.all_gather(column_parts[3], "dp", axis=0, tiled=True),
        lax.all_gather(column_parts[4], "dp", axis=0, tiled=True),
        lax.all_gather(column_parts[5], "dp", axis=0, tiled=True),
        lax.all_gather(column_parts[6], "dp", axis=0, tiled=True),
        lax.all_gather(column_parts[7], "dp", axis=0, tiled=True),
        lax.all_gather(column_parts[8], "dp", axis=0, tiled=True),
    )


def reduce_columns_first(grads_all):
    column_sums = (
        lax.psum_scatter(
            grads_all[0].astype(jnp.bfloat16), "fsdp", scatter_dimension=1, tiled=True
        ).astype(jnp.float32),
        lax.psum_scatter(
            grads_all[1].astype(jnp.bfloat16), "fsdp", scatter_dimension=1, tiled=True
        ).astype(jnp.float32),
        lax.psum_scatter(
            grads_all[2].astype(jnp.bfloat16), "fsdp", scatter_dimension=1, tiled=True
        ).astype(jnp.float32),
        lax.psum_scatter(
            grads_all[3].astype(jnp.bfloat16), "fsdp", scatter_dimension=1, tiled=True
        ).astype(jnp.float32),
        lax.psum_scatter(
            grads_all[4].astype(jnp.bfloat16), "fsdp", scatter_dimension=1, tiled=True
        ).astype(jnp.float32),
        lax.psum_scatter(
            grads_all[5].astype(jnp.bfloat16), "fsdp", scatter_dimension=1, tiled=True
        ).astype(jnp.float32),
        lax.psum_scatter(
            grads_all[6].astype(jnp.bfloat16), "fsdp", scatter_dimension=1, tiled=True
        ).astype(jnp.float32),
        lax.psum_scatter(
            grads_all[7].astype(jnp.bfloat16), "fsdp", scatter_dimension=1, tiled=True
        ).astype(jnp.float32),
        lax.psum_scatter(
            grads_all[8].astype(jnp.bfloat16), "fsdp", scatter_dimension=1, tiled=True
        ).astype(jnp.float32),
    )
    return (
        lax.psum_scatter(
            column_sums[0].astype(jnp.bfloat16), "dp", scatter_dimension=0, tiled=True
        ).astype(jnp.float32),
        lax.psum_scatter(
            column_sums[1].astype(jnp.bfloat16), "dp", scatter_dimension=0, tiled=True
        ).astype(jnp.float32),
        lax.psum_scatter(
            column_sums[2].astype(jnp.bfloat16), "dp", scatter_dimension=0, tiled=True
        ).astype(jnp.float32),
        lax.psum_scatter(
            column_sums[3].astype(jnp.bfloat16), "dp", scatter_dimension=0, tiled=True
        ).astype(jnp.float32),
        lax.psum_scatter(
            column_sums[4].astype(jnp.bfloat16), "dp", scatter_dimension=0, tiled=True
        ).astype(jnp.float32),
        lax.psum_scatter(
            column_sums[5].astype(jnp.bfloat16), "dp", scatter_dimension=0, tiled=True
        ).astype(jnp.float32),
        lax.psum_scatter(
            column_sums[6].astype(jnp.bfloat16), "dp", scatter_dimension=0, tiled=True
        ).astype(jnp.float32),
        lax.psum_scatter(
            column_sums[7].astype(jnp.bfloat16), "dp", scatter_dimension=0, tiled=True
        ).astype(jnp.float32),
        lax.psum_scatter(
            column_sums[8].astype(jnp.bfloat16), "dp", scatter_dimension=0, tiled=True
        ).astype(jnp.float32),
    )


MESH = pl.DeviceIdType.MESH
BF = jnp.bfloat16
F32 = jnp.float32

GROUPS = (
    ("s", 0, 1),
    ("s", 1, 3),
    ("s", 3, 5),
    ("s", 5, 7),
    ("u", 0, 96),
    ("u", 96, 192),
    ("d", 0, 256),
    ("d", 256, 512),
    ("d", 512, 768),
)
PLANE = 8
N_GROUPS = len(GROUPS)
SQ = (7, 4, 2, 2, 48, 768)
UP = (2, 2, 4, 2, 192, 384)
DOWN = (4, 2, 2, 2, 96, 768)


class Place:
    def __init__(self):
        dp = lax.axis_index("dp")
        fs = lax.axis_index("fsdp")
        self.y = lax.div(dp, 2)
        self.c = lax.rem(dp, 2)
        self.z = lax.div(fs, 2)
        self.x = lax.rem(fs, 2)
        c, x, y = self.c, self.x, self.y
        self.p1 = ((1 - c) * (1 - x) + c * x, (1 - c) * y + c * (1 - y))
        self.p2 = ((1 - c) * x + c * (1 - x), (1 - c) * (1 - y) + c * y)
        self.own = (x, y)
        self.diag = (1 - x, 1 - y)

    def dev(self, xy, z=None, c=None):
        z = self.z if z is None else z
        c = self.c if c is None else c
        return (xy[1] * 2 + c, z * 2 + xy[0])

    def sibling(self):
        return self.dev(self.own, c=1 - self.c)

    def peer(self, k):
        return lax.rem(self.z + k, 4)

    def everyone(self):
        return [self.sibling(), self.dev(self.p1), self.dev(self.p2), self.dev(self.diag)] + [
            self.dev(self.own, z=self.peer(k)) for k in (1, 2, 3)
        ]


def greet(me):
    bar = pltpu.get_barrier_semaphore()
    for d in me.everyone():
        pl.semaphore_signal(bar, inc=1, device_id=d, device_id_type=MESH)
    pl.semaphore_wait(bar, 7)


def square_lanes(y):
    return pl.ds(pl.multiple_of(y * 384, 128), 384)


def blocks(refs, g, xy, c, z=slice(None)):
    sq, up, down = refs
    x, y = xy
    kind, lo, hi = GROUPS[g]
    if kind == "s":
        return sq.at[lo:hi, z, x, c, :, square_lanes(y)]
    if kind == "u":
        return up.at[y, c, z, x, lo:hi]
    return down.at[z, x, y, c, :, lo:hi]


def plane(down, g, c, z):
    _, lo, hi = GROUPS[g]
    return down.at[z, :, :, c, :, lo:hi]


def rcopy(src, dst, ssem, rsem, dev):
    return pltpu.make_async_remote_copy(
        src_ref=src, dst_ref=dst, send_sem=ssem, recv_sem=rsem, device_id=dev, device_id_type=MESH
    )


class Gather:
    def __init__(self, me, refs, ssem, rsem):
        self.me, self.refs, self.ssem, self.rsem = me, refs, ssem, rsem

    def copy(self, g, i, incoming=False):
        me = self.me
        ss, rs = self.ssem.at[g, i], self.rsem.at[g, i]
        side = 1 if incoming else 0
        c = me.c
        ways = ((me.own, me.p1), (me.own, me.p2), (me.p1, me.diag))
        if i < 3:
            b = blocks(self.refs, g, ways[i][side], c, me.z)
            return rcopy(b, b, ss, rs, me.dev(me.p1 if i == 0 else me.p2))
        if i < 6:
            k = i - 2
            z = lax.rem(me.z + 4 - k, 4) if incoming else me.z
            b = blocks(self.refs, g, me.own, c, z)
            return rcopy(b, b, ss, rs, me.dev(me.own, z=me.peer(k)))
        if i < 10:
            cc = 1 - c if incoming else c
            what = ((me.own, me.own), (me.p1, me.p2), (me.p2, me.p1), (me.diag, me.diag))[i - 6][side]
            b = blocks(self.refs, g, what, cc)
            return rcopy(b, b, ss, rs, me.sibling())
        way, k = (i - 10) // 3, (i - 10) % 3 + 1
        b = blocks(self.refs, g, ways[way][side], c, lax.rem(me.z + 4 - k, 4))
        return rcopy(b, b, ss, rs, me.dev(me.p1 if way == 0 else me.p2))

    def go(self, g, *which):
        for i in which:
            self.copy(g, i).start()

    def got(self, g, *which):
        for i in which:
            self.copy(g, i, True).wait_recv()

    def start(self, g):
        self.go(g, 0, 1, 3, 4, 5)

    def step0(self, g):
        self.got(g, 0)
        self.go(g, 2)

    def step1(self, g):
        for k in range(3):
            self.got(g, 3 + k)
            self.go(g, 13 + k, 10 + k)
        self.go(g, 6)

    def step2(self, g):
        for k in range(3):
            self.got(g, 10 + k)
            self.go(g, 16 + k)
        self.go(g, 7)

    def step3(self, g):
        self.got(g, 1, 13, 14, 15)
        self.go(g, 8)

    def step4(self, g):
        self.got(g, 2, 16, 17, 18)
        self.go(g, 9)

    def arrived(self, g):
        self.got(g, 6, 7, 8, 9)

    def sent(self, g):
        for i in range(19):
            self.copy(g, i).wait_send()


class Scatter:
    def __init__(self, me, refs, sib, r1, r2, r3, rp, ssem, rsem):
        self.me, self.refs, self.sib = me, refs, sib
        self.r1, self.r2, self.r3 = r1, r2, r3
        self.pz, self.p2, self.p1 = rp
        self.ssem, self.rsem = ssem, rsem

    def sib_view(self, g, xy, z=slice(None)):
        sq, up, down = self.sib
        x, y = xy
        kind, lo, hi = GROUPS[g]
        if kind == "s":
            return sq.at[lo:hi, z, x, :, square_lanes(y)]
        if kind == "u":
            return up.at[y, z, x, lo:hi]
        return down.at[z, x, y, :, lo:hi]

    def plane_of(self, g, c, z):
        return plane(self.refs[2], g, c, z)

    def sib_plane(self, g, z):
        _, lo, hi = GROUPS[g]
        return self.sib[2].at[z, :, :, :, lo:hi]

    def slot(self, bufs, g, i):
        kind, lo, hi = GROUPS[g]
        if kind == "s":
            return bufs[0].at[i, lo:hi]
        buf = bufs[1 if kind == "u" else 2]
        if kind == "d":
            return buf.at[i, :, :, lo:hi] if len(buf.shape) == 4 else buf.at[i, :, lo:hi]
        return buf.at[i, :, lo:hi] if len(buf.shape) == 4 else buf.at[i, lo:hi]

    def copy(self, g, i):
        me = self.me
        c = me.c
        ss, rs = self.ssem.at[g, i], self.rsem.at[g, i]
        if g == PLANE:
            if i < 4:
                z = me.peer(i + 1)
                return rcopy(self.plane_of(g, 1 - c, z), self.sib_plane(g, z), ss, rs, me.sibling())
            if i < 7:
                k = i - 3
                src = self.plane_of(g, c, me.peer(k))
                return rcopy(src, self.pz.at[k - 1], ss, rs, me.dev(me.own, z=me.peer(k)))
            if i < 9:
                src = blocks(self.refs, g, (me.diag, me.p2)[i - 7], c, me.z)
                return rcopy(src, self.p2.at[i - 7], ss, rs, me.dev(me.p2))
            return rcopy(blocks(self.refs, g, me.p1, c, me.z), self.p1, ss, rs, me.dev(me.p1))
        if i < 4:
            what = (me.p1, me.diag, me.p2, me.own)[i]
            return rcopy(blocks(self.refs, g, what, 1 - c), self.sib_view(g, what), ss, rs, me.sibling())
        if i < 6:
            src = blocks(self.refs, g, (me.diag, me.p2)[i - 4], c)
            return rcopy(src, self.slot(self.r1, g, i - 4), ss, rs, me.dev(me.p2))
        if i == 6:
            return rcopy(blocks(self.refs, g, me.p1, c), self.slot(self.r2, g, 0), ss, rs, me.dev(me.p1))
        k = i - 6
        src = blocks(self.refs, g, me.own, c, me.peer(k))
        return rcopy(src, self.slot(self.r3, g, k - 1), ss, rs, me.dev(me.own, z=me.peer(k)))

    def go(self, g, *which):
        for i in which:
            self.copy(g, i).start()

    def got(self, g, i):
        self.copy(g, i).wait_recv()

    def add(self, here, *others):
        total = here[...].astype(F32)
        for other in others:
            total = total + other[...].astype(F32)
        here[...] = total.astype(BF)

    def start(self, g):
        self.go(g, 0, 1, 2, 3)

    def step1(self, g):
        me = self.me
        if g == PLANE:
            for k in (1, 2, 3):
                z = me.peer(k)
                self.got(g, k - 1)
                self.add(self.plane_of(g, me.c, z), self.sib_plane(g, z))
                self.go(g, 3 + k)
            return
        for i, what, out in ((1, me.diag, 4), (0, me.p2, 5)):
            self.got(g, i)
            self.add(blocks(self.refs, g, what, me.c), self.sib_view(g, what))
            self.go(g, out)

    def step2(self, g):
        me = self.me
        if g == PLANE:
            for i in (3, 4, 5, 6):
                self.got(g, i)
            here = self.plane_of(g, me.c, me.z)
            self.add(here, self.sib_plane(g, me.z), *[self.pz.at[k] for k in range(3)])
            self.go(g, 7, 8)
            return
        self.got(g, 2)
        self.got(g, 4)
        here = blocks(self.refs, g, me.p1, me.c)
        self.add(here, self.sib_view(g, me.p1), self.slot(self.r1, g, 0))
        self.go(g, 6)

    def step3(self, g):
        me = self.me
        if g == PLANE:
            self.got(g, 7)
            self.add(blocks(self.refs, g, me.p1, me.c, me.z), self.p2.at[0])
            self.go(g, 9)
            return
        self.got(g, 3)
        self.got(g, 5)
        self.got(g, 6)
        here = blocks(self.refs, g, me.own, me.c)
        self.add(here, self.sib_view(g, me.own), self.slot(self.r1, g, 1), self.slot(self.r2, g, 0))
        self.go(g, 7, 8, 9)

    def finish(self, g):
        me = self.me
        total = blocks(self.refs, g, me.own, me.c, me.z)[...].astype(F32)
        if g == PLANE:
            self.got(g, 8)
            self.got(g, 9)
            return total + self.p2[1].astype(F32) + self.p1[...].astype(F32)
        for k in (1, 2, 3):
            self.got(g, 6 + k)
            total = total + self.slot(self.r3, g, k - 1)[...].astype(F32)
        return total

    def sent(self, g):
        for i in range(10):
            self.copy(g, i).wait_send()


class VectorSum:
    def __init__(self, me, vec, buf, ssem, rsem):
        self.me, self.vec, self.buf, self.ssem, self.rsem = me, vec, buf, ssem, rsem

    def copy(self, i, incoming=False):
        me = self.me
        if i < 3:
            z = lax.rem(me.z + 3 - i, 4) if incoming else me.z
            b, d = self.buf.at[z], me.dev(me.own, z=me.peer(i + 1))
        elif i == 3:
            return rcopy(self.buf.at[4], self.buf.at[5], self.ssem.at[i], self.rsem.at[i], me.sibling())
        else:
            x, y = ((1 - me.x, me.y), (me.x, 1 - me.y), me.diag)[i - 4]
            fx, fy = (x, y) if incoming else me.own
            b, d = self.buf.at[6 + fx + 2 * fy], me.dev((x, y))
        return rcopy(b, b, self.ssem.at[i], self.rsem.at[i], d)

    def send(self, first, last):
        for i in range(first, last):
            self.copy(i).start()

    def got(self, first, last):
        for i in range(first, last):
            self.copy(i, True).wait_recv()

    def send_z(self):
        self.buf[self.me.z] = self.vec[...]
        self.send(0, 3)

    def send_core(self):
        self.got(0, 3)
        b = self.buf
        b[4] = (b[0] + b[1]) + (b[2] + b[3])
        self.send(3, 4)

    def send_beside(self):
        self.got(3, 4)
        b = self.buf
        b[6 + self.me.x + 2 * self.me.y] = b[4] + b[5]
        self.send(4, 7)

    def take(self):
        self.got(4, 7)
        b = self.buf
        self.vec[...] = (b[6] + b[7]) + (b[8] + b[9])
        for i in range(7):
            self.copy(i).wait_send()


def place_squares(me, shards, sq, room, ssem, rsem):
    rows = lax.broadcasted_iota(jnp.int32, (192, 384), 0)
    lanes = lax.broadcasted_iota(jnp.int32, (192, 384), 1)
    spot = jnp.where(lanes == rows + me.c * 192, 1.0, 0.0).astype(BF)
    for m in range(7):
        t = dg(shards[m][...], spot, 0, 0).astype(BF)
        for half in range(2):
            room[half, 48 * m : 48 * m + 48, 0:384] = t[48 * half : 48 * half + 48]
    area = (pl.ds(0, 336), pl.ds(0, 384))
    swap = rcopy(room.at[(1 - me.c, *area)], room.at[(2, *area)], ssem, rsem, me.sibling())
    swap.start()
    swap.wait()
    for m in range(7):
        rows = slice(48 * m, 48 * m + 48)
        both = room[me.c, rows, 0:384].astype(F32) + room[2, rows, 0:384].astype(F32)
        sq[m, me.z, me.x, me.c, :, square_lanes(me.y)] = both.astype(BF)


GAIN, SHIFT, POOL = 0, 2, 4


def dg(a, b, ca, cb):
    return lax.dot_general(a, b, (((ca,), (cb,)), ((), ())), preferred_element_type=F32)


def weight(r, m):
    return r.sq[m].reshape(768, 768)


def weight_up(r, j):
    left = r.up[:, :, j, 0].reshape(768, 384)
    right = r.up[:, :, j, 1].reshape(768, 384)
    return jnp.concatenate([left, right], axis=1)


def weight_down(r, y, c, lo, hi):
    return r.down[:, :, y, c, :, lo:hi].reshape(768, hi - lo)


def set_masks(r, length):
    for i in range(2):
        row = lax.broadcasted_iota(jnp.int32, (256, 384), 0) + 256 * i
        col = lax.broadcasted_iota(jnp.int32, (256, 384), 1) + 128 * i
        ok = (jnp.abs(row - col) <= WIN) & ((row >= length) == (col >= length))
        r.bias1[i] = jnp.where(ok, 0.0, -1e30)
    row = lax.broadcasted_iota(jnp.int32, (512, 128), 0)
    col = lax.broadcasted_iota(jnp.int32, (512, 128), 1) * STRIDE
    ok = (jnp.abs(row - col) <= PWIN // 2) & ((row >= length) == (col >= length))
    r.bias2[...] = jnp.where(ok, 0.0, -1e30)


def low_lanes(rows):
    return lax.broadcasted_iota(jnp.int32, (rows, 128), 1) < HD


def two_heads(pair):
    low = low_lanes(pair.shape[0])
    zero = jnp.zeros_like(pair)
    return jnp.concatenate([jnp.where(low, pair, zero), jnp.where(low, zero, pair)], axis=0)


def side_by_side(stacked):
    n = stacked.shape[0] // 2
    return jnp.where(low_lanes(n), stacked[:n], stacked[n:])


def pair_lanes(p):
    return pl.ds(pl.multiple_of(p * 128, 128), 128)


def softmax_out(scores, bias, values, lse_ref, p):
    scores = scores + jnp.concatenate([bias, bias], axis=0)
    highest = jnp.max(scores, axis=-1, keepdims=True)
    terms = jnp.exp(scores - highest)
    summed = jnp.sum(terms, axis=-1, keepdims=True)
    probs = (terms * (1.0 / summed)).astype(BF)
    lane = lax.broadcasted_iota(jnp.int32, lse_ref.shape, 1)
    lse_ref[...] = jnp.where(lane == p, highest + jnp.log(summed), lse_ref[...])
    return side_by_side(dg(probs, values, 1, 0))


def scores_of(query, keys):
    scaled = two_heads(query * jnp.asarray(0.125, BF))
    return scaled, dg(scaled, keys, 1, 1)


def softmax_back(scores, bias, lse_ref, p, grad, values):
    scores = scores + jnp.concatenate([bias, bias], axis=0)
    lane = lax.broadcasted_iota(jnp.int32, lse_ref.shape, 1)
    lse = jnp.sum(jnp.where(lane == p, lse_ref[...], 0.0), axis=-1, keepdims=True)
    probs = jnp.exp(scores - lse)
    grad_probs = dg(grad, values, 1, 1)
    row_terms = jnp.sum(probs * grad_probs, axis=-1, keepdims=True)
    return probs.astype(BF), (probs * (grad_probs - row_terms)).astype(BF)


def project(r, lo, hi):
    @pl.loop(lo, hi)
    def _(m):
        r.qkv[m] = dg(r.tokens[...], weight(r, m), 1, 1).astype(BF)


def project_pool(r, i):
    full = None
    for l in range(6):
        lanes = slice(l * 128, l * 128 + 128)
        if l % 3 == 0:
            full = dg(r.tokens[...], r.sq[3 + i, 2 * (l // 3) : 2 * (l // 3) + 2].reshape(384, 768), 1, 1)
        r.kt[i, l, 0:8] = jnp.zeros((8, 128), F32)
        r.kt[i, l, 520:528] = jnp.zeros((8, 128), F32)
        r.kt[i, l, 8:520] = full[:, (l % 3) * 128 : (l % 3) * 128 + 128]
        total = None
        for t in range(5):
            term = r.pool[t, i : i + 1, lanes] * r.kt[i, l, pl.ds(6 + t, 128, stride=STRIDE), :]
            total = term if total is None else total + term
        r.kp[i, :, lanes] = total.astype(BF)


def at_steps(p, hooks):
    for at, hook in (hooks or {}).items():
        pl.when(p == at)(hook)


def level_one(r, hooks=None):
    @pl.loop(0, HEADS // 2)
    def _(p):
        at_steps(p, hooks)
        lanes = pair_lanes(p)
        for i in range(2):
            rows, cols = pl.ds(256 * i, 256), pl.ds(128 * i, 384)
            _, scores = scores_of(r.qkv[0, rows, lanes], r.qkv[1, cols, lanes])
            out = softmax_out(scores, r.bias1[i], r.qkv[2, cols, lanes], r.lse.at[pl.ds(512 * i, 512)], p)
            r.first[rows, lanes] = out.astype(BF)


def level_two(r):
    r.q2[...] = dg(r.first[...], weight(r, 5), 1, 1).astype(BF)

    @pl.loop(0, HEADS // 2)
    def _(p):
        lanes = pair_lanes(p)
        _, scores = scores_of(r.q2[:, lanes], r.kp[0, :, lanes])
        out = softmax_out(scores, r.bias2[...], r.kp[1, :, lanes], r.lse, p + HEADS // 2)
        r.mixed[:, lanes] = (r.first[:, lanes].astype(F32) + out).astype(BF)


def norm_parts(x):
    average = jnp.mean(x, axis=-1, keepdims=True)
    centred = x - average
    inverse = lax.rsqrt(jnp.mean(centred * centred, axis=-1, keepdims=True) + 1e-05)
    return centred * inverse, inverse


def norm_back(n, inverse, gain, grad):
    scaled = grad * gain
    return (
        scaled - jnp.mean(scaled, axis=-1, keepdims=True) - n * jnp.mean(scaled * n, axis=-1, keepdims=True)
    ) * inverse


def first_norm(r):
    r.acc[...] = dg(r.mixed[...], weight(r, 6), 1, 1)

    @pl.loop(0, 4)
    def _(i):
        rows = pl.ds(pl.multiple_of(i * 128, 128), 128)
        n, inverse = norm_parts(r.tokens[rows].astype(F32) + r.acc[rows])
        r.n1[rows] = n
        r.inv1[rows] = inverse
        r.hlow[rows] = (n * r.gains[0:1] + r.shifts[0:1]).astype(BF)


def ffn_up(r):
    k = math.sqrt(2.0 / math.pi)

    @pl.loop(0, 4)
    def _(j):
        for i in range(2):
            rows = pl.ds(256 * i, 256)
            u = dg(r.hlow[rows], weight_up(r, j), 1, 0)
            square = u * u
            t = jnp.tanh(k * u * (1.0 + 0.044715 * square))
            half = 0.5 * (1.0 + t)
            r.act[j, rows] = (u * half).astype(BF)
            slope = half + (0.5 * k) * u * (1.0 - t * t) * (1.0 + (3 * 0.044715) * square)
            r.gd[j, rows] = slope.astype(BF)


def ffn_down(r, lo, hi):
    @pl.loop(0, 2)
    def _(i):
        rows = pl.ds(pl.multiple_of(256 * i, 256), 256)
        total = r.acc[rows] if lo else None
        for j in range(4):
            term = dg(r.act[j, rows, lo:hi], weight_down(r, j // 2, j % 2, lo, hi), 1, 1)
            total = term if total is None else total + term
        r.acc[rows] = total


def second_norm(r):
    r.vec[...] = jnp.zeros_like(r.vec)

    @pl.loop(0, 4)
    def _(i):
        rows = pl.ds(pl.multiple_of(i * 128, 128), 128)
        hidden = r.n1[rows] * r.gains[0:1] + r.shifts[0:1]
        n, inverse = norm_parts(hidden + r.acc[rows])
        grad = r.og[rows].astype(F32)
        r.og[rows] = (n * r.gains[1:2] + r.shifts[1:2]).astype(BF)
        r.vec[GAIN + 1 : GAIN + 2] += jnp.sum(grad * n, axis=0, keepdims=True)
        r.vec[SHIFT + 1 : SHIFT + 2] += jnp.sum(grad, axis=0, keepdims=True)
        d = norm_back(n, inverse, r.gains[1:2], grad)
        r.dr[rows] = d
        r.dlow[rows] = d.astype(BF)


def back_down(r, c, lo, hi):
    @pl.loop(0, 2)
    def _(y):
        j = y * 2 + c
        t = dg(r.dlow[...], weight_down(r, y, c, lo, hi), 1, 0)
        r.gd[j, :, lo:hi] = (r.gd[j, :, lo:hi].astype(F32) * t).astype(BF)
        for i in range(2):
            g = dg(r.dlow[:, 384 * i : 384 * i + 384], r.act[j, :, lo:hi], 0, 0).astype(BF)
            r.down[2 * i : 2 * i + 2, :, y, c, :, lo:hi] = g.reshape(2, 2, 96, hi - lo)


def back_first_norm(r):
    @pl.loop(0, 2)
    def _(i):
        rows = pl.ds(pl.multiple_of(256 * i, 256), 256)
        total = r.dr[rows]
        for j in range(4):
            total = total + dg(r.gd[j, rows], weight_up(r, j), 1, 1)
        r.acc[rows] = total

    @pl.loop(0, 4)
    def _(i):
        rows = pl.ds(pl.multiple_of(i * 128, 128), 128)
        grad = r.acc[rows]
        n = r.n1[rows]
        r.vec[GAIN : GAIN + 1] += jnp.sum(grad * n, axis=0, keepdims=True)
        r.vec[SHIFT : SHIFT + 1] += jnp.sum(grad, axis=0, keepdims=True)
        d = norm_back(n, r.inv1[rows], r.gains[0:1], grad)
        r.dr[rows] = d
        r.dlow[rows] = d.astype(BF)


def grad_up(r):
    @pl.loop(0, 4)
    def _(j):
        for i in range(2):
            g = dg(r.hlow[:, 384 * i : 384 * i + 384], r.gd[j], 0, 0).astype(BF)
            for x in range(2):
                r.up[i, :, j, x] = g[:, x * 384 : (x + 1) * 384].reshape(2, 192, 384)


def set_grad(r, m, left, right):
    for i in range(2):
        g = dg(left[:, 384 * i : 384 * i + 384], right, 0, 0).astype(BF)
        r.sq[m, 2 * i : 2 * i + 2] = g.reshape(2, 2, 2, 48, 768)


def back_out(r):
    r.acc[...] = dg(r.dlow[...], weight(r, 6), 1, 0)
    set_grad(r, 6, r.dlow[...], r.mixed[...])


def back_level_two(r, hooks=None):
    @pl.loop(0, HEADS // 2)
    def _(p):
        at_steps(p, hooks)
        lanes = pair_lanes(p)
        scaled, scores = scores_of(r.q2[:, lanes], r.kp[0, :, lanes])
        grad = two_heads(r.acc[:, lanes].astype(BF))
        probs, grad_scores = softmax_back(
            scores, r.bias2[...], r.lse, p + HEADS // 2, grad, r.kp[1, :, lanes]
        )
        r.dpool[1][0:128, lanes] = dg(probs, grad, 0, 0).astype(BF).astype(F32)
        r.dpool[0][0:128, lanes] = dg(grad_scores, scaled, 0, 0).astype(BF).astype(F32)
        r.dq2[:, lanes] = (side_by_side(dg(grad_scores, r.kp[0, :, lanes], 1, 0)) * 0.125).astype(BF)

    r.dfirst[...] = (r.acc[...] + dg(r.dq2[...], weight(r, 5), 1, 0)).astype(BF)
    set_grad(r, 5, r.dq2[...], r.first[...])


def back_pool(r, i):
    r.dpool[i][128:136] = jnp.zeros((8, 768), F32)
    for l in range(6):
        lanes = slice(l * 128, l * 128 + 128)
        here = r.dpool[i][0:128, lanes]
        after = r.dpool[i][1:129, lanes]
        for t in range(5):
            term = here * r.kt[i, l, pl.ds(6 + t, 128, stride=STRIDE), :]
            at = POOL + 2 * t + i
            r.vec[at : at + 1, lanes] = jnp.sum(term, axis=0, keepdims=True)
        k = [r.pool[t, i : i + 1, lanes] for t in range(5)]
        r.kt[i, l, pl.ds(8, 128, stride=STRIDE), :] = k[2] * here
        r.kt[i, l, pl.ds(9, 128, stride=STRIDE), :] = k[3] * here
        r.kt[i, l, pl.ds(10, 128, stride=STRIDE), :] = k[4] * here + k[0] * after
        r.kt[i, l, pl.ds(11, 128, stride=STRIDE), :] = k[1] * after
    grad = jnp.concatenate([r.kt[i, l, 8:520].astype(BF) for l in range(6)], axis=1)
    finish_projection(r, 3 + i, grad)


def finish_projection(r, m, grad):
    r.dr[...] = r.dr[...] + dg(grad, weight(r, m), 1, 0)
    set_grad(r, m, grad, r.tokens[...])


def back_level_one(r, hooks=None):
    @pl.loop(0, HEADS)
    def _(step):
        at_steps(step, hooks)
        p, i = lax.div(step, 2), lax.rem(step, 2)
        lanes = pair_lanes(p)
        rows = pl.ds(pl.multiple_of(256 * i, 256), 256)
        cols = pl.ds(pl.multiple_of(128 * i, 128), 384)
        scaled, scores = scores_of(r.qkv[0, rows, lanes], r.qkv[1, cols, lanes])
        grad = two_heads(r.dfirst[rows, lanes])
        stacked = r.lse.at[pl.ds(pl.multiple_of(512 * i, 512), 512)]
        probs, grad_scores = softmax_back(scores, r.bias1[i], stacked, p, grad, r.qkv[2, cols, lanes])

        @pl.when(i == 0)
        def _():
            r.acc[:, 0:256] = jnp.zeros((512, 256), F32)

        r.acc[cols, 0:128] += dg(grad_scores, scaled, 0, 0)
        r.acc[cols, 128:256] += dg(probs, grad, 0, 0)
        dq = side_by_side(dg(grad_scores, r.qkv[1, cols, lanes], 1, 0)) * 0.125
        r.dqkv[0, rows, lanes] = dq.astype(BF)

        @pl.when(i == 1)
        def _():
            r.dqkv[1, :, lanes] = r.acc[:, 0:128].astype(BF)
            r.dqkv[2, :, lanes] = r.acc[:, 128:256].astype(BF)


class Refs:
    pass


ACTIVE = dict(
    qkv=((3, 512, 768), BF),
    kt=((2, 6, 528, 128), F32),
    kp=((2, 128, 768), BF),
    first=((512, 768), BF),
    q2=((512, 768), BF),
    mixed=((512, 768), BF),
    n1=((512, 768), F32),
    inv1=((512, 1), F32),
    hlow=((512, 768), BF),
    act=((4, 512, 768), BF),
    gd=((4, 512, 768), BF),
    dr=((512, 768), F32),
    acc=((512, 768), F32),
    dlow=((512, 768), BF),
    lse=((1024, 128), F32),
    bias1=((2, 256, 384), F32),
    bias2=((512, 128), F32),
)


def alias_late(r):
    r.dq2 = r.act.at[0]
    r.dfirst = r.act.at[1]
    r.dqkv = r.gd
    r.dpool = (r.n1.at[pl.ds(0, 136)], r.n1.at[pl.ds(256, 136)])


def slots(n):
    return dict(
        sq=((n, 7, 4, 48, 384), BF),
        up=((n, 4, 192, 384), BF),
        down=((n, 4, 96, 512), BF),
    )


BUFFERS = dict(
    tokens=((512, 768), BF),
    og=((512, 768), BF),
    gains=((2, 768), F32),
    shifts=((2, 768), F32),
    pool=((5, 2, 768), F32),
    shards=((7, 192, 96), BF),
    sq=(SQ, BF),
    up=(UP, BF),
    down=(DOWN, BF),
    s_sq=((7, 4, 2, 48, 768), BF),
    s_up=((2, 4, 2, 192, 384), BF),
    s_down=((4, 2, 2, 96, 768), BF),
    **{"r1_" + k: v for k, v in slots(2).items()},
    **{"r2_" + k: v for k, v in slots(1).items()},
    r3_sq=((3, 7, 48, 384), BF),
    pz=((3, 2, 2, 96, 256), BF),
    p2=((2, 96, 256), BF),
    p1=((96, 256), BF),
    b_sq=((7, 2, 48, 384), F32),
    b_up=((192, 384), F32),
    b_down=((96, 768), F32),
    vec=((16, 768), F32),
    r3_up=((3, 192, 384), BF),
    r3_down=((3, 96, 512), BF),
    vbuf=((10, 16, 768), F32),
    **ACTIVE,
)
SEMS = dict(load=20, swap=2, ag_s=(N_GROUPS, 19), ag_r=(N_GROUPS, 19), rs_s=(N_GROUPS, 10), rs_r=(N_GROUPS, 10), vs=7, vr=7, ends=4, endr=4, outs=13)


def layer_kernel(*refs):
    r = Refs()
    names = (
        ["length", "tokens_in", "og_in", "gains_in", "shifts_in", "pool_in"]
        + [f"shard{m}" for m in range(7)]
        + ["up_in", "down_in", "out", "din", "o_vec", "o_sq", "o_up", "o_down"]
        + list(BUFFERS)
        + list(SEMS)
    )
    for name, ref in zip(names, refs):
        setattr(r, name, ref)
    alias_late(r)
    me = Place()

    shards = [r.shards.at[m] for m in range(7)]
    pairs = [(getattr(r, f"shard{m}"), shards[m]) for m in range(7)]
    pairs += [
        (r.down_in, r.down.at[me.z, me.x, me.y, me.c]),
        (r.up_in, r.up.at[me.y, me.c, me.z, me.x]),
        (r.tokens_in, r.tokens),
        (r.pool_in, r.pool),
        (r.gains_in, r.gains),
        (r.shifts_in, r.shifts),
        (r.og_in, r.og),
    ]
    loads = [pltpu.make_async_copy(a, b, r.load.at[i]) for i, (a, b) in enumerate(pairs)]
    for cp in loads:
        cp.start()
    greet(me)
    weights = (r.sq, r.up, r.down)
    gat = Gather(me, weights, r.ag_s, r.ag_r)
    sca = Scatter(
        me,
        weights,
        (r.s_sq, r.s_up, r.s_down),
        (r.r1_sq, r.r1_up, r.r1_down),
        (r.r2_sq, r.r2_up, r.r2_down),
        (r.r3_sq, r.r3_up, r.r3_down),
        (r.pz, r.p2, r.p1),
        r.rs_s,
        r.rs_r,
    )

    loads[7].wait()
    gat.start(6)
    for cp in loads[:7]:
        cp.wait()
    place_squares(me, shards, r.sq, r.act, r.swap.at[0], r.swap.at[1])
    for g in range(4):
        gat.start(g)
    gat.step0(6)
    loads[8].wait()
    for g in (4, 5, 7, 8):
        gat.start(g)
    set_masks(r, r.length[0])
    gat.step1(6)
    gat.step0(0)
    gat.step0(1)
    gat.step1(0)
    gat.step0(2)
    gat.step1(1)
    gat.step0(3)
    gat.step2(6)
    gat.step2(0)
    gat.step1(2)
    gat.step0(4)
    gat.step2(1)
    gat.step3(0)
    gat.step1(3)
    gat.step0(5)
    gat.step2(2)
    gat.step3(1)
    gat.step4(0)
    gat.step1(4)
    for cp in loads[9:]:
        cp.wait()
    gat.arrived(0)
    project(r, 0, 1)
    gat.step2(3)
    gat.step3(2)
    gat.step4(1)
    gat.step1(5)
    gat.step0(7)
    gat.step0(8)
    gat.step1(7)
    gat.arrived(1)
    project(r, 1, 3)
    gat.step2(4)
    gat.step3(3)
    gat.step4(2)
    gat.step1(8)
    gat.arrived(2)
    project_pool(r, 0)
    project_pool(r, 1)

    def ahead_b():
        gat.step3(4)
        gat.step4(3)

    level_one(r, {2: lambda: gat.step2(5), 4: ahead_b})
    gat.step2(7)
    gat.step3(5)
    gat.step3(6)
    gat.step4(6)
    gat.step4(4)
    gat.arrived(3)
    level_two(r)
    gat.step2(8)
    gat.step3(7)
    gat.step4(5)
    first_norm(r)
    gat.step3(8)
    gat.step4(7)
    gat.arrived(4)
    gat.arrived(5)
    ffn_up(r)
    gat.step4(8)
    gat.arrived(6)
    gat.arrived(7)
    ffn_down(r, 0, 512)
    gat.arrived(8)
    ffn_down(r, 512, 768)
    second_norm(r)
    out = pltpu.make_async_copy(r.og, r.out, r.load.at[0])
    out.start()
    for g in range(N_GROUPS):
        gat.sent(g)

    def flush(src, dst, i):
        cp = pltpu.make_async_copy(src, dst, r.outs.at[i])
        cp.start()
        pending.append(cp)

    pending = []

    def give(g):
        kind, lo, hi = GROUPS[g]
        if kind == "u":
            r.b_up[lo:hi] = sca.finish(g)
            flush(r.b_up.at[lo:hi], r.o_up.at[lo:hi], g)
        else:
            r.b_down[:, lo:hi] = sca.finish(g)
            flush(r.b_down.at[:, lo:hi], r.o_down.at[:, lo:hi], g)

    def end_swap(g, incoming=False):
        _, lo, hi = GROUPS[g]
        b = r.b_sq.at[lo:hi, 1 - me.c if incoming else me.c]
        return rcopy(b, b, r.ends.at[g], r.endr.at[g], me.sibling())

    def end(g):
        _, lo, hi = GROUPS[g]
        r.b_sq[lo:hi, me.c] = sca.finish(g)
        end_swap(g).start()
        flush(r.b_sq.at[lo:hi, me.c], r.o_sq.at[lo:hi, me.c], g)

    def close(g):
        _, lo, hi = GROUPS[g]
        end_swap(g, True).wait_recv()
        flush(r.b_sq.at[lo:hi, 1 - me.c], r.o_sq.at[lo:hi, 1 - me.c], N_GROUPS + g)

    for g in (6, 8, 7):
        _, lo, hi = GROUPS[g]
        back_down(r, 1 - me.c, lo, hi)
        sca.start(g)
        back_down(r, me.c, lo, hi)
        sca.step1(g)
    sca.step2(6)
    back_first_norm(r)
    grad_up(r)
    sca.start(4)
    sca.start(5)
    sca.step2(7)
    sca.step3(6)
    back_out(r)
    sca.step1(4)
    sca.step1(5)
    back_level_two(r)
    sca.start(3)
    sca.step3(7)
    back_pool(r, 0)
    sca.step1(3)
    sca.step2(8)
    back_pool(r, 1)
    sca.start(2)
    total = VectorSum(me, r.vec, r.vbuf, r.vs, r.vr)
    total.send_z()

    back_level_one(
        r,
        {
            2: lambda: sca.step1(2),
            3: lambda: sca.step2(4),
            7: total.send_core,
            8: lambda: sca.step2(5),
            9: total.send_beside,
            11: lambda: sca.step3(4),
        },
    )
    finish_projection(r, 1, r.dqkv[1])
    finish_projection(r, 2, r.dqkv[2])
    sca.start(1)
    sca.step2(3)
    sca.step3(5)
    finish_projection(r, 0, r.dqkv[0])
    sca.start(0)
    sca.step1(1)
    sca.step1(0)
    sca.step3(8)
    r.dlow[...] = r.dr[...].astype(BF)
    din = pltpu.make_async_copy(r.dlow, r.din, r.load.at[1])
    din.start()
    sca.step2(2)
    sca.step3(3)
    for g in (6, 7, 4, 5):
        give(g)
    sca.step3(2)
    sca.step2(1)
    sca.step2(0)
    give(8)
    end(3)
    sca.step3(1)
    sca.step3(0)
    end(2)
    close(3)
    close(2)
    total.take()
    vec_out = pltpu.make_async_copy(r.vec, r.o_vec, r.load.at[2])
    vec_out.start()
    end(1)
    end(0)
    for g in range(N_GROUPS):
        sca.sent(g)
    close(1)
    close(0)
    for g in range(4):
        end_swap(g).wait_send()
    for cp in [*pending, out, din, vec_out]:
        cp.wait()


def layer(length, tokens, og, gains, shifts, pool, squares, up, down):
    hbm = pl.BlockSpec(memory_space=pl.ANY)
    return pl.pallas_call(
        layer_kernel,
        out_shape=[
            jax.ShapeDtypeStruct((512, 768), BF),
            jax.ShapeDtypeStruct((512, 768), BF),
            jax.ShapeDtypeStruct((16, 768), F32),
            jax.ShapeDtypeStruct((7, 2, 48, 384), F32),
            jax.ShapeDtypeStruct((192, 384), F32),
            jax.ShapeDtypeStruct((96, 768), F32),
        ],
        in_specs=[pl.BlockSpec(memory_space=pltpu.SMEM)] + [hbm] * 14,
        out_specs=[hbm] * 6,
        scratch_shapes=[pltpu.VMEM(*s) for s in BUFFERS.values()]
        + [pltpu.SemaphoreType.DMA(s if isinstance(s, tuple) else (s,)) for s in SEMS.values()],
        compiler_params=pltpu.CompilerParams(
            collective_id=0, has_side_effects=True, vmem_limit_bytes=VMEM_LIMIT
        ),
    )(length, tokens, og, gains, shifts, pool, *squares, up, down)


VMEM_LIMIT = 63 * 2**20


def ending_kernel(*refs):
    o_act, o_din, o_up, o_down = refs[6], refs[7], refs[15], refs[16]
    o_sq = refs[8:15]
    o_gain, o_shift, o_pool, vec, sq, turned, sem = refs[17:]
    copies = [
        pltpu.make_async_copy(a, b, sem.at[i])
        for i, (a, b) in enumerate(zip(refs[:6], (o_act, o_din, vec, sq, o_up, o_down)))
    ]
    for i in (3, 2, 0, 1, 4, 5):
        copies[i].start()
    core = lax.rem(lax.axis_index("dp"), 2)
    mine = pl.ds(pl.multiple_of(core * 192, 8), 192)
    copies[3].wait()
    for m in range(7):
        turned[...] = jnp.transpose(sq[m].reshape(96, 384))
        o_sq[m][...] = turned[mine, :]
    copies[2].wait()
    o_gain[...] = vec[GAIN : GAIN + 2]
    o_shift[...] = vec[SHIFT : SHIFT + 2]
    for t in range(5):
        o_pool[t] = vec[POOL + 2 * t : POOL + 2 * t + 2]
    for i in (0, 1, 4, 5):
        copies[i].wait()


def ending(*parts):
    vmem = pl.BlockSpec(memory_space=pltpu.VMEM)
    shapes = [((512, 768), BF)] * 2 + [((192, 96), F32)] * 7 + [((192, 384), F32), ((96, 768), F32)]
    shapes += [((2, 768), F32)] * 2 + [((5, 2, 768), F32)]
    return pl.pallas_call(
        ending_kernel,
        out_shape=[jax.ShapeDtypeStruct(*s) for s in shapes],
        in_specs=[pl.BlockSpec(memory_space=pl.ANY)] * 6,
        out_specs=[vmem] * len(shapes),
        scratch_shapes=[
            pltpu.VMEM((16, 768), F32),
            pltpu.VMEM((7, 2, 48, 384), F32),
            pltpu.VMEM((384, 96), F32),
            pltpu.SemaphoreType.DMA((6,)),
        ],
        compiler_params=pltpu.CompilerParams(vmem_limit_bytes=VMEM_LIMIT),
    )(*parts)


def local_kernels(
    tokens,
    doc_lengths,
    w_query,
    w_key,
    w_value,
    w_query2,
    w_key2,
    w_value2,
    w_out,
    w_up,
    w_down,
    norm_gains,
    norm_shifts,
    pool_kernels,
    out_grad,
):
    squares = (w_query, w_key, w_value, w_key2, w_value2, w_query2, w_out)
    ends = layer(
        doc_lengths,
        tokens,
        out_grad,
        norm_gains,
        norm_shifts,
        pool_kernels.transpose(1, 0, 2),
        squares,
        w_up,
        w_down.T,
    )
    act, din, g_q, g_k, g_v, g_k2, g_v2, g_q2, g_out, g_up, g_down, gain, shift, pools = ending(*ends)
    return (
        act,
        din,
        g_q,
        g_k,
        g_v,
        g_q2,
        g_k2,
        g_v2,
        g_out,
        g_up,
        g_down.T,
        gain,
        shift,
        pools.transpose(1, 0, 2),
    )


def local(
    tokens,
    doc_lengths,
    w_query,
    w_key,
    w_value,
    w_query2,
    w_key2,
    w_value2,
    w_out,
    w_up,
    w_down,
    norm_gains,
    norm_shifts,
    pool_kernels,
    out_grad,
):
    shards = (w_query, w_key, w_value, w_query2, w_key2, w_value2, w_out, w_up, w_down)
    forward_weights = gather_first(shards)
    (
        full_query,
        full_key,
        full_value,
        full_query2,
        full_key2,
        full_value2,
        full_out,
        full_up,
        full_down,
    ) = forward_weights
    seq_rows = tokens.shape[0]
    length = doc_lengths[0]
    positions = jnp.arange(seq_rows, dtype=jnp.int32)
    padding = positions >= length
    allowed_one = (jnp.abs(positions[:, None] - positions[None, :]) <= WIN) & (
        padding[:, None] == padding[None, :]
    )
    pooled_at = positions[: seq_rows // STRIDE] * STRIDE
    allowed_two = (jnp.abs(positions[:, None] - pooled_at[None, :]) <= PWIN // 2) & (
        padding[:, None] == (pooled_at >= length)[None, :]
    )
    score_scale = 1.0 / math.sqrt(HD)
    query = matmul(tokens, full_query).astype(jnp.bfloat16)
    keys = matmul(tokens, full_key).astype(jnp.bfloat16)
    values = matmul(tokens, full_value).astype(jnp.bfloat16)
    key_two = matmul(tokens, full_key2)
    value_two = matmul(tokens, full_value2)
    key_pool_f, pool_key_back = jax.vjp(pool_rows, key_two, pool_kernels[0])
    value_pool_f, pool_value_back = jax.vjp(pool_rows, value_two, pool_kernels[1])
    key_pool = key_pool_f.astype(jnp.bfloat16)
    value_pool = value_pool_f.astype(jnp.bfloat16)
    first_f, log_one = level_forward(query, keys, values, allowed_one, score_scale)
    first = first_f.astype(jnp.bfloat16)
    query_two = matmul(first, full_query2).astype(jnp.bfloat16)
    second, log_two = level_forward(query_two, key_pool, value_pool, allowed_two, score_scale)
    mixed = (first.astype(jnp.float32) + second).astype(jnp.bfloat16)
    branch = matmul(mixed, full_out)
    hidden, norm_one_back = jax.vjp(
        layer_norm, tokens.astype(jnp.float32) + branch, norm_gains[0], norm_shifts[0]
    )
    hidden_low = hidden.astype(jnp.bfloat16)
    upper = matmul(hidden_low, full_up)
    activated_f, gelu_back = jax.vjp(gelu_tanh, upper)
    activated = activated_f.astype(jnp.bfloat16)
    resid_two = hidden + matmul(activated, full_down)
    result, norm_two_back = jax.vjp(layer_norm, resid_two, norm_gains[1], norm_shifts[1])
    activations = result.astype(jnp.bfloat16)
    back_weights = gather_second(shards)
    (
        back_query,
        back_key,
        back_value,
        back_query2,
        back_key2,
        back_value2,
        back_out,
        back_up,
        back_down,
    ) = back_weights
    d_resid_two, d_gain_two, d_shift_two = norm_two_back(out_grad.astype(jnp.float32))
    d_ffn = d_resid_two.astype(jnp.bfloat16)
    grad_down = inner_rows(activated, d_ffn)
    d_upper = gelu_back(outer_cols(d_ffn, back_down))[0].astype(jnp.bfloat16)
    grad_up = inner_rows(hidden_low, d_upper)
    d_hidden = d_resid_two + outer_cols(d_upper, back_up)
    d_resid_one, d_gain_one, d_shift_one = norm_one_back(d_hidden)
    d_branch = d_resid_one.astype(jnp.bfloat16)
    grad_out = inner_rows(mixed, d_branch)
    d_mixed = outer_cols(d_branch, back_out)
    d_query_two_f, d_key_pool_f, d_value_pool_f = level_backward(
        query_two,
        key_pool,
        value_pool,
        allowed_two,
        score_scale,
        log_two,
        d_mixed.astype(jnp.bfloat16),
    )
    d_query_two = d_query_two_f.astype(jnp.bfloat16)
    d_key_pool = d_key_pool_f.astype(jnp.bfloat16)
    d_value_pool = d_value_pool_f.astype(jnp.bfloat16)
    grad_query2 = inner_rows(first, d_query_two)
    d_first = (d_mixed + outer_cols(d_query_two, back_query2)).astype(jnp.bfloat16)
    d_query_f, d_keys_f, d_values_f = level_backward(
        query, keys, values, allowed_one, score_scale, log_one, d_first
    )
    d_query = d_query_f.astype(jnp.bfloat16)
    d_keys = d_keys_f.astype(jnp.bfloat16)
    d_values = d_values_f.astype(jnp.bfloat16)
    d_key_two_f, d_pool_key = pool_key_back(d_key_pool.astype(jnp.float32))
    d_value_two_f, d_pool_value = pool_value_back(d_value_pool.astype(jnp.float32))
    d_key_two = d_key_two_f.astype(jnp.bfloat16)
    d_value_two = d_value_two_f.astype(jnp.bfloat16)
    grad_query = inner_rows(tokens, d_query)
    grad_key = inner_rows(tokens, d_keys)
    grad_value = inner_rows(tokens, d_values)
    grad_key2 = inner_rows(tokens, d_key_two)
    grad_value2 = inner_rows(tokens, d_value_two)
    d_tokens = (
        d_resid_one
        + outer_cols(d_query, back_query)
        + outer_cols(d_keys, back_key)
        + outer_cols(d_values, back_value)
    )
    d_tokens = d_tokens + outer_cols(d_key_two, back_key2) + outer_cols(d_value_two, back_value2)
    grads_all = (
        grad_query,
        grad_key,
        grad_value,
        grad_query2,
        grad_key2,
        grad_value2,
        grad_out,
        grad_up,
        grad_down,
    )
    owned = reduce_columns_first(grads_all)
    gain_stack = jnp.stack([d_gain_one, d_gain_two])
    shift_stack = jnp.stack([d_shift_one, d_shift_two])
    pool_stack = jnp.stack([d_pool_key, d_pool_value])
    vector_sums = lax.psum((gain_stack, shift_stack, pool_stack), ("dp", "fsdp"))
    return (
        activations,
        d_tokens.astype(jnp.bfloat16),
        owned[0],
        owned[1],
        owned[2],
        owned[3],
        owned[4],
        owned[5],
        owned[6],
        owned[7],
        owned[8],
        vector_sums[0],
        vector_sums[1],
        vector_sums[2],
    )


def solution(mesh):
    fits = mesh.shape["dp"] == 4 and mesh.shape["fsdp"] == 8
    return jax.shard_map(
        local_kernels if fits else local,
        mesh=mesh,
        in_specs=(
            P(("dp", "fsdp"), None),
            P(("dp", "fsdp")),
            P("dp", "fsdp"),
            P("dp", "fsdp"),
            P("dp", "fsdp"),
            P("dp", "fsdp"),
            P("dp", "fsdp"),
            P("dp", "fsdp"),
            P("dp", "fsdp"),
            P("dp", "fsdp"),
            P("dp", "fsdp"),
            P(),
            P(),
            P(),
            P(("dp", "fsdp"), None),
        ),
        out_specs=(
            P(("dp", "fsdp"), None),
            P(("dp", "fsdp"), None),
            P("dp", "fsdp"),
            P("dp", "fsdp"),
            P("dp", "fsdp"),
            P("dp", "fsdp"),
            P("dp", "fsdp"),
            P("dp", "fsdp"),
            P("dp", "fsdp"),
            P("dp", "fsdp"),
            P("dp", "fsdp"),
            P(),
            P(),
            P(),
        ),
        check_vma=False,
    )
```

```python
import math

import jax
import jax.numpy as jnp
from jax import lax
from jax.experimental import pallas as pl
from jax.experimental.pallas import tpu as pltpu
from jax.sharding import PartitionSpec as P

HEADS = 12
HD = 64
WIN = 128
PWIN = 512
STRIDE = 4


def matmul(left_mat, right_mat):
    return jnp.dot(left_mat, right_mat, preferred_element_type=jnp.float32)


def inner_rows(left_mat, right_mat):
    return lax.dot_general(
        left_mat, right_mat, (((0,), (0,)), ((), ())), preferred_element_type=jnp.float32
    )


def outer_cols(left_mat, right_mat):
    return lax.dot_general(
        left_mat, right_mat, (((1,), (1,)), ((), ())), preferred_element_type=jnp.float32
    )


def layer_norm(inputs, norm_gain, norm_shift):
    average = jnp.mean(inputs, axis=-1, keepdims=True)
    centred = inputs - average
    variance = jnp.mean(centred * centred, axis=-1, keepdims=True)
    return centred * lax.rsqrt(variance + 1e-05) * norm_gain + norm_shift


def gelu_tanh(inputs):
    return jax.nn.gelu(inputs, approximate=True)


def pool_rows(inputs, kernel):
    side_rows = (kernel.shape[0] - 1) // 2
    pooled_rows = inputs.shape[0] // STRIDE
    padded = jnp.pad(inputs, ((side_rows, side_rows), (0, 0)))
    summed = jnp.zeros((pooled_rows, inputs.shape[1]), jnp.float32)
    for offset in range(kernel.shape[0]):
        summed = summed + kernel[offset] * padded[offset : offset + inputs.shape[0] : STRIDE]
    return summed


def split_heads(matrix):
    return matrix.reshape(matrix.shape[0], HEADS // 2, 2, HD).transpose(1, 0, 2, 3)


def join_heads(groups):
    return groups.transpose(1, 0, 2, 3).reshape(groups.shape[1], HEADS * HD)


def masked_scores(query, keys, allowed, score_scale):
    raw_scores = (
        jnp.einsum("ihd,jhd->hij", query, keys, preferred_element_type=jnp.float32) * score_scale
    )
    return jnp.where(allowed[None], raw_scores, -1e30)


def attend_forward(query, keys, values, allowed, score_scale):
    scores = masked_scores(query, keys, allowed, score_scale)
    highest = jnp.max(scores, axis=-1, keepdims=True)
    expo_terms = jnp.exp(scores - highest)
    summed = jnp.sum(expo_terms, axis=-1, keepdims=True)
    soft_weights = (expo_terms / summed).astype(jnp.bfloat16)
    result = jnp.einsum("hij,jhd->ihd", soft_weights, values, preferred_element_type=jnp.float32)
    return (result, (highest + jnp.log(summed))[..., 0])


def attend_backward(query, keys, values, allowed, score_scale, log_total, grad_result):
    scores = masked_scores(query, keys, allowed, score_scale)
    soft_weights = jnp.exp(scores - log_total[..., None])
    grad_soft = jnp.einsum("ihd,jhd->hij", grad_result, values, preferred_element_type=jnp.float32)
    grad_values = jnp.einsum(
        "hij,ihd->jhd",
        soft_weights.astype(jnp.bfloat16),
        grad_result,
        preferred_element_type=jnp.float32,
    )
    row_terms = jnp.sum(soft_weights * grad_soft, axis=-1, keepdims=True)
    grad_scores = (soft_weights * (grad_soft - row_terms)).astype(jnp.bfloat16)
    grad_query = (
        jnp.einsum("hij,jhd->ihd", grad_scores, keys, preferred_element_type=jnp.float32)
        * score_scale
    )
    grad_keys = (
        jnp.einsum("hij,ihd->jhd", grad_scores, query, preferred_element_type=jnp.float32)
        * score_scale
    )
    return (grad_query, grad_keys, grad_values)


def level_forward(query, keys, values, allowed, score_scale):

    def one_group(group_parts):
        return attend_forward(group_parts[0], group_parts[1], group_parts[2], allowed, score_scale)

    results, log_totals = lax.map(
        one_group, (split_heads(query), split_heads(keys), split_heads(values))
    )
    return (join_heads(results), log_totals)


def level_backward(query, keys, values, allowed, score_scale, log_totals, grad_result):

    def one_group(group_parts):
        return attend_backward(
            group_parts[0],
            group_parts[1],
            group_parts[2],
            allowed,
            score_scale,
            group_parts[3],
            group_parts[4],
        )

    grad_query, grad_keys, grad_values = lax.map(
        one_group,
        (
            split_heads(query),
            split_heads(keys),
            split_heads(values),
            log_totals,
            split_heads(grad_result),
        ),
    )
    return (join_heads(grad_query), join_heads(grad_keys), join_heads(grad_values))


def gather_first(shards):
    column_parts = (
        lax.all_gather(shards[0], "fsdp", axis=1, tiled=True),
        lax.all_gather(shards[1], "fsdp", axis=1, tiled=True),
        lax.all_gather(shards[2], "fsdp", axis=1, tiled=True),
        lax.all_gather(shards[3], "fsdp", axis=1, tiled=True),
        lax.all_gather(shards[4], "fsdp", axis=1, tiled=True),
        lax.all_gather(shards[5], "fsdp", axis=1, tiled=True),
        lax.all_gather(shards[6], "fsdp", axis=1, tiled=True),
        lax.all_gather(shards[7], "fsdp", axis=1, tiled=True),
        lax.all_gather(shards[8], "fsdp", axis=1, tiled=True),
    )
    return (
        lax.all_gather(column_parts[0], "dp", axis=0, tiled=True),
        lax.all_gather(column_parts[1], "dp", axis=0, tiled=True),
        lax.all_gather(column_parts[2], "dp", axis=0, tiled=True),
        lax.all_gather(column_parts[3], "dp", axis=0, tiled=True),
        lax.all_gather(column_parts[4], "dp", axis=0, tiled=True),
        lax.all_gather(column_parts[5], "dp", axis=0, tiled=True),
        lax.all_gather(column_parts[6], "dp", axis=0, tiled=True),
        lax.all_gather(column_parts[7], "dp", axis=0, tiled=True),
        lax.all_gather(column_parts[8], "dp", axis=0, tiled=True),
    )


def gather_second(shards):
    column_parts = (
        lax.all_gather(shards[0], "fsdp", axis=1, tiled=True),
        lax.all_gather(shards[1], "fsdp", axis=1, tiled=True),
        lax.all_gather(shards[2], "fsdp", axis=1, tiled=True),
        lax.all_gather(shards[3], "fsdp", axis=1, tiled=True),
        lax.all_gather(shards[4], "fsdp", axis=1, tiled=True),
        lax.all_gather(shards[5], "fsdp", axis=1, tiled=True),
        lax.all_gather(shards[6], "fsdp", axis=1, tiled=True),
        lax.all_gather(shards[7], "fsdp", axis=1, tiled=True),
        lax.all_gather(shards[8], "fsdp", axis=1, tiled=True),
    )
    return (
        lax.all_gather(column_parts[0], "dp", axis=0, tiled=True),
        lax.all_gather(column_parts[1], "dp", axis=0, tiled=True),
        lax.all_gather(column_parts[2], "dp", axis=0, tiled=True),
        lax.all_gather(column_parts[3], "dp", axis=0, tiled=True),
        lax.all_gather(column_parts[4], "dp", axis=0, tiled=True),
        lax.all_gather(column_parts[5], "dp", axis=0, tiled=True),
        lax.all_gather(column_parts[6], "dp", axis=0, tiled=True),
        lax.all_gather(column_parts[7], "dp", axis=0, tiled=True),
        lax.all_gather(column_parts[8], "dp", axis=0, tiled=True),
    )


def reduce_columns_first(grads_all):
    column_sums = (
        lax.psum_scatter(
            grads_all[0].astype(jnp.bfloat16), "fsdp", scatter_dimension=1, tiled=True
        ).astype(jnp.float32),
        lax.psum_scatter(
            grads_all[1].astype(jnp.bfloat16), "fsdp", scatter_dimension=1, tiled=True
        ).astype(jnp.float32),
        lax.psum_scatter(
            grads_all[2].astype(jnp.bfloat16), "fsdp", scatter_dimension=1, tiled=True
        ).astype(jnp.float32),
        lax.psum_scatter(
            grads_all[3].astype(jnp.bfloat16), "fsdp", scatter_dimension=1, tiled=True
        ).astype(jnp.float32),
        lax.psum_scatter(
            grads_all[4].astype(jnp.bfloat16), "fsdp", scatter_dimension=1, tiled=True
        ).astype(jnp.float32),
        lax.psum_scatter(
            grads_all[5].astype(jnp.bfloat16), "fsdp", scatter_dimension=1, tiled=True
        ).astype(jnp.float32),
        lax.psum_scatter(
            grads_all[6].astype(jnp.bfloat16), "fsdp", scatter_dimension=1, tiled=True
        ).astype(jnp.float32),
        lax.psum_scatter(
            grads_all[7].astype(jnp.bfloat16), "fsdp", scatter_dimension=1, tiled=True
        ).astype(jnp.float32),
        lax.psum_scatter(
            grads_all[8].astype(jnp.bfloat16), "fsdp", scatter_dimension=1, tiled=True
        ).astype(jnp.float32),
    )
    return (
        lax.psum_scatter(
            column_sums[0].astype(jnp.bfloat16), "dp", scatter_dimension=0, tiled=True
        ).astype(jnp.float32),
        lax.psum_scatter(
            column_sums[1].astype(jnp.bfloat16), "dp", scatter_dimension=0, tiled=True
        ).astype(jnp.float32),
        lax.psum_scatter(
            column_sums[2].astype(jnp.bfloat16), "dp", scatter_dimension=0, tiled=True
        ).astype(jnp.float32),
        lax.psum_scatter(
            column_sums[3].astype(jnp.bfloat16), "dp", scatter_dimension=0, tiled=True
        ).astype(jnp.float32),
        lax.psum_scatter(
            column_sums[4].astype(jnp.bfloat16), "dp", scatter_dimension=0, tiled=True
        ).astype(jnp.float32),
        lax.psum_scatter(
            column_sums[5].astype(jnp.bfloat16), "dp", scatter_dimension=0, tiled=True
        ).astype(jnp.float32),
        lax.psum_scatter(
            column_sums[6].astype(jnp.bfloat16), "dp", scatter_dimension=0, tiled=True
        ).astype(jnp.float32),
        lax.psum_scatter(
            column_sums[7].astype(jnp.bfloat16), "dp", scatter_dimension=0, tiled=True
        ).astype(jnp.float32),
        lax.psum_scatter(
            column_sums[8].astype(jnp.bfloat16), "dp", scatter_dimension=0, tiled=True
        ).astype(jnp.float32),
    )


MESH = pl.DeviceIdType.MESH
BF = jnp.bfloat16
F32 = jnp.float32

GROUPS = (
    ("s", 0, 1),
    ("s", 1, 2),
    ("s", 3, 5),
    ("s", 5, 7),
    ("u", 0, 96),
    ("u", 96, 192),
    ("d", 0, 256),
    ("d", 256, 512),
    ("d", 512, 768),
    ("s", 2, 3),
)
SQUARES = (0, 1, 2, 3, 9)
PLANE = 8
N_GROUPS = len(GROUPS)
SQ = (7, 4, 2, 2, 48, 768)
UP = (2, 2, 4, 2, 192, 384)
DOWN = (4, 2, 2, 2, 96, 768)


class Place:
    def __init__(self):
        dp = lax.axis_index("dp")
        fs = lax.axis_index("fsdp")
        self.y = lax.div(dp, 2)
        self.c = lax.rem(dp, 2)
        self.z = lax.div(fs, 2)
        self.x = lax.rem(fs, 2)
        c, x, y = self.c, self.x, self.y
        self.p1 = ((1 - c) * (1 - x) + c * x, (1 - c) * y + c * (1 - y))
        self.p2 = ((1 - c) * x + c * (1 - x), (1 - c) * (1 - y) + c * y)
        self.own = (x, y)
        self.diag = (1 - x, 1 - y)

    def dev(self, xy, z=None, c=None):
        z = self.z if z is None else z
        c = self.c if c is None else c
        return (xy[1] * 2 + c, z * 2 + xy[0])

    def sibling(self):
        return self.dev(self.own, c=1 - self.c)

    def peer(self, k):
        return lax.rem(self.z + k, 4)

    def everyone(self):
        return [self.sibling(), self.dev(self.p1), self.dev(self.p2), self.dev(self.diag)] + [
            self.dev(self.own, z=self.peer(k)) for k in (1, 2, 3)
        ]


def greet(me):
    bar = pltpu.get_barrier_semaphore()
    for d in me.everyone():
        pl.semaphore_signal(bar, inc=1, device_id=d, device_id_type=MESH)
    pl.semaphore_wait(bar, 7)


def square_lanes(y):
    return pl.ds(pl.multiple_of(y * 384, 128), 384)


def blocks(refs, g, xy, c, z=slice(None)):
    sq, up, down = refs
    x, y = xy
    kind, lo, hi = GROUPS[g]
    if kind == "s":
        return sq.at[lo:hi, z, x, c, :, square_lanes(y)]
    if kind == "u":
        return up.at[y, c, z, x, lo:hi]
    return down.at[z, x, y, c, :, lo:hi]


def plane(down, g, c, z):
    _, lo, hi = GROUPS[g]
    return down.at[z, :, :, c, :, lo:hi]


def rcopy(src, dst, ssem, rsem, dev):
    return pltpu.make_async_remote_copy(
        src_ref=src, dst_ref=dst, send_sem=ssem, recv_sem=rsem, device_id=dev, device_id_type=MESH
    )


class Gather:
    def __init__(self, me, refs, ssem, rsem):
        self.me, self.refs, self.ssem, self.rsem = me, refs, ssem, rsem

    def copy(self, g, i, incoming=False):
        me = self.me
        ss, rs = self.ssem.at[g, i], self.rsem.at[g, i]
        side = 1 if incoming else 0
        c = me.c
        ways = ((me.own, me.p1), (me.own, me.p2), (me.p1, me.diag))
        if i < 3:
            b = blocks(self.refs, g, ways[i][side], c, me.z)
            return rcopy(b, b, ss, rs, me.dev(me.p1 if i == 0 else me.p2))
        if i < 6:
            k = i - 2
            z = lax.rem(me.z + 4 - k, 4) if incoming else me.z
            b = plane(self.refs[2], g, c, z) if g == PLANE else blocks(self.refs, g, me.own, c, z)
            return rcopy(b, b, ss, rs, me.dev(me.own, z=me.peer(k)))
        if i < 10:
            cc = 1 - c if incoming else c
            what = ((me.own, me.own), (me.p1, me.p2), (me.p2, me.p1), (me.diag, me.diag))[i - 6][side]
            if g == PLANE:
                b = plane(self.refs[2], g, cc, lax.rem(me.z + 4 - (i - 6), 4))
            else:
                b = blocks(self.refs, g, what, cc)
            return rcopy(b, b, ss, rs, me.sibling())
        way, k = (i - 10) // 3, (i - 10) % 3 + 1
        b = blocks(self.refs, g, ways[way][side], c, lax.rem(me.z + 4 - k, 4))
        return rcopy(b, b, ss, rs, me.dev(me.p1 if way == 0 else me.p2))

    def go(self, g, *which):
        for i in which:
            self.copy(g, i).start()

    def got(self, g, *which):
        for i in which:
            self.copy(g, i, True).wait_recv()

    def start(self, g):
        self.go(g, *((0, 1) if g == PLANE else (0, 1, 3, 4, 5)))

    def step0(self, g):
        self.got(g, 0)
        self.go(g, 2)

    def step1(self, g):
        if g == PLANE:
            self.got(g, 1, 2)
            self.go(g, 3, 4, 5, 6)
            return
        for k in range(3):
            self.got(g, 3 + k)
            self.go(g, 13 + k, 10 + k)
        self.go(g, 6)

    def step2(self, g):
        for k in range(3):
            self.got(g, 10 + k)
            self.go(g, 16 + k)
        self.go(g, 7)

    def step3(self, g):
        self.got(g, 1, 13, 14, 15)
        self.go(g, 8)

    def step4(self, g):
        if g == PLANE:
            for i in (3, 4, 5):
                self.got(g, i)
                self.go(g, i + 4)
            return
        self.got(g, 2, 16, 17, 18)
        self.go(g, 9)

    def arrived(self, g):
        self.got(g, 6, 7, 8, 9)

    def sent(self, g):
        for i in range(10 if g == PLANE else 19):
            self.copy(g, i).wait_send()


class Scatter:
    def __init__(self, me, refs, sib, r1, r2, r3, rp, ssem, rsem):
        self.me, self.refs, self.sib = me, refs, sib
        self.r1, self.r2, self.r3 = r1, r2, r3
        self.pz, self.p2, self.p1 = rp
        self.ssem, self.rsem = ssem, rsem

    def sib_view(self, g, xy, z=slice(None)):
        sq, up, down = self.sib
        x, y = xy
        kind, lo, hi = GROUPS[g]
        if kind == "s":
            return sq.at[lo:hi, z, x, :, square_lanes(y)]
        if kind == "u":
            return up.at[y, z, x, lo:hi]
        return down.at[z, x, y, :, lo:hi]

    def plane_of(self, g, c, z):
        return plane(self.refs[2], g, c, z)

    def sib_plane(self, g, z):
        _, lo, hi = GROUPS[g]
        return self.sib[2].at[z, :, :, :, lo:hi]

    def slot(self, bufs, g, i):
        kind, lo, hi = GROUPS[g]
        if kind == "s":
            return bufs[0].at[i, lo:hi]
        buf = bufs[1 if kind == "u" else 2]
        if kind == "d":
            return buf.at[i, :, :, lo:hi] if len(buf.shape) == 4 else buf.at[i, :, lo:hi]
        return buf.at[i, :, lo:hi] if len(buf.shape) == 4 else buf.at[i, lo:hi]

    def copy(self, g, i):
        me = self.me
        c = me.c
        ss, rs = self.ssem.at[g, i], self.rsem.at[g, i]
        if g == PLANE:
            if i < 4:
                z = me.peer(i + 1)
                return rcopy(self.plane_of(g, 1 - c, z), self.sib_plane(g, z), ss, rs, me.sibling())
            if i < 7:
                k = i - 3
                src = self.plane_of(g, c, me.peer(k))
                return rcopy(src, self.pz.at[k - 1], ss, rs, me.dev(me.own, z=me.peer(k)))
            if i < 9:
                src = blocks(self.refs, g, (me.diag, me.p2)[i - 7], c, me.z)
                return rcopy(src, self.p2.at[i - 7], ss, rs, me.dev(me.p2))
            return rcopy(blocks(self.refs, g, me.p1, c, me.z), self.p1, ss, rs, me.dev(me.p1))
        if i < 4:
            what = (me.p1, me.diag, me.p2, me.own)[i]
            return rcopy(blocks(self.refs, g, what, 1 - c), self.sib_view(g, what), ss, rs, me.sibling())
        if i < 6:
            src = blocks(self.refs, g, (me.diag, me.p2)[i - 4], c)
            return rcopy(src, self.slot(self.r1, g, i - 4), ss, rs, me.dev(me.p2))
        if i == 6:
            return rcopy(blocks(self.refs, g, me.p1, c), self.slot(self.r2, g, 0), ss, rs, me.dev(me.p1))
        k = i - 6
        src = blocks(self.refs, g, me.own, c, me.peer(k))
        return rcopy(src, self.slot(self.r3, g, k - 1), ss, rs, me.dev(me.own, z=me.peer(k)))

    def go(self, g, *which):
        for i in which:
            self.copy(g, i).start()

    def got(self, g, i):
        self.copy(g, i).wait_recv()

    def add(self, here, *others):
        total = here[...].astype(F32)
        for other in others:
            total = total + other[...].astype(F32)
        here[...] = total.astype(BF)

    def start(self, g):
        self.go(g, 0, 1, 2, 3)

    def step1(self, g):
        me = self.me
        if g == PLANE:
            for k in (1, 2, 3):
                z = me.peer(k)
                self.got(g, k - 1)
                self.add(self.plane_of(g, me.c, z), self.sib_plane(g, z))
                self.go(g, 3 + k)
            return
        for i, what, out in ((1, me.diag, 4), (0, me.p2, 5)):
            self.got(g, i)
            self.add(blocks(self.refs, g, what, me.c), self.sib_view(g, what))
            self.go(g, out)

    def step2(self, g):
        me = self.me
        if g == PLANE:
            for i in (3, 4, 5, 6):
                self.got(g, i)
            here = self.plane_of(g, me.c, me.z)
            self.add(here, self.sib_plane(g, me.z), *[self.pz.at[k] for k in range(3)])
            self.go(g, 7, 8)
            return
        self.got(g, 2)
        self.got(g, 4)
        here = blocks(self.refs, g, me.p1, me.c)
        self.add(here, self.sib_view(g, me.p1), self.slot(self.r1, g, 0))
        self.go(g, 6)

    def step3(self, g):
        me = self.me
        if g == PLANE:
            self.got(g, 7)
            self.add(blocks(self.refs, g, me.p1, me.c, me.z), self.p2.at[0])
            self.go(g, 9)
            return
        self.got(g, 3)
        self.got(g, 5)
        self.got(g, 6)
        here = blocks(self.refs, g, me.own, me.c)
        self.add(here, self.sib_view(g, me.own), self.slot(self.r1, g, 1), self.slot(self.r2, g, 0))
        self.go(g, 7, 8, 9)

    def finish(self, g):
        me = self.me
        total = blocks(self.refs, g, me.own, me.c, me.z)[...].astype(F32)
        if g == PLANE:
            self.got(g, 8)
            self.got(g, 9)
            return total + self.p2[1].astype(F32) + self.p1[...].astype(F32)
        for k in (1, 2, 3):
            self.got(g, 6 + k)
            total = total + self.slot(self.r3, g, k - 1)[...].astype(F32)
        return total

    def sent(self, g):
        for i in range(10):
            self.copy(g, i).wait_send()


class VectorSum:
    def __init__(self, me, vec, buf, ssem, rsem):
        self.me, self.vec, self.buf, self.ssem, self.rsem = me, vec, buf, ssem, rsem

    def copy(self, i, incoming=False):
        me = self.me
        if i < 3:
            z = lax.rem(me.z + 3 - i, 4) if incoming else me.z
            b, d = self.buf.at[z], me.dev(me.own, z=me.peer(i + 1))
        elif i == 3:
            return rcopy(self.buf.at[4], self.buf.at[5], self.ssem.at[i], self.rsem.at[i], me.sibling())
        else:
            x, y = ((1 - me.x, me.y), (me.x, 1 - me.y), me.diag)[i - 4]
            fx, fy = (x, y) if incoming else me.own
            b, d = self.buf.at[6 + fx + 2 * fy], me.dev((x, y))
        return rcopy(b, b, self.ssem.at[i], self.rsem.at[i], d)

    def send(self, first, last):
        for i in range(first, last):
            self.copy(i).start()

    def got(self, first, last):
        for i in range(first, last):
            self.copy(i, True).wait_recv()

    def send_z(self):
        self.buf[self.me.z] = self.vec[...]
        self.send(0, 3)

    def send_core(self):
        self.got(0, 3)
        b = self.buf
        b[4] = (b[0] + b[1]) + (b[2] + b[3])
        self.send(3, 4)

    def send_beside(self):
        self.got(3, 4)
        b = self.buf
        b[6 + self.me.x + 2 * self.me.y] = b[4] + b[5]
        self.send(4, 7)

    def take(self):
        self.got(4, 7)
        b = self.buf
        self.vec[...] = (b[6] + b[7]) + (b[8] + b[9])
        for i in range(7):
            self.copy(i).wait_send()


def place_squares(me, shards, sq, room, ssem, rsem):
    rows = lax.broadcasted_iota(jnp.int32, (192, 384), 0)
    lanes = lax.broadcasted_iota(jnp.int32, (192, 384), 1)
    spot = jnp.where(lanes == rows + me.c * 192, 1.0, 0.0).astype(BF)
    for m in range(7):
        t = dg(shards[m][...], spot, 0, 0).astype(BF)
        for half in range(2):
            room[half, 48 * m : 48 * m + 48, 0:384] = t[48 * half : 48 * half + 48]
    area = (pl.ds(0, 336), pl.ds(0, 384))
    swap = rcopy(room.at[(1 - me.c, *area)], room.at[(2, *area)], ssem, rsem, me.sibling())
    swap.start()
    swap.wait()
    for m in range(7):
        rows = slice(48 * m, 48 * m + 48)
        both = room[me.c, rows, 0:384].astype(F32) + room[2, rows, 0:384].astype(F32)
        sq[m, me.z, me.x, me.c, :, square_lanes(me.y)] = both.astype(BF)


GAIN, SHIFT, POOL = 0, 2, 4


def dg(a, b, ca, cb):
    return lax.dot_general(a, b, (((ca,), (cb,)), ((), ())), preferred_element_type=F32)


def weight(r, m):
    return r.sq[m].reshape(768, 768)


def weight_up(r, j):
    left = r.up[:, :, j, 0].reshape(768, 384)
    right = r.up[:, :, j, 1].reshape(768, 384)
    return jnp.concatenate([left, right], axis=1)


def weight_down(r, y, c, lo, hi):
    return r.down[:, :, y, c, :, lo:hi].reshape(768, hi - lo)


def set_masks(r, length):
    for i in range(2):
        row = lax.broadcasted_iota(jnp.int32, (256, 384), 0) + 256 * i
        col = lax.broadcasted_iota(jnp.int32, (256, 384), 1) + 128 * i
        ok = (jnp.abs(row - col) <= WIN) & ((row >= length) == (col >= length))
        r.bias1[i] = jnp.where(ok, 0.0, -1e30)
    row = lax.broadcasted_iota(jnp.int32, (512, 128), 0)
    col = lax.broadcasted_iota(jnp.int32, (512, 128), 1) * STRIDE
    ok = (jnp.abs(row - col) <= PWIN // 2) & ((row >= length) == (col >= length))
    r.bias2[...] = jnp.where(ok, 0.0, -1e30)


def low_lanes(rows):
    return lax.broadcasted_iota(jnp.int32, (rows, 128), 1) < HD


def two_heads(pair):
    low = low_lanes(pair.shape[0])
    zero = jnp.zeros_like(pair)
    return jnp.concatenate([jnp.where(low, pair, zero), jnp.where(low, zero, pair)], axis=0)


def side_by_side(stacked):
    n = stacked.shape[0] // 2
    return jnp.where(low_lanes(n), stacked[:n], stacked[n:])


def pair_lanes(p):
    return pl.ds(pl.multiple_of(p * 128, 128), 128)


def softmax_out(scores, bias, values, lse_ref, p):
    scores = scores + jnp.concatenate([bias, bias], axis=0)
    highest = jnp.max(scores, axis=-1, keepdims=True)
    terms = jnp.exp(scores - highest)
    summed = jnp.sum(terms, axis=-1, keepdims=True)
    probs = (terms * (1.0 / summed)).astype(BF)
    lane = lax.broadcasted_iota(jnp.int32, lse_ref.shape, 1)
    lse_ref[...] = jnp.where(lane == p, highest + jnp.log(summed), lse_ref[...])
    return side_by_side(dg(probs, values, 1, 0))


def scores_of(query, keys):
    scaled = two_heads(query * jnp.asarray(0.125, BF))
    return scaled, dg(scaled, keys, 1, 1)


def softmax_back(scores, bias, lse_ref, p, grad, values):
    scores = scores + jnp.concatenate([bias, bias], axis=0)
    lane = lax.broadcasted_iota(jnp.int32, lse_ref.shape, 1)
    lse = jnp.sum(jnp.where(lane == p, lse_ref[...], 0.0), axis=-1, keepdims=True)
    probs = jnp.exp(scores - lse)
    grad_probs = dg(grad, values, 1, 1)
    row_terms = jnp.sum(probs * grad_probs, axis=-1, keepdims=True)
    return probs.astype(BF), (probs * (grad_probs - row_terms)).astype(BF)


def project(r, lo, hi):
    @pl.loop(lo, hi)
    def _(m):
        r.qkv[m] = dg(r.tokens[...], weight(r, m), 1, 1).astype(BF)


def project_pool(r, i):
    full = None
    for l in range(6):
        lanes = slice(l * 128, l * 128 + 128)
        if l % 3 == 0:
            full = dg(r.tokens[...], r.sq[3 + i, 2 * (l // 3) : 2 * (l // 3) + 2].reshape(384, 768), 1, 1)
        r.kt[i, l, 0:8] = jnp.zeros((8, 128), F32)
        r.kt[i, l, 520:528] = jnp.zeros((8, 128), F32)
        r.kt[i, l, 8:520] = full[:, (l % 3) * 128 : (l % 3) * 128 + 128]
        total = None
        for t in range(5):
            term = r.pool[t, i : i + 1, lanes] * r.kt[i, l, pl.ds(6 + t, 128, stride=STRIDE), :]
            total = term if total is None else total + term
        r.kp[i, :, lanes] = total.astype(BF)


def at_steps(p, hooks):
    for at, hook in (hooks or {}).items():
        pl.when(p == at)(hook)


def level_one(r, hooks=None):
    @pl.loop(0, HEADS // 2)
    def _(p):
        at_steps(p, hooks)
        lanes = pair_lanes(p)
        for i in range(2):
            rows, cols = pl.ds(256 * i, 256), pl.ds(128 * i, 384)
            _, scores = scores_of(r.qkv[0, rows, lanes], r.qkv[1, cols, lanes])
            out = softmax_out(scores, r.bias1[i], r.qkv[2, cols, lanes], r.lse.at[pl.ds(512 * i, 512)], p)
            r.first[rows, lanes] = out.astype(BF)


def level_two(r, hooks=None):
    r.q2[...] = dg(r.first[...], weight(r, 5), 1, 1).astype(BF)

    @pl.loop(0, HEADS // 2)
    def _(p):
        at_steps(p, hooks)
        lanes = pair_lanes(p)
        _, scores = scores_of(r.q2[:, lanes], r.kp[0, :, lanes])
        out = softmax_out(scores, r.bias2[...], r.kp[1, :, lanes], r.lse, p + HEADS // 2)
        r.mixed[:, lanes] = (r.first[:, lanes].astype(F32) + out).astype(BF)


def norm_parts(x):
    average = jnp.mean(x, axis=-1, keepdims=True)
    centred = x - average
    inverse = lax.rsqrt(jnp.mean(centred * centred, axis=-1, keepdims=True) + 1e-05)
    return centred * inverse, inverse


def norm_back(n, inverse, gain, grad):
    scaled = grad * gain
    return (
        scaled - jnp.mean(scaled, axis=-1, keepdims=True) - n * jnp.mean(scaled * n, axis=-1, keepdims=True)
    ) * inverse


def first_norm(r):
    r.acc[...] = dg(r.mixed[...], weight(r, 6), 1, 1)

    @pl.loop(0, 4)
    def _(i):
        rows = pl.ds(pl.multiple_of(i * 128, 128), 128)
        n, inverse = norm_parts(r.tokens[rows].astype(F32) + r.acc[rows])
        r.n1[rows] = n
        r.inv1[rows] = inverse
        r.hlow[rows] = (n * r.gains[0:1] + r.shifts[0:1]).astype(BF)


def ffn_up(r, hooks=None):
    k = math.sqrt(2.0 / math.pi)

    @pl.loop(0, 4)
    def _(j):
        at_steps(j, hooks)
        for i in range(2):
            rows = pl.ds(256 * i, 256)
            u = dg(r.hlow[rows], weight_up(r, j), 1, 0)
            square = u * u
            half = 0.5 + 0.5 * jnp.tanh(u * (k + (k * 0.044715) * square))
            value = u * half
            r.act[j, rows] = value.astype(BF)
            slope = half + value * (1.0 - half) * (2 * k + (6 * k * 0.044715) * square)
            r.gd[j, rows] = slope.astype(BF)


def ffn_down(r, lo, hi, first):
    @pl.loop(0, 2)
    def _(i):
        rows = pl.ds(pl.multiple_of(256 * i, 256), 256)
        total = None if first else r.acc[rows]
        for j in range(4):
            term = dg(r.act[j, rows, lo:hi], weight_down(r, j // 2, j % 2, lo, hi), 1, 1)
            total = term if total is None else total + term
        r.acc[rows] = total


def second_norm(r):
    r.vec[...] = jnp.zeros_like(r.vec)

    @pl.loop(0, 4)
    def _(i):
        rows = pl.ds(pl.multiple_of(i * 128, 128), 128)
        hidden = r.n1[rows] * r.gains[0:1] + r.shifts[0:1]
        n, inverse = norm_parts(hidden + r.acc[rows])
        grad = r.og[rows].astype(F32)
        r.og[rows] = (n * r.gains[1:2] + r.shifts[1:2]).astype(BF)
        r.vec[GAIN + 1 : GAIN + 2] += jnp.sum(grad * n, axis=0, keepdims=True)
        r.vec[SHIFT + 1 : SHIFT + 2] += jnp.sum(grad, axis=0, keepdims=True)
        d = norm_back(n, inverse, r.gains[1:2], grad)
        r.dr[rows] = d
        r.dlow[rows] = d.astype(BF)


def back_down(r, c, lo, hi):
    @pl.loop(0, 2)
    def _(y):
        j = y * 2 + c
        t = dg(r.dlow[...], weight_down(r, y, c, lo, hi), 1, 0)
        r.gd[j, :, lo:hi] = (r.gd[j, :, lo:hi].astype(F32) * t).astype(BF)
        g = dg(r.dlow[...], r.act[j, :, lo:hi], 0, 0).astype(BF)
        r.down[:, :, y, c, :, lo:hi] = g.reshape(4, 2, 96, hi - lo)


def back_hidden(r):
    @pl.loop(0, 2)
    def _(i):
        rows = pl.ds(pl.multiple_of(256 * i, 256), 256)
        total = r.dr[rows]
        for j in range(4):
            total = total + dg(r.gd[j, rows], weight_up(r, j), 1, 1)
        r.acc[rows] = total


def back_first_norm(r):
    @pl.loop(0, 4)
    def _(i):
        rows = pl.ds(pl.multiple_of(i * 128, 128), 128)
        grad = r.acc[rows]
        n = r.n1[rows]
        r.vec[GAIN : GAIN + 1] += jnp.sum(grad * n, axis=0, keepdims=True)
        r.vec[SHIFT : SHIFT + 1] += jnp.sum(grad, axis=0, keepdims=True)
        d = norm_back(n, r.inv1[rows], r.gains[0:1], grad)
        r.dr[rows] = d
        r.dlow[rows] = d.astype(BF)


def grad_up(r):
    @pl.loop(0, 4)
    def _(j):
        for i in range(2):
            g = dg(r.hlow[:, 384 * i : 384 * i + 384], r.gd[j], 0, 0).astype(BF)
            for x in range(2):
                r.up[i, :, j, x] = g[:, x * 384 : (x + 1) * 384].reshape(2, 192, 384)


def set_grad(r, m, left, right):
    for i in range(2):
        g = dg(left[:, 384 * i : 384 * i + 384], right, 0, 0).astype(BF)
        r.sq[m, 2 * i : 2 * i + 2] = g.reshape(2, 2, 2, 48, 768)


def back_out(r):
    r.acc[...] = dg(r.dlow[...], weight(r, 6), 1, 0)
    set_grad(r, 6, r.dlow[...], r.mixed[...])


def back_level_two(r, hooks=None):
    @pl.loop(0, HEADS // 2)
    def _(p):
        at_steps(p, hooks)
        lanes = pair_lanes(p)
        scaled, scores = scores_of(r.q2[:, lanes], r.kp[0, :, lanes])
        grad = two_heads(r.acc[:, lanes].astype(BF))
        probs, grad_scores = softmax_back(
            scores, r.bias2[...], r.lse, p + HEADS // 2, grad, r.kp[1, :, lanes]
        )
        r.dpool[1][0:128, lanes] = dg(probs, grad, 0, 0).astype(BF).astype(F32)
        r.dpool[0][0:128, lanes] = dg(grad_scores, scaled, 0, 0).astype(BF).astype(F32)
        r.dq2[:, lanes] = (side_by_side(dg(grad_scores, r.kp[0, :, lanes], 1, 0)) * 0.125).astype(BF)

    r.dfirst[...] = (r.acc[...] + dg(r.dq2[...], weight(r, 5), 1, 0)).astype(BF)
    set_grad(r, 5, r.dq2[...], r.first[...])


def back_pool(r, i):
    r.dpool[i][128:136] = jnp.zeros((8, 768), F32)
    for l in range(6):
        lanes = slice(l * 128, l * 128 + 128)
        here = r.dpool[i][0:128, lanes]
        after = r.dpool[i][1:129, lanes]
        for t in range(5):
            term = here * r.kt[i, l, pl.ds(6 + t, 128, stride=STRIDE), :]
            at = POOL + 2 * t + i
            r.vec[at : at + 1, lanes] = jnp.sum(term, axis=0, keepdims=True)
        k = [r.pool[t, i : i + 1, lanes] for t in range(5)]
        r.kt[i, l, pl.ds(8, 128, stride=STRIDE), :] = k[2] * here
        r.kt[i, l, pl.ds(9, 128, stride=STRIDE), :] = k[3] * here
        r.kt[i, l, pl.ds(10, 128, stride=STRIDE), :] = k[4] * here + k[0] * after
        r.kt[i, l, pl.ds(11, 128, stride=STRIDE), :] = k[1] * after
    grad = jnp.concatenate([r.kt[i, l, 8:520].astype(BF) for l in range(6)], axis=1)
    finish_projection(r, 3 + i, grad)


def finish_projection(r, m, grad):
    r.dr[...] = r.dr[...] + dg(grad, weight(r, m), 1, 0)
    set_grad(r, m, grad, r.tokens[...])


def back_level_one(r, hooks=None):
    @pl.loop(0, HEADS)
    def _(step):
        at_steps(step, hooks)
        p, i = lax.div(step, 2), lax.rem(step, 2)
        lanes = pair_lanes(p)
        rows = pl.ds(pl.multiple_of(256 * i, 256), 256)
        cols = pl.ds(pl.multiple_of(128 * i, 128), 384)
        scaled, scores = scores_of(r.qkv[0, rows, lanes], r.qkv[1, cols, lanes])
        grad = two_heads(r.dfirst[rows, lanes])
        stacked = r.lse.at[pl.ds(pl.multiple_of(512 * i, 512), 512)]
        probs, grad_scores = softmax_back(scores, r.bias1[i], stacked, p, grad, r.qkv[2, cols, lanes])

        @pl.when(i == 0)
        def _():
            r.acc[:, 0:256] = jnp.zeros((512, 256), F32)

        r.acc[cols, 0:128] += dg(grad_scores, scaled, 0, 0)
        r.acc[cols, 128:256] += dg(probs, grad, 0, 0)
        dq = side_by_side(dg(grad_scores, r.qkv[1, cols, lanes], 1, 0)) * 0.125
        r.dqkv[0, rows, lanes] = dq.astype(BF)

        @pl.when(i == 1)
        def _():
            r.dqkv[1, :, lanes] = r.acc[:, 0:128].astype(BF)
            r.dqkv[2, :, lanes] = r.acc[:, 128:256].astype(BF)


class Refs:
    pass


ACTIVE = dict(
    qkv=((3, 512, 768), BF),
    kt=((2, 6, 528, 128), F32),
    kp=((2, 128, 768), BF),
    first=((512, 768), BF),
    q2=((512, 768), BF),
    mixed=((512, 768), BF),
    n1=((512, 768), F32),
    inv1=((512, 1), F32),
    hlow=((512, 768), BF),
    act=((4, 512, 768), BF),
    gd=((4, 512, 768), BF),
    dr=((512, 768), F32),
    acc=((512, 768), F32),
    dlow=((512, 768), BF),
    lse=((1024, 128), F32),
    bias1=((2, 256, 384), F32),
    bias2=((512, 128), F32),
)


def alias_late(r):
    r.dq2 = r.act.at[0]
    r.dfirst = r.act.at[1]
    r.dqkv = r.gd
    r.dpool = (r.n1.at[pl.ds(0, 136)], r.n1.at[pl.ds(256, 136)])


def slots(n):
    return dict(
        sq=((n, 7, 4, 48, 384), BF),
        up=((n, 4, 192, 384), BF),
        down=((n, 4, 96, 512), BF),
    )


BUFFERS = dict(
    tokens=((512, 768), BF),
    og=((512, 768), BF),
    gains=((2, 768), F32),
    shifts=((2, 768), F32),
    pool=((5, 2, 768), F32),
    shards=((7, 192, 96), BF),
    sq=(SQ, BF),
    up=(UP, BF),
    down=(DOWN, BF),
    s_sq=((7, 4, 2, 48, 768), BF),
    s_up=((2, 4, 2, 192, 384), BF),
    s_down=((4, 2, 2, 96, 768), BF),
    **{"r1_" + k: v for k, v in slots(2).items()},
    **{"r2_" + k: v for k, v in slots(1).items()},
    r3_sq=((3, 7, 48, 384), BF),
    pz=((3, 2, 2, 96, 256), BF),
    p2=((2, 96, 256), BF),
    p1=((96, 256), BF),
    b_sq=((7, 2, 48, 384), F32),
    b_up=((192, 384), F32),
    b_down=((96, 768), F32),
    vec=((16, 768), F32),
    r3_up=((3, 192, 384), BF),
    r3_down=((3, 96, 512), BF),
    vbuf=((10, 16, 768), F32),
    **ACTIVE,
)
SEMS = dict(load=20, swap=2, ag_s=(N_GROUPS, 19), ag_r=(N_GROUPS, 19), rs_s=(N_GROUPS, 10), rs_r=(N_GROUPS, 10), vs=7, vr=7, ends=N_GROUPS, endr=N_GROUPS, outs=2 * N_GROUPS)


def layer_kernel(*refs):
    r = Refs()
    names = (
        ["length", "tokens_in", "og_in", "gains_in", "shifts_in", "pool_in"]
        + [f"shard{m}" for m in range(7)]
        + ["up_in", "down_in", "out", "din", "o_vec", "o_sq", "o_up", "o_down"]
        + list(BUFFERS)
        + list(SEMS)
    )
    for name, ref in zip(names, refs):
        setattr(r, name, ref)
    alias_late(r)
    me = Place()

    shards = [r.shards.at[m] for m in range(7)]
    pairs = [(getattr(r, f"shard{m}"), shards[m]) for m in range(7)]
    pairs += [
        (r.down_in, r.down.at[me.z, me.x, me.y, me.c]),
        (r.up_in, r.up.at[me.y, me.c, me.z, me.x]),
        (r.tokens_in, r.tokens),
        (r.pool_in, r.pool),
        (r.gains_in, r.gains),
        (r.shifts_in, r.shifts),
        (r.og_in, r.og),
    ]
    loads = [pltpu.make_async_copy(a, b, r.load.at[i]) for i, (a, b) in enumerate(pairs)]
    for cp in loads:
        cp.start()
    greet(me)
    weights = (r.sq, r.up, r.down)
    gat = Gather(me, weights, r.ag_s, r.ag_r)
    sca = Scatter(
        me,
        weights,
        (r.s_sq, r.s_up, r.s_down),
        (r.r1_sq, r.r1_up, r.r1_down),
        (r.r2_sq, r.r2_up, r.r2_down),
        (r.r3_sq, r.r3_up, r.r3_down),
        (r.pz, r.p2, r.p1),
        r.rs_s,
        r.rs_r,
    )

    loads[7].wait()
    gat.start(8)
    gat.go(6, 0, 1)
    for cp in loads[:7]:
        cp.wait()
    place_squares(me, shards, r.sq, r.act, r.swap.at[0], r.swap.at[1])
    for g in (0, 1, 9, 2, 3):
        gat.start(g)
    gat.step0(8)
    gat.step0(6)
    loads[8].wait()
    gat.start(4)
    gat.start(5)
    gat.go(6, 3, 4, 5)
    gat.start(7)
    set_masks(r, r.length[0])
    gat.step0(0)
    gat.step0(1)
    gat.step1(0)
    gat.step0(9)
    gat.step0(2)
    gat.step1(1)
    gat.step1(9)
    gat.step0(3)
    gat.step2(0)
    gat.step1(2)
    gat.step0(4)
    gat.step2(1)
    gat.step2(9)
    gat.step3(0)
    gat.step1(3)
    gat.step0(5)
    gat.step2(2)
    gat.step3(1)
    gat.step4(0)
    gat.step1(4)
    for cp in loads[9:]:
        cp.wait()
    gat.arrived(0)
    project(r, 0, 1)
    gat.step2(3)
    gat.step3(9)
    gat.step3(2)
    gat.step4(1)
    gat.step1(5)
    gat.step0(7)
    gat.step4(9)
    gat.arrived(1)
    project(r, 1, 2)
    gat.step1(6)
    gat.step2(4)
    gat.arrived(9)
    project(r, 2, 3)
    gat.step1(7)
    gat.step1(8)

    def ahead_a():
        gat.step4(2)
        gat.step2(5)

    level_one(r, {2: lambda: gat.step3(3), 4: ahead_a})
    gat.step3(4)
    gat.arrived(2)
    project_pool(r, 0)
    project_pool(r, 1)
    gat.step4(3)
    gat.step2(6)
    gat.arrived(3)

    def ahead_c():
        gat.step4(4)
        gat.step3(5)

    level_two(r, {3: ahead_c, 5: lambda: gat.step2(7)})
    first_norm(r)
    gat.step4(5)
    gat.arrived(4)
    gat.arrived(5)
    ffn_up(r, {1: lambda: gat.step3(6), 2: lambda: gat.step4(8), 3: lambda: gat.step4(6)})
    gat.step3(7)
    gat.arrived(8)
    ffn_down(r, 512, 768, True)
    gat.arrived(6)
    gat.step4(7)
    ffn_down(r, 0, 256, False)
    gat.arrived(7)
    ffn_down(r, 256, 512, False)
    second_norm(r)
    out = pltpu.make_async_copy(r.og, r.out, r.load.at[0])
    out.start()
    for g in range(N_GROUPS):
        gat.sent(g)

    def flush(src, dst, i):
        cp = pltpu.make_async_copy(src, dst, r.outs.at[i])
        cp.start()
        pending.append(cp)

    pending = []

    def give(g):
        kind, lo, hi = GROUPS[g]
        if kind == "u":
            r.b_up[lo:hi] = sca.finish(g)
            flush(r.b_up.at[lo:hi], r.o_up.at[lo:hi], g)
        else:
            r.b_down[:, lo:hi] = sca.finish(g)
            flush(r.b_down.at[:, lo:hi], r.o_down.at[:, lo:hi], g)

    def end_swap(g, incoming=False):
        _, lo, hi = GROUPS[g]
        b = r.b_sq.at[lo:hi, 1 - me.c if incoming else me.c]
        return rcopy(b, b, r.ends.at[g], r.endr.at[g], me.sibling())

    def end(g):
        _, lo, hi = GROUPS[g]
        r.b_sq[lo:hi, me.c] = sca.finish(g)
        end_swap(g).start()
        flush(r.b_sq.at[lo:hi, me.c], r.o_sq.at[lo:hi, me.c], g)

    def close(g):
        _, lo, hi = GROUPS[g]
        end_swap(g, True).wait_recv()
        flush(r.b_sq.at[lo:hi, 1 - me.c], r.o_sq.at[lo:hi, 1 - me.c], N_GROUPS + g)

    for g in (6, 8, 7):
        _, lo, hi = GROUPS[g]
        back_down(r, 1 - me.c, lo, hi)
        sca.start(g)
        back_down(r, me.c, lo, hi)
        sca.step1(g)
    sca.step2(6)
    back_hidden(r)
    grad_up(r)
    sca.start(4)
    sca.start(5)
    back_first_norm(r)
    sca.step2(7)
    sca.step3(6)
    back_out(r)
    sca.step1(4)
    sca.step1(5)
    back_level_two(r)
    sca.start(3)
    sca.step3(7)
    back_pool(r, 0)
    sca.step1(3)
    sca.step2(8)
    back_pool(r, 1)
    sca.start(2)
    total = VectorSum(me, r.vec, r.vbuf, r.vs, r.vr)
    total.send_z()

    back_level_one(
        r,
        {
            0: lambda: sca.step2(4),
            2: lambda: sca.step1(2),
            5: lambda: sca.step2(5),
            7: total.send_core,
            9: total.send_beside,
            11: lambda: sca.step3(4),
        },
    )
    finish_projection(r, 1, r.dqkv[1])
    sca.start(1)
    finish_projection(r, 2, r.dqkv[2])
    sca.start(9)
    sca.step1(1)
    sca.step2(3)
    finish_projection(r, 0, r.dqkv[0])
    sca.start(0)
    sca.step1(9)
    sca.step3(5)
    sca.step1(0)
    sca.step3(8)
    r.dlow[...] = r.dr[...].astype(BF)
    din = pltpu.make_async_copy(r.dlow, r.din, r.load.at[1])
    din.start()
    sca.step2(2)
    sca.step3(3)
    for g in (6, 7, 4, 5):
        give(g)
    sca.step2(1)
    sca.step3(2)
    sca.step2(9)
    give(8)
    sca.step3(1)
    sca.step2(0)
    end(3)
    sca.step3(9)
    sca.step3(0)
    end(2)
    close(3)
    close(2)
    total.take()
    vec_out = pltpu.make_async_copy(r.vec, r.o_vec, r.load.at[2])
    vec_out.start()
    end(1)
    end(9)
    end(0)
    for g in range(N_GROUPS):
        sca.sent(g)
    close(1)
    close(9)
    close(0)
    for g in SQUARES:
        end_swap(g).wait_send()
    for cp in [*pending, out, din, vec_out]:
        cp.wait()


def layer(length, tokens, og, gains, shifts, pool, squares, up, down):
    hbm = pl.BlockSpec(memory_space=pl.ANY)
    return pl.pallas_call(
        layer_kernel,
        out_shape=[
            jax.ShapeDtypeStruct((512, 768), BF),
            jax.ShapeDtypeStruct((512, 768), BF),
            jax.ShapeDtypeStruct((16, 768), F32),
            jax.ShapeDtypeStruct((7, 2, 48, 384), F32),
            jax.ShapeDtypeStruct((192, 384), F32),
            jax.ShapeDtypeStruct((96, 768), F32),
        ],
        in_specs=[pl.BlockSpec(memory_space=pltpu.SMEM)] + [hbm] * 14,
        out_specs=[hbm] * 6,
        scratch_shapes=[pltpu.VMEM(*s) for s in BUFFERS.values()]
        + [pltpu.SemaphoreType.DMA(s if isinstance(s, tuple) else (s,)) for s in SEMS.values()],
        compiler_params=pltpu.CompilerParams(
            collective_id=0, has_side_effects=True, vmem_limit_bytes=VMEM_LIMIT
        ),
    )(length, tokens, og, gains, shifts, pool, *squares, up, down)


VMEM_LIMIT = 63 * 2**20


def ending_kernel(*refs):
    o_act, o_din, o_up, o_down = refs[6], refs[7], refs[15], refs[16]
    o_sq = refs[8:15]
    o_gain, o_shift, o_pool, vec, sq, turned, sem = refs[17:]
    copies = [
        pltpu.make_async_copy(a, b, sem.at[i])
        for i, (a, b) in enumerate(zip(refs[:6], (o_act, o_din, vec, sq, o_up, o_down)))
    ]
    for i in (3, 2, 0, 1, 4, 5):
        copies[i].start()
    core = lax.rem(lax.axis_index("dp"), 2)
    mine = pl.ds(pl.multiple_of(core * 192, 8), 192)
    copies[3].wait()
    for m in range(7):
        turned[...] = jnp.transpose(sq[m].reshape(96, 384))
        o_sq[m][...] = turned[mine, :]
    copies[2].wait()
    o_gain[...] = vec[GAIN : GAIN + 2]
    o_shift[...] = vec[SHIFT : SHIFT + 2]
    for t in range(5):
        o_pool[t] = vec[POOL + 2 * t : POOL + 2 * t + 2]
    for i in (0, 1, 4, 5):
        copies[i].wait()


def ending(*parts):
    vmem = pl.BlockSpec(memory_space=pltpu.VMEM)
    shapes = [((512, 768), BF)] * 2 + [((192, 96), F32)] * 7 + [((192, 384), F32), ((96, 768), F32)]
    shapes += [((2, 768), F32)] * 2 + [((5, 2, 768), F32)]
    return pl.pallas_call(
        ending_kernel,
        out_shape=[jax.ShapeDtypeStruct(*s) for s in shapes],
        in_specs=[pl.BlockSpec(memory_space=pl.ANY)] * 6,
        out_specs=[vmem] * len(shapes),
        scratch_shapes=[
            pltpu.VMEM((16, 768), F32),
            pltpu.VMEM((7, 2, 48, 384), F32),
            pltpu.VMEM((384, 96), F32),
            pltpu.SemaphoreType.DMA((6,)),
        ],
        compiler_params=pltpu.CompilerParams(vmem_limit_bytes=VMEM_LIMIT),
    )(*parts)


def local_kernels(
    tokens,
    doc_lengths,
    w_query,
    w_key,
    w_value,
    w_query2,
    w_key2,
    w_value2,
    w_out,
    w_up,
    w_down,
    norm_gains,
    norm_shifts,
    pool_kernels,
    out_grad,
):
    squares = (w_query, w_key, w_value, w_key2, w_value2, w_query2, w_out)
    ends = layer(
        doc_lengths,
        tokens,
        out_grad,
        norm_gains,
        norm_shifts,
        pool_kernels.transpose(1, 0, 2),
        squares,
        w_up,
        w_down.T,
    )
    act, din, g_q, g_k, g_v, g_k2, g_v2, g_q2, g_out, g_up, g_down, gain, shift, pools = ending(*ends)
    return (
        act,
        din,
        g_q,
        g_k,
        g_v,
        g_q2,
        g_k2,
        g_v2,
        g_out,
        g_up,
        g_down.T,
        gain,
        shift,
        pools.transpose(1, 0, 2),
    )


def local(
    tokens,
    doc_lengths,
    w_query,
    w_key,
    w_value,
    w_query2,
    w_key2,
    w_value2,
    w_out,
    w_up,
    w_down,
    norm_gains,
    norm_shifts,
    pool_kernels,
    out_grad,
):
    shards = (w_query, w_key, w_value, w_query2, w_key2, w_value2, w_out, w_up, w_down)
    forward_weights = gather_first(shards)
    (
        full_query,
        full_key,
        full_value,
        full_query2,
        full_key2,
        full_value2,
        full_out,
        full_up,
        full_down,
    ) = forward_weights
    seq_rows = tokens.shape[0]
    length = doc_lengths[0]
    positions = jnp.arange(seq_rows, dtype=jnp.int32)
    padding = positions >= length
    allowed_one = (jnp.abs(positions[:, None] - positions[None, :]) <= WIN) & (
        padding[:, None] == padding[None, :]
    )
    pooled_at = positions[: seq_rows // STRIDE] * STRIDE
    allowed_two = (jnp.abs(positions[:, None] - pooled_at[None, :]) <= PWIN // 2) & (
        padding[:, None] == (pooled_at >= length)[None, :]
    )
    score_scale = 1.0 / math.sqrt(HD)
    query = matmul(tokens, full_query).astype(jnp.bfloat16)
    keys = matmul(tokens, full_key).astype(jnp.bfloat16)
    values = matmul(tokens, full_value).astype(jnp.bfloat16)
    key_two = matmul(tokens, full_key2)
    value_two = matmul(tokens, full_value2)
    key_pool_f, pool_key_back = jax.vjp(pool_rows, key_two, pool_kernels[0])
    value_pool_f, pool_value_back = jax.vjp(pool_rows, value_two, pool_kernels[1])
    key_pool = key_pool_f.astype(jnp.bfloat16)
    value_pool = value_pool_f.astype(jnp.bfloat16)
    first_f, log_one = level_forward(query, keys, values, allowed_one, score_scale)
    first = first_f.astype(jnp.bfloat16)
    query_two = matmul(first, full_query2).astype(jnp.bfloat16)
    second, log_two = level_forward(query_two, key_pool, value_pool, allowed_two, score_scale)
    mixed = (first.astype(jnp.float32) + second).astype(jnp.bfloat16)
    branch = matmul(mixed, full_out)
    hidden, norm_one_back = jax.vjp(
        layer_norm, tokens.astype(jnp.float32) + branch, norm_gains[0], norm_shifts[0]
    )
    hidden_low = hidden.astype(jnp.bfloat16)
    upper = matmul(hidden_low, full_up)
    activated_f, gelu_back = jax.vjp(gelu_tanh, upper)
    activated = activated_f.astype(jnp.bfloat16)
    resid_two = hidden + matmul(activated, full_down)
    result, norm_two_back = jax.vjp(layer_norm, resid_two, norm_gains[1], norm_shifts[1])
    activations = result.astype(jnp.bfloat16)
    back_weights = gather_second(shards)
    (
        back_query,
        back_key,
        back_value,
        back_query2,
        back_key2,
        back_value2,
        back_out,
        back_up,
        back_down,
    ) = back_weights
    d_resid_two, d_gain_two, d_shift_two = norm_two_back(out_grad.astype(jnp.float32))
    d_ffn = d_resid_two.astype(jnp.bfloat16)
    grad_down = inner_rows(activated, d_ffn)
    d_upper = gelu_back(outer_cols(d_ffn, back_down))[0].astype(jnp.bfloat16)
    grad_up = inner_rows(hidden_low, d_upper)
    d_hidden = d_resid_two + outer_cols(d_upper, back_up)
    d_resid_one, d_gain_one, d_shift_one = norm_one_back(d_hidden)
    d_branch = d_resid_one.astype(jnp.bfloat16)
    grad_out = inner_rows(mixed, d_branch)
    d_mixed = outer_cols(d_branch, back_out)
    d_query_two_f, d_key_pool_f, d_value_pool_f = level_backward(
        query_two,
        key_pool,
        value_pool,
        allowed_two,
        score_scale,
        log_two,
        d_mixed.astype(jnp.bfloat16),
    )
    d_query_two = d_query_two_f.astype(jnp.bfloat16)
    d_key_pool = d_key_pool_f.astype(jnp.bfloat16)
    d_value_pool = d_value_pool_f.astype(jnp.bfloat16)
    grad_query2 = inner_rows(first, d_query_two)
    d_first = (d_mixed + outer_cols(d_query_two, back_query2)).astype(jnp.bfloat16)
    d_query_f, d_keys_f, d_values_f = level_backward(
        query, keys, values, allowed_one, score_scale, log_one, d_first
    )
    d_query = d_query_f.astype(jnp.bfloat16)
    d_keys = d_keys_f.astype(jnp.bfloat16)
    d_values = d_values_f.astype(jnp.bfloat16)
    d_key_two_f, d_pool_key = pool_key_back(d_key_pool.astype(jnp.float32))
    d_value_two_f, d_pool_value = pool_value_back(d_value_pool.astype(jnp.float32))
    d_key_two = d_key_two_f.astype(jnp.bfloat16)
    d_value_two = d_value_two_f.astype(jnp.bfloat16)
    grad_query = inner_rows(tokens, d_query)
    grad_key = inner_rows(tokens, d_keys)
    grad_value = inner_rows(tokens, d_values)
    grad_key2 = inner_rows(tokens, d_key_two)
    grad_value2 = inner_rows(tokens, d_value_two)
    d_tokens = (
        d_resid_one
        + outer_cols(d_query, back_query)
        + outer_cols(d_keys, back_key)
        + outer_cols(d_values, back_value)
    )
    d_tokens = d_tokens + outer_cols(d_key_two, back_key2) + outer_cols(d_value_two, back_value2)
    grads_all = (
        grad_query,
        grad_key,
        grad_value,
        grad_query2,
        grad_key2,
        grad_value2,
        grad_out,
        grad_up,
        grad_down,
    )
    owned = reduce_columns_first(grads_all)
    gain_stack = jnp.stack([d_gain_one, d_gain_two])
    shift_stack = jnp.stack([d_shift_one, d_shift_two])
    pool_stack = jnp.stack([d_pool_key, d_pool_value])
    vector_sums = lax.psum((gain_stack, shift_stack, pool_stack), ("dp", "fsdp"))
    return (
        activations,
        d_tokens.astype(jnp.bfloat16),
        owned[0],
        owned[1],
        owned[2],
        owned[3],
        owned[4],
        owned[5],
        owned[6],
        owned[7],
        owned[8],
        vector_sums[0],
        vector_sums[1],
        vector_sums[2],
    )


def solution(mesh):
    fits = mesh.shape["dp"] == 4 and mesh.shape["fsdp"] == 8
    return jax.shard_map(
        local_kernels if fits else local,
        mesh=mesh,
        in_specs=(
            P(("dp", "fsdp"), None),
            P(("dp", "fsdp")),
            P("dp", "fsdp"),
            P("dp", "fsdp"),
            P("dp", "fsdp"),
            P("dp", "fsdp"),
            P("dp", "fsdp"),
            P("dp", "fsdp"),
            P("dp", "fsdp"),
            P("dp", "fsdp"),
            P("dp", "fsdp"),
            P(),
            P(),
            P(),
            P(("dp", "fsdp"), None),
        ),
        out_specs=(
            P(("dp", "fsdp"), None),
            P(("dp", "fsdp"), None),
            P("dp", "fsdp"),
            P("dp", "fsdp"),
            P("dp", "fsdp"),
            P("dp", "fsdp"),
            P("dp", "fsdp"),
            P("dp", "fsdp"),
            P("dp", "fsdp"),
            P("dp", "fsdp"),
            P("dp", "fsdp"),
            P(),
            P(),
            P(),
        ),
        check_vma=False,
    )
```

```python
import math

import jax
import jax.numpy as jnp
from jax import lax
from jax.experimental import pallas as pl
from jax.experimental.pallas import tpu as pltpu
from jax.sharding import PartitionSpec as P

HEADS = 12
HD = 64
WIN = 128
PWIN = 512
STRIDE = 4


def matmul(left_mat, right_mat):
    return jnp.dot(left_mat, right_mat, preferred_element_type=jnp.float32)


def inner_rows(left_mat, right_mat):
    return lax.dot_general(
        left_mat, right_mat, (((0,), (0,)), ((), ())), preferred_element_type=jnp.float32
    )


def outer_cols(left_mat, right_mat):
    return lax.dot_general(
        left_mat, right_mat, (((1,), (1,)), ((), ())), preferred_element_type=jnp.float32
    )


def layer_norm(inputs, norm_gain, norm_shift):
    average = jnp.mean(inputs, axis=-1, keepdims=True)
    centred = inputs - average
    variance = jnp.mean(centred * centred, axis=-1, keepdims=True)
    return centred * lax.rsqrt(variance + 1e-05) * norm_gain + norm_shift


def gelu_tanh(inputs):
    return jax.nn.gelu(inputs, approximate=True)


def pool_rows(inputs, kernel):
    side_rows = (kernel.shape[0] - 1) // 2
    pooled_rows = inputs.shape[0] // STRIDE
    padded = jnp.pad(inputs, ((side_rows, side_rows), (0, 0)))
    summed = jnp.zeros((pooled_rows, inputs.shape[1]), jnp.float32)
    for offset in range(kernel.shape[0]):
        summed = summed + kernel[offset] * padded[offset : offset + inputs.shape[0] : STRIDE]
    return summed


def split_heads(matrix):
    return matrix.reshape(matrix.shape[0], HEADS // 2, 2, HD).transpose(1, 0, 2, 3)


def join_heads(groups):
    return groups.transpose(1, 0, 2, 3).reshape(groups.shape[1], HEADS * HD)


def masked_scores(query, keys, allowed, score_scale):
    raw_scores = (
        jnp.einsum("ihd,jhd->hij", query, keys, preferred_element_type=jnp.float32) * score_scale
    )
    return jnp.where(allowed[None], raw_scores, -1e30)


def attend_forward(query, keys, values, allowed, score_scale):
    scores = masked_scores(query, keys, allowed, score_scale)
    highest = jnp.max(scores, axis=-1, keepdims=True)
    expo_terms = jnp.exp(scores - highest)
    summed = jnp.sum(expo_terms, axis=-1, keepdims=True)
    soft_weights = (expo_terms / summed).astype(jnp.bfloat16)
    result = jnp.einsum("hij,jhd->ihd", soft_weights, values, preferred_element_type=jnp.float32)
    return (result, (highest + jnp.log(summed))[..., 0])


def attend_backward(query, keys, values, allowed, score_scale, log_total, grad_result):
    scores = masked_scores(query, keys, allowed, score_scale)
    soft_weights = jnp.exp(scores - log_total[..., None])
    grad_soft = jnp.einsum("ihd,jhd->hij", grad_result, values, preferred_element_type=jnp.float32)
    grad_values = jnp.einsum(
        "hij,ihd->jhd",
        soft_weights.astype(jnp.bfloat16),
        grad_result,
        preferred_element_type=jnp.float32,
    )
    row_terms = jnp.sum(soft_weights * grad_soft, axis=-1, keepdims=True)
    grad_scores = (soft_weights * (grad_soft - row_terms)).astype(jnp.bfloat16)
    grad_query = (
        jnp.einsum("hij,jhd->ihd", grad_scores, keys, preferred_element_type=jnp.float32)
        * score_scale
    )
    grad_keys = (
        jnp.einsum("hij,ihd->jhd", grad_scores, query, preferred_element_type=jnp.float32)
        * score_scale
    )
    return (grad_query, grad_keys, grad_values)


def level_forward(query, keys, values, allowed, score_scale):

    def one_group(group_parts):
        return attend_forward(group_parts[0], group_parts[1], group_parts[2], allowed, score_scale)

    results, log_totals = lax.map(
        one_group, (split_heads(query), split_heads(keys), split_heads(values))
    )
    return (join_heads(results), log_totals)


def level_backward(query, keys, values, allowed, score_scale, log_totals, grad_result):

    def one_group(group_parts):
        return attend_backward(
            group_parts[0],
            group_parts[1],
            group_parts[2],
            allowed,
            score_scale,
            group_parts[3],
            group_parts[4],
        )

    grad_query, grad_keys, grad_values = lax.map(
        one_group,
        (
            split_heads(query),
            split_heads(keys),
            split_heads(values),
            log_totals,
            split_heads(grad_result),
        ),
    )
    return (join_heads(grad_query), join_heads(grad_keys), join_heads(grad_values))


def gather_first(shards):
    column_parts = (
        lax.all_gather(shards[0], "fsdp", axis=1, tiled=True),
        lax.all_gather(shards[1], "fsdp", axis=1, tiled=True),
        lax.all_gather(shards[2], "fsdp", axis=1, tiled=True),
        lax.all_gather(shards[3], "fsdp", axis=1, tiled=True),
        lax.all_gather(shards[4], "fsdp", axis=1, tiled=True),
        lax.all_gather(shards[5], "fsdp", axis=1, tiled=True),
        lax.all_gather(shards[6], "fsdp", axis=1, tiled=True),
        lax.all_gather(shards[7], "fsdp", axis=1, tiled=True),
        lax.all_gather(shards[8], "fsdp", axis=1, tiled=True),
    )
    return (
        lax.all_gather(column_parts[0], "dp", axis=0, tiled=True),
        lax.all_gather(column_parts[1], "dp", axis=0, tiled=True),
        lax.all_gather(column_parts[2], "dp", axis=0, tiled=True),
        lax.all_gather(column_parts[3], "dp", axis=0, tiled=True),
        lax.all_gather(column_parts[4], "dp", axis=0, tiled=True),
        lax.all_gather(column_parts[5], "dp", axis=0, tiled=True),
        lax.all_gather(column_parts[6], "dp", axis=0, tiled=True),
        lax.all_gather(column_parts[7], "dp", axis=0, tiled=True),
        lax.all_gather(column_parts[8], "dp", axis=0, tiled=True),
    )


def gather_second(shards):
    column_parts = (
        lax.all_gather(shards[0], "fsdp", axis=1, tiled=True),
        lax.all_gather(shards[1], "fsdp", axis=1, tiled=True),
        lax.all_gather(shards[2], "fsdp", axis=1, tiled=True),
        lax.all_gather(shards[3], "fsdp", axis=1, tiled=True),
        lax.all_gather(shards[4], "fsdp", axis=1, tiled=True),
        lax.all_gather(shards[5], "fsdp", axis=1, tiled=True),
        lax.all_gather(shards[6], "fsdp", axis=1, tiled=True),
        lax.all_gather(shards[7], "fsdp", axis=1, tiled=True),
        lax.all_gather(shards[8], "fsdp", axis=1, tiled=True),
    )
    return (
        lax.all_gather(column_parts[0], "dp", axis=0, tiled=True),
        lax.all_gather(column_parts[1], "dp", axis=0, tiled=True),
        lax.all_gather(column_parts[2], "dp", axis=0, tiled=True),
        lax.all_gather(column_parts[3], "dp", axis=0, tiled=True),
        lax.all_gather(column_parts[4], "dp", axis=0, tiled=True),
        lax.all_gather(column_parts[5], "dp", axis=0, tiled=True),
        lax.all_gather(column_parts[6], "dp", axis=0, tiled=True),
        lax.all_gather(column_parts[7], "dp", axis=0, tiled=True),
        lax.all_gather(column_parts[8], "dp", axis=0, tiled=True),
    )


def reduce_columns_first(grads_all):
    column_sums = (
        lax.psum_scatter(
            grads_all[0].astype(jnp.bfloat16), "fsdp", scatter_dimension=1, tiled=True
        ).astype(jnp.float32),
        lax.psum_scatter(
            grads_all[1].astype(jnp.bfloat16), "fsdp", scatter_dimension=1, tiled=True
        ).astype(jnp.float32),
        lax.psum_scatter(
            grads_all[2].astype(jnp.bfloat16), "fsdp", scatter_dimension=1, tiled=True
        ).astype(jnp.float32),
        lax.psum_scatter(
            grads_all[3].astype(jnp.bfloat16), "fsdp", scatter_dimension=1, tiled=True
        ).astype(jnp.float32),
        lax.psum_scatter(
            grads_all[4].astype(jnp.bfloat16), "fsdp", scatter_dimension=1, tiled=True
        ).astype(jnp.float32),
        lax.psum_scatter(
            grads_all[5].astype(jnp.bfloat16), "fsdp", scatter_dimension=1, tiled=True
        ).astype(jnp.float32),
        lax.psum_scatter(
            grads_all[6].astype(jnp.bfloat16), "fsdp", scatter_dimension=1, tiled=True
        ).astype(jnp.float32),
        lax.psum_scatter(
            grads_all[7].astype(jnp.bfloat16), "fsdp", scatter_dimension=1, tiled=True
        ).astype(jnp.float32),
        lax.psum_scatter(
            grads_all[8].astype(jnp.bfloat16), "fsdp", scatter_dimension=1, tiled=True
        ).astype(jnp.float32),
    )
    return (
        lax.psum_scatter(
            column_sums[0].astype(jnp.bfloat16), "dp", scatter_dimension=0, tiled=True
        ).astype(jnp.float32),
        lax.psum_scatter(
            column_sums[1].astype(jnp.bfloat16), "dp", scatter_dimension=0, tiled=True
        ).astype(jnp.float32),
        lax.psum_scatter(
            column_sums[2].astype(jnp.bfloat16), "dp", scatter_dimension=0, tiled=True
        ).astype(jnp.float32),
        lax.psum_scatter(
            column_sums[3].astype(jnp.bfloat16), "dp", scatter_dimension=0, tiled=True
        ).astype(jnp.float32),
        lax.psum_scatter(
            column_sums[4].astype(jnp.bfloat16), "dp", scatter_dimension=0, tiled=True
        ).astype(jnp.float32),
        lax.psum_scatter(
            column_sums[5].astype(jnp.bfloat16), "dp", scatter_dimension=0, tiled=True
        ).astype(jnp.float32),
        lax.psum_scatter(
            column_sums[6].astype(jnp.bfloat16), "dp", scatter_dimension=0, tiled=True
        ).astype(jnp.float32),
        lax.psum_scatter(
            column_sums[7].astype(jnp.bfloat16), "dp", scatter_dimension=0, tiled=True
        ).astype(jnp.float32),
        lax.psum_scatter(
            column_sums[8].astype(jnp.bfloat16), "dp", scatter_dimension=0, tiled=True
        ).astype(jnp.float32),
    )


MESH = pl.DeviceIdType.MESH
BF = jnp.bfloat16
F32 = jnp.float32

GROUPS = (
    ("s", 0, 1),
    ("s", 1, 2),
    ("s", 3, 5),
    ("s", 5, 7),
    ("u", 0, 96),
    ("u", 96, 192),
    ("d", 0, 256),
    ("d", 256, 512),
    ("d", 512, 768),
    ("s", 2, 3),
)
SQUARES = (0, 1, 2, 3, 9)
PLANE = 8
N_GROUPS = len(GROUPS)
SQ = (7, 4, 2, 2, 48, 768)
UP = (2, 2, 4, 2, 192, 384)
DOWN = (4, 2, 2, 2, 96, 768)


class Place:
    def __init__(self):
        dp = lax.axis_index("dp")
        fs = lax.axis_index("fsdp")
        self.y = lax.div(dp, 2)
        self.c = lax.rem(dp, 2)
        self.z = lax.div(fs, 2)
        self.x = lax.rem(fs, 2)
        c, x, y = self.c, self.x, self.y
        self.p1 = ((1 - c) * (1 - x) + c * x, (1 - c) * y + c * (1 - y))
        self.p2 = ((1 - c) * x + c * (1 - x), (1 - c) * (1 - y) + c * y)
        self.own = (x, y)
        self.diag = (1 - x, 1 - y)

    def dev(self, xy, z=None, c=None):
        z = self.z if z is None else z
        c = self.c if c is None else c
        return (xy[1] * 2 + c, z * 2 + xy[0])

    def sibling(self):
        return self.dev(self.own, c=1 - self.c)

    def peer(self, k):
        return lax.rem(self.z + k, 4)

    def everyone(self):
        return [self.sibling(), self.dev(self.p1), self.dev(self.p2), self.dev(self.diag)] + [
            self.dev(self.own, z=self.peer(k)) for k in (1, 2, 3)
        ]


def greet(me):
    bar = pltpu.get_barrier_semaphore()
    for d in me.everyone():
        pl.semaphore_signal(bar, inc=1, device_id=d, device_id_type=MESH)
    pl.semaphore_wait(bar, 7)


def square_lanes(y):
    return pl.ds(pl.multiple_of(y * 384, 128), 384)


def blocks(refs, g, xy, c, z=slice(None)):
    sq, up, down = refs
    x, y = xy
    kind, lo, hi = GROUPS[g]
    if kind == "s":
        return sq.at[lo:hi, z, x, c, :, square_lanes(y)]
    if kind == "u":
        return up.at[y, c, z, x, lo:hi]
    return down.at[z, x, y, c, :, lo:hi]


def half(refs, g, c):
    sq, up, down = refs
    kind, lo, hi = GROUPS[g]
    if kind == "s":
        return sq.at[lo:hi, :, :, c]
    if kind == "u":
        return up.at[:, c, :, :, lo:hi]
    return down.at[:, :, :, c, :, lo:hi]


def plane(down, g, c, z):
    _, lo, hi = GROUPS[g]
    return down.at[z, :, :, c, :, lo:hi]


def rcopy(src, dst, ssem, rsem, dev):
    return pltpu.make_async_remote_copy(
        src_ref=src, dst_ref=dst, send_sem=ssem, recv_sem=rsem, device_id=dev, device_id_type=MESH
    )


class Gather:
    def __init__(self, me, refs, ssem, rsem):
        self.me, self.refs, self.ssem, self.rsem = me, refs, ssem, rsem

    def copy(self, g, i, incoming=False):
        me = self.me
        together = min(i, 6) if i < 10 else (i - 10) // 3
        first = 0 if i in (3, 4, 5) and g != PLANE else together
        ss = self.ssem.at[g, i - 7 if i in (10, 11, 12) else first]
        rs = self.rsem.at[g, i - 3 if i in (10, 11, 12) else together]
        side = 1 if incoming else 0
        c = me.c
        ways = ((me.own, me.p1), (me.own, me.p2), (me.p1, me.diag))
        if i < 3:
            b = blocks(self.refs, g, ways[i][side], c, me.z)
            return rcopy(b, b, ss, rs, me.dev(me.p1 if i == 0 else me.p2))
        if i < 6:
            k = i - 2
            z = lax.rem(me.z + 4 - k, 4) if incoming else me.z
            b = plane(self.refs[2], g, c, z) if g == PLANE else blocks(self.refs, g, me.own, c, z)
            return rcopy(b, b, ss, rs, me.dev(me.own, z=me.peer(k)))
        if i < 10:
            cc = 1 - c if incoming else c
            what = ((me.own, me.own), (me.p1, me.p2), (me.p2, me.p1), (me.diag, me.diag))[i - 6][side]
            if g == PLANE:
                b = plane(self.refs[2], g, cc, lax.rem(me.z + 4 - (i - 6), 4))
            else:
                b = blocks(self.refs, g, what, cc)
            return rcopy(b, b, ss, rs, me.sibling())
        way, k = (i - 10) // 3, (i - 10) % 3 + 1
        b = blocks(self.refs, g, ways[way][side], c, lax.rem(me.z + 4 - k, 4))
        return rcopy(b, b, ss, rs, me.dev(me.p1 if way == 0 else me.p2))

    def go(self, g, *which):
        for i in which:
            self.copy(g, i).start()

    def got(self, g, *which):
        for i in which:
            self.copy(g, i, True).wait_recv()

    def whole(self, g, at, ref):
        return rcopy(ref, ref, self.ssem.at[g, at], self.rsem.at[g, at], self.me.sibling())

    def start(self, g):
        self.go(g, *((0, 1) if g == PLANE else (0, 1, 3, 4, 5)))

    def step0(self, g):
        self.got(g, 0)
        self.go(g, 2)

    def step1(self, g):
        if g == PLANE:
            self.got(g, 1, 2)
            self.go(g, 3, 4, 5, 6)
            return
        for k in range(3):
            self.got(g, 3 + k)
            self.go(g, 13 + k, 10 + k)
        self.go(g, 6)

    def step2(self, g):
        for k in range(3):
            self.got(g, 10 + k)
            self.go(g, 16 + k)
        self.go(g, 7)

    def step3(self, g):
        self.whole(g, 1, blocks(self.refs, g, self.me.p2, self.me.c)).wait_recv()
        self.go(g, 8)

    def step4(self, g):
        if g == PLANE:
            for i in (3, 4, 5):
                self.got(g, i)
                self.go(g, i + 4)
            return
        self.whole(g, 2, blocks(self.refs, g, self.me.diag, self.me.c)).wait_recv()
        self.go(g, 9)

    def arrived(self, g):
        self.whole(g, 6, half(self.refs, g, 1 - self.me.c)).wait_recv()

    def sent(self, g):
        me = self.me
        if g == PLANE:
            for i in range(6):
                self.copy(g, i).wait_send()
        else:
            for at in range(3):
                self.whole(g, at, blocks(self.refs, g, me.own, me.c)).wait_send()
            for i in (10, 11, 12):
                self.copy(g, i).wait_send()
        self.whole(g, 6, half(self.refs, g, me.c)).wait_send()


class Scatter:
    def __init__(self, me, refs, sib, r1, r2, r3, rp, ssem, rsem):
        self.me, self.refs, self.sib = me, refs, sib
        self.r1, self.r2, self.r3 = r1, r2, r3
        self.pz, self.p2, self.p1 = rp
        self.ssem, self.rsem = ssem, rsem

    def sib_view(self, g, xy, z=slice(None)):
        sq, up, down = self.sib
        x, y = xy
        kind, lo, hi = GROUPS[g]
        if kind == "s":
            return sq.at[lo:hi, z, x, :, square_lanes(y)]
        if kind == "u":
            return up.at[y, z, x, lo:hi]
        return down.at[z, x, y, :, lo:hi]

    def plane_of(self, g, c, z):
        return plane(self.refs[2], g, c, z)

    def sib_plane(self, g, z):
        _, lo, hi = GROUPS[g]
        return self.sib[2].at[z, :, :, :, lo:hi]

    def slot(self, bufs, g, i):
        kind, lo, hi = GROUPS[g]
        if kind == "s":
            return bufs[0].at[i, lo:hi]
        buf = bufs[1 if kind == "u" else 2]
        if kind == "d":
            return buf.at[i, :, :, lo:hi] if len(buf.shape) == 4 else buf.at[i, :, lo:hi]
        return buf.at[i, :, lo:hi] if len(buf.shape) == 4 else buf.at[i, lo:hi]

    def copy(self, g, i):
        me = self.me
        c = me.c
        ss, rs = self.ssem.at[g, max(i - 3, 0)], self.rsem.at[g, i]
        if g == PLANE:
            if i < 4:
                z = me.peer(i + 1)
                return rcopy(self.plane_of(g, 1 - c, z), self.sib_plane(g, z), ss, rs, me.sibling())
            if i < 7:
                k = i - 3
                src = self.plane_of(g, c, me.peer(k))
                return rcopy(src, self.pz.at[k - 1], ss, rs, me.dev(me.own, z=me.peer(k)))
            if i < 9:
                src = blocks(self.refs, g, (me.diag, me.p2)[i - 7], c, me.z)
                return rcopy(src, self.p2.at[i - 7], ss, rs, me.dev(me.p2))
            return rcopy(blocks(self.refs, g, me.p1, c, me.z), self.p1, ss, rs, me.dev(me.p1))
        if i < 4:
            what = (me.p1, me.diag, me.p2, me.own)[i]
            return rcopy(blocks(self.refs, g, what, 1 - c), self.sib_view(g, what), ss, rs, me.sibling())
        if i < 6:
            src = blocks(self.refs, g, (me.diag, me.p2)[i - 4], c)
            return rcopy(src, self.slot(self.r1, g, i - 4), ss, rs, me.dev(me.p2))
        if i == 6:
            return rcopy(blocks(self.refs, g, me.p1, c), self.slot(self.r2, g, 0), ss, rs, me.dev(me.p1))
        k = i - 6
        src = blocks(self.refs, g, me.own, c, me.peer(k))
        return rcopy(src, self.slot(self.r3, g, k - 1), ss, rs, me.dev(me.own, z=me.peer(k)))

    def go(self, g, *which):
        for i in which:
            self.copy(g, i).start()

    def got(self, g, i):
        self.copy(g, i).wait_recv()

    def add(self, here, *others):
        total = here[...].astype(F32)
        for other in others:
            total = total + other[...].astype(F32)
        here[...] = total.astype(BF)

    def start(self, g):
        self.go(g, 0, 1, 2, 3)

    def step1(self, g):
        me = self.me
        if g == PLANE:
            for k in (1, 2, 3):
                z = me.peer(k)
                self.got(g, k - 1)
                self.add(self.plane_of(g, me.c, z), self.sib_plane(g, z))
                self.go(g, 3 + k)
            return
        for i, what, out in ((1, me.diag, 4), (0, me.p2, 5)):
            self.got(g, i)
            self.add(blocks(self.refs, g, what, me.c), self.sib_view(g, what))
            self.go(g, out)

    def step2(self, g):
        me = self.me
        if g == PLANE:
            for i in (3, 4, 5, 6):
                self.got(g, i)
            here = self.plane_of(g, me.c, me.z)
            self.add(here, self.sib_plane(g, me.z), *[self.pz.at[k] for k in range(3)])
            self.go(g, 7, 8)
            return
        self.got(g, 2)
        self.got(g, 4)
        here = blocks(self.refs, g, me.p1, me.c)
        self.add(here, self.sib_view(g, me.p1), self.slot(self.r1, g, 0))
        self.go(g, 6)

    def step3(self, g):
        me = self.me
        if g == PLANE:
            self.got(g, 7)
            self.add(blocks(self.refs, g, me.p1, me.c, me.z), self.p2.at[0])
            self.go(g, 9)
            return
        self.got(g, 3)
        self.got(g, 5)
        self.got(g, 6)
        here = blocks(self.refs, g, me.own, me.c)
        self.add(here, self.sib_view(g, me.own), self.slot(self.r1, g, 1), self.slot(self.r2, g, 0))
        self.go(g, 7, 8, 9)

    def finish(self, g):
        me = self.me
        total = blocks(self.refs, g, me.own, me.c, me.z)[...].astype(F32)
        if g == PLANE:
            self.got(g, 8)
            self.got(g, 9)
            return total + self.p2[1].astype(F32) + self.p1[...].astype(F32)
        for k in (1, 2, 3):
            self.got(g, 6 + k)
            total = total + self.slot(self.r3, g, k - 1)[...].astype(F32)
        return total

    def sent(self, g):
        away = half(self.refs, g, 1 - self.me.c)
        rcopy(away, away, self.ssem.at[g, 0], self.rsem.at[g, 0], self.me.sibling()).wait_send()
        for i in range(4, 10):
            self.copy(g, i).wait_send()


class VectorSum:
    def __init__(self, me, vec, buf, ssem, rsem):
        self.me, self.vec, self.buf, self.ssem, self.rsem = me, vec, buf, ssem, rsem

    def copy(self, i, incoming=False):
        me = self.me
        if i < 3:
            z = lax.rem(me.z + 3 - i, 4) if incoming else me.z
            b, d = self.buf.at[z], me.dev(me.own, z=me.peer(i + 1))
        elif i == 3:
            return rcopy(self.buf.at[4], self.buf.at[5], self.ssem.at[i], self.rsem.at[i], me.sibling())
        else:
            x, y = ((1 - me.x, me.y), (me.x, 1 - me.y), me.diag)[i - 4]
            fx, fy = (x, y) if incoming else me.own
            b, d = self.buf.at[6 + fx + 2 * fy], me.dev((x, y))
        return rcopy(b, b, self.ssem.at[i], self.rsem.at[i], d)

    def send(self, first, last):
        for i in range(first, last):
            self.copy(i).start()

    def got(self, first, last):
        for i in range(first, last):
            self.copy(i, True).wait_recv()

    def send_z(self):
        self.buf[self.me.z] = self.vec[...]
        self.send(0, 3)

    def send_core(self):
        self.got(0, 3)
        b = self.buf
        b[4] = (b[0] + b[1]) + (b[2] + b[3])
        self.send(3, 4)

    def send_beside(self):
        self.got(3, 4)
        b = self.buf
        b[6 + self.me.x + 2 * self.me.y] = b[4] + b[5]
        self.send(4, 7)

    def take(self):
        self.got(4, 7)
        b = self.buf
        self.vec[...] = (b[6] + b[7]) + (b[8] + b[9])
        for i in range(7):
            self.copy(i).wait_send()


def place_squares(me, shards, sq, room, ssem, rsem):
    rows = lax.broadcasted_iota(jnp.int32, (192, 384), 0)
    lanes = lax.broadcasted_iota(jnp.int32, (192, 384), 1)
    spot = jnp.where(lanes == rows + me.c * 192, 1.0, 0.0).astype(BF)
    for m in range(7):
        t = dg(shards[m][...], spot, 0, 0).astype(BF)
        for half in range(2):
            room[half, 48 * m : 48 * m + 48, 0:384] = t[48 * half : 48 * half + 48]
    area = (pl.ds(0, 336), pl.ds(0, 384))
    swap = rcopy(room.at[(1 - me.c, *area)], room.at[(2, *area)], ssem, rsem, me.sibling())
    swap.start()
    swap.wait()
    for m in range(7):
        rows = slice(48 * m, 48 * m + 48)
        both = room[me.c, rows, 0:384].astype(F32) + room[2, rows, 0:384].astype(F32)
        sq[m, me.z, me.x, me.c, :, square_lanes(me.y)] = both.astype(BF)


GAIN, SHIFT, POOL = 0, 2, 4


def dg(a, b, ca, cb):
    return lax.dot_general(a, b, (((ca,), (cb,)), ((), ())), preferred_element_type=F32)


def weight(r, m):
    return r.sq[m].reshape(768, 768)


def weight_up(r, j):
    left = r.up[:, :, j, 0].reshape(768, 384)
    right = r.up[:, :, j, 1].reshape(768, 384)
    return jnp.concatenate([left, right], axis=1)


def weight_down(r, y, c, lo, hi):
    return r.down[:, :, y, c, :, lo:hi].reshape(768, hi - lo)


def set_masks(r, length):
    for i in range(2):
        row = lax.broadcasted_iota(jnp.int32, (256, 384), 0) + 256 * i
        col = lax.broadcasted_iota(jnp.int32, (256, 384), 1) + 128 * i
        ok = (jnp.abs(row - col) <= WIN) & ((row >= length) == (col >= length))
        r.bias1[i] = jnp.where(ok, 0.0, -1e30)
    row = lax.broadcasted_iota(jnp.int32, (512, 128), 0)
    col = lax.broadcasted_iota(jnp.int32, (512, 128), 1) * STRIDE
    ok = (jnp.abs(row - col) <= PWIN // 2) & ((row >= length) == (col >= length))
    r.bias2[...] = jnp.where(ok, 0.0, -1e30)


def low_lanes(rows):
    return lax.broadcasted_iota(jnp.int32, (rows, 128), 1) < HD


def two_heads(pair):
    low = low_lanes(pair.shape[0])
    zero = jnp.zeros_like(pair)
    return jnp.concatenate([jnp.where(low, pair, zero), jnp.where(low, zero, pair)], axis=0)


def side_by_side(stacked):
    n = stacked.shape[0] // 2
    return jnp.where(low_lanes(n), stacked[:n], stacked[n:])


def pair_lanes(p):
    return pl.ds(pl.multiple_of(p * 128, 128), 128)


def softmax_out(scores, bias, values, lse_ref, p):
    scores = scores + jnp.concatenate([bias, bias], axis=0)
    highest = jnp.max(scores, axis=-1, keepdims=True)
    terms = jnp.exp(scores - highest)
    summed = jnp.sum(terms, axis=-1, keepdims=True)
    probs = (terms * (1.0 / summed)).astype(BF)
    lane = lax.broadcasted_iota(jnp.int32, lse_ref.shape, 1)
    lse_ref[...] = jnp.where(lane == p, highest + jnp.log(summed), lse_ref[...])
    return side_by_side(dg(probs, values, 1, 0))


def scores_of(query, keys):
    scaled = two_heads(query * jnp.asarray(0.125, BF))
    return scaled, dg(scaled, keys, 1, 1)


def softmax_back(scores, bias, lse_ref, p, grad, values):
    scores = scores + jnp.concatenate([bias, bias], axis=0)
    lane = lax.broadcasted_iota(jnp.int32, lse_ref.shape, 1)
    lse = jnp.sum(jnp.where(lane == p, lse_ref[...], 0.0), axis=-1, keepdims=True)
    probs = jnp.exp(scores - lse)
    grad_probs = dg(grad, values, 1, 1)
    row_terms = jnp.sum(probs * grad_probs, axis=-1, keepdims=True)
    return probs.astype(BF), (probs * (grad_probs - row_terms)).astype(BF)


def project(r, lo, hi):
    @pl.loop(lo, hi)
    def _(m):
        r.qkv[m] = dg(r.tokens[...], weight(r, m), 1, 1).astype(BF)


def project_pool(r, i):
    full = None
    for l in range(6):
        lanes = slice(l * 128, l * 128 + 128)
        if l % 3 == 0:
            full = dg(r.tokens[...], r.sq[3 + i, 2 * (l // 3) : 2 * (l // 3) + 2].reshape(384, 768), 1, 1)
        r.kt[i, l, 0:8] = jnp.zeros((8, 128), F32)
        r.kt[i, l, 520:528] = jnp.zeros((8, 128), F32)
        r.kt[i, l, 8:520] = full[:, (l % 3) * 128 : (l % 3) * 128 + 128]
        total = None
        for t in range(5):
            term = r.pool[t, i : i + 1, lanes] * r.kt[i, l, pl.ds(6 + t, 128, stride=STRIDE), :]
            total = term if total is None else total + term
        r.kp[i, :, lanes] = total.astype(BF)


def at_steps(p, hooks):
    for at, hook in (hooks or {}).items():
        pl.when(p == at)(hook)


def level_one(r, hooks=None):
    @pl.loop(0, HEADS // 2)
    def _(p):
        at_steps(p, hooks)
        lanes = pair_lanes(p)
        for i in range(2):
            rows, cols = pl.ds(256 * i, 256), pl.ds(128 * i, 384)
            _, scores = scores_of(r.qkv[0, rows, lanes], r.qkv[1, cols, lanes])
            out = softmax_out(scores, r.bias1[i], r.qkv[2, cols, lanes], r.lse.at[pl.ds(512 * i, 512)], p)
            r.first[rows, lanes] = out.astype(BF)


def level_two(r, hooks=None):
    r.q2[...] = dg(r.first[...], weight(r, 5), 1, 1).astype(BF)

    @pl.loop(0, HEADS // 2)
    def _(p):
        at_steps(p, hooks)
        lanes = pair_lanes(p)
        _, scores = scores_of(r.q2[:, lanes], r.kp[0, :, lanes])
        out = softmax_out(scores, r.bias2[...], r.kp[1, :, lanes], r.lse, p + HEADS // 2)
        r.mixed[:, lanes] = (r.first[:, lanes].astype(F32) + out).astype(BF)


def norm_parts(x):
    average = jnp.mean(x, axis=-1, keepdims=True)
    centred = x - average
    inverse = lax.rsqrt(jnp.mean(centred * centred, axis=-1, keepdims=True) + 1e-05)
    return centred * inverse, inverse


def norm_back(n, inverse, gain, grad):
    scaled = grad * gain
    return (
        scaled - jnp.mean(scaled, axis=-1, keepdims=True) - n * jnp.mean(scaled * n, axis=-1, keepdims=True)
    ) * inverse


def first_norm(r):
    r.acc[...] = dg(r.mixed[...], weight(r, 6), 1, 1)

    @pl.loop(0, 4)
    def _(i):
        rows = pl.ds(pl.multiple_of(i * 128, 128), 128)
        n, inverse = norm_parts(r.tokens[rows].astype(F32) + r.acc[rows])
        r.n1[rows] = n
        r.inv1[rows] = inverse
        r.hlow[rows] = (n * r.gains[0:1] + r.shifts[0:1]).astype(BF)


def ffn_up(r, hooks=None):
    k = math.sqrt(2.0 / math.pi)

    @pl.loop(0, 4)
    def _(j):
        at_steps(j, hooks)
        for i in range(2):
            rows = pl.ds(256 * i, 256)
            u = dg(r.hlow[rows], weight_up(r, j), 1, 0)
            square = u * u
            half = 0.5 + 0.5 * jnp.tanh(u * (k + (k * 0.044715) * square))
            value = u * half
            r.act[j, rows] = value.astype(BF)
            slope = half + value * (1.0 - half) * (2 * k + (6 * k * 0.044715) * square)
            r.gd[j, rows] = slope.astype(BF)


def ffn_down(r, lo, hi, first):
    @pl.loop(0, 2)
    def _(i):
        rows = pl.ds(pl.multiple_of(256 * i, 256), 256)
        total = None if first else r.acc[rows]
        for j in range(4):
            term = dg(r.act[j, rows, lo:hi], weight_down(r, j // 2, j % 2, lo, hi), 1, 1)
            total = term if total is None else total + term
        r.acc[rows] = total


def second_norm(r):
    r.vec[...] = jnp.zeros_like(r.vec)

    @pl.loop(0, 4)
    def _(i):
        rows = pl.ds(pl.multiple_of(i * 128, 128), 128)
        hidden = r.n1[rows] * r.gains[0:1] + r.shifts[0:1]
        n, inverse = norm_parts(hidden + r.acc[rows])
        grad = r.og[rows].astype(F32)
        r.og[rows] = (n * r.gains[1:2] + r.shifts[1:2]).astype(BF)
        r.vec[GAIN + 1 : GAIN + 2] += jnp.sum(grad * n, axis=0, keepdims=True)
        r.vec[SHIFT + 1 : SHIFT + 2] += jnp.sum(grad, axis=0, keepdims=True)
        d = norm_back(n, inverse, r.gains[1:2], grad)
        r.dr[rows] = d
        r.dlow[rows] = d.astype(BF)


def back_down(r, c, lo, hi):
    @pl.loop(0, 2)
    def _(y):
        j = y * 2 + c
        t = dg(r.dlow[...], weight_down(r, y, c, lo, hi), 1, 0)
        r.gd[j, :, lo:hi] = (r.gd[j, :, lo:hi].astype(F32) * t).astype(BF)
        g = dg(r.dlow[...], r.act[j, :, lo:hi], 0, 0).astype(BF)
        r.down[:, :, y, c, :, lo:hi] = g.reshape(4, 2, 96, hi - lo)


def back_hidden(r):
    @pl.loop(0, 2)
    def _(i):
        rows = pl.ds(pl.multiple_of(256 * i, 256), 256)
        total = r.dr[rows]
        for j in range(4):
            total = total + dg(r.gd[j, rows], weight_up(r, j), 1, 1)
        r.acc[rows] = total


def back_first_norm(r):
    @pl.loop(0, 4)
    def _(i):
        rows = pl.ds(pl.multiple_of(i * 128, 128), 128)
        grad = r.acc[rows]
        n = r.n1[rows]
        r.vec[GAIN : GAIN + 1] += jnp.sum(grad * n, axis=0, keepdims=True)
        r.vec[SHIFT : SHIFT + 1] += jnp.sum(grad, axis=0, keepdims=True)
        d = norm_back(n, r.inv1[rows], r.gains[0:1], grad)
        r.dr[rows] = d
        r.dlow[rows] = d.astype(BF)


def grad_up(r):
    @pl.loop(0, 4)
    def _(j):
        for i in range(2):
            g = dg(r.hlow[:, 384 * i : 384 * i + 384], r.gd[j], 0, 0).astype(BF)
            for x in range(2):
                r.up[i, :, j, x] = g[:, x * 384 : (x + 1) * 384].reshape(2, 192, 384)


def set_grad(r, m, left, right):
    for i in range(2):
        g = dg(left[:, 384 * i : 384 * i + 384], right, 0, 0).astype(BF)
        r.sq[m, 2 * i : 2 * i + 2] = g.reshape(2, 2, 2, 48, 768)


def back_out(r):
    r.acc[...] = dg(r.dlow[...], weight(r, 6), 1, 0)
    set_grad(r, 6, r.dlow[...], r.mixed[...])


def back_level_two(r, hooks=None):
    @pl.loop(0, HEADS // 2)
    def _(p):
        at_steps(p, hooks)
        lanes = pair_lanes(p)
        scaled, scores = scores_of(r.q2[:, lanes], r.kp[0, :, lanes])
        grad = two_heads(r.acc[:, lanes].astype(BF))
        probs, grad_scores = softmax_back(
            scores, r.bias2[...], r.lse, p + HEADS // 2, grad, r.kp[1, :, lanes]
        )
        r.dpool[1][0:128, lanes] = dg(probs, grad, 0, 0).astype(BF).astype(F32)
        r.dpool[0][0:128, lanes] = dg(grad_scores, scaled, 0, 0).astype(BF).astype(F32)
        r.dq2[:, lanes] = (side_by_side(dg(grad_scores, r.kp[0, :, lanes], 1, 0)) * 0.125).astype(BF)

    r.dfirst[...] = (r.acc[...] + dg(r.dq2[...], weight(r, 5), 1, 0)).astype(BF)
    set_grad(r, 5, r.dq2[...], r.first[...])


def back_pool(r, i):
    r.dpool[i][128:136] = jnp.zeros((8, 768), F32)
    for l in range(6):
        lanes = slice(l * 128, l * 128 + 128)
        here = r.dpool[i][0:128, lanes]
        after = r.dpool[i][1:129, lanes]
        for t in range(5):
            term = here * r.kt[i, l, pl.ds(6 + t, 128, stride=STRIDE), :]
            at = POOL + 2 * t + i
            r.vec[at : at + 1, lanes] = jnp.sum(term, axis=0, keepdims=True)
        k = [r.pool[t, i : i + 1, lanes] for t in range(5)]
        r.kt[i, l, pl.ds(8, 128, stride=STRIDE), :] = k[2] * here
        r.kt[i, l, pl.ds(9, 128, stride=STRIDE), :] = k[3] * here
        r.kt[i, l, pl.ds(10, 128, stride=STRIDE), :] = k[4] * here + k[0] * after
        r.kt[i, l, pl.ds(11, 128, stride=STRIDE), :] = k[1] * after
    grad = jnp.concatenate([r.kt[i, l, 8:520].astype(BF) for l in range(6)], axis=1)
    finish_projection(r, 3 + i, grad)


def finish_projection(r, m, grad):
    r.dr[...] = r.dr[...] + dg(grad, weight(r, m), 1, 0)
    set_grad(r, m, grad, r.tokens[...])


def back_level_one(r, hooks=None):
    @pl.loop(0, HEADS)
    def _(step):
        at_steps(step, hooks)
        p, i = lax.div(step, 2), lax.rem(step, 2)
        lanes = pair_lanes(p)
        rows = pl.ds(pl.multiple_of(256 * i, 256), 256)
        cols = pl.ds(pl.multiple_of(128 * i, 128), 384)
        scaled, scores = scores_of(r.qkv[0, rows, lanes], r.qkv[1, cols, lanes])
        grad = two_heads(r.dfirst[rows, lanes])
        stacked = r.lse.at[pl.ds(pl.multiple_of(512 * i, 512), 512)]
        probs, grad_scores = softmax_back(scores, r.bias1[i], stacked, p, grad, r.qkv[2, cols, lanes])

        @pl.when(i == 0)
        def _():
            r.acc[:, 0:256] = jnp.zeros((512, 256), F32)

        r.acc[cols, 0:128] += dg(grad_scores, scaled, 0, 0)
        r.acc[cols, 128:256] += dg(probs, grad, 0, 0)
        dq = side_by_side(dg(grad_scores, r.qkv[1, cols, lanes], 1, 0)) * 0.125
        r.dqkv[0, rows, lanes] = dq.astype(BF)

        @pl.when(i == 1)
        def _():
            r.dqkv[1, :, lanes] = r.acc[:, 0:128].astype(BF)
            r.dqkv[2, :, lanes] = r.acc[:, 128:256].astype(BF)


class Refs:
    pass


ACTIVE = dict(
    qkv=((3, 512, 768), BF),
    kt=((2, 6, 528, 128), F32),
    kp=((2, 128, 768), BF),
    first=((512, 768), BF),
    q2=((512, 768), BF),
    mixed=((512, 768), BF),
    n1=((512, 768), F32),
    inv1=((512, 1), F32),
    hlow=((512, 768), BF),
    act=((4, 512, 768), BF),
    gd=((4, 512, 768), BF),
    dr=((512, 768), F32),
    acc=((512, 768), F32),
    dlow=((512, 768), BF),
    lse=((1024, 128), F32),
    bias1=((2, 256, 384), F32),
    bias2=((512, 128), F32),
)


def alias_late(r):
    r.dq2 = r.act.at[0]
    r.dfirst = r.act.at[1]
    r.dqkv = r.gd
    r.dpool = (r.n1.at[pl.ds(0, 136)], r.n1.at[pl.ds(256, 136)])


def slots(n):
    return dict(
        sq=((n, 7, 4, 48, 384), BF),
        up=((n, 4, 192, 384), BF),
        down=((n, 4, 96, 512), BF),
    )


BUFFERS = dict(
    tokens=((512, 768), BF),
    og=((512, 768), BF),
    gains=((2, 768), F32),
    shifts=((2, 768), F32),
    pool=((5, 2, 768), F32),
    shards=((7, 192, 96), BF),
    sq=(SQ, BF),
    up=(UP, BF),
    down=(DOWN, BF),
    s_sq=((7, 4, 2, 48, 768), BF),
    s_up=((2, 4, 2, 192, 384), BF),
    s_down=((4, 2, 2, 96, 768), BF),
    **{"r1_" + k: v for k, v in slots(2).items()},
    **{"r2_" + k: v for k, v in slots(1).items()},
    r3_sq=((3, 7, 48, 384), BF),
    pz=((3, 2, 2, 96, 256), BF),
    p2=((2, 96, 256), BF),
    p1=((96, 256), BF),
    b_sq=((7, 2, 48, 384), F32),
    b_up=((192, 384), F32),
    b_down=((96, 768), F32),
    vec=((16, 768), F32),
    r3_up=((3, 192, 384), BF),
    r3_down=((3, 96, 512), BF),
    vbuf=((10, 16, 768), F32),
    **ACTIVE,
)
SEMS = dict(
    load=18, swap=2, send=(N_GROUPS, 7), ag_r=(N_GROUPS, 10), rs_r=(N_GROUPS, 10), vs=7, vr=7, ends=5, endr=5
)


def layer_kernel(*refs):
    r = Refs()
    names = (
        ["length", "tokens_in", "og_in", "gains_in", "shifts_in", "pool_in"]
        + [f"shard{m}" for m in range(7)]
        + ["up_in", "down_in", "out", "din", "o_vec", "o_sq", "o_up", "o_down"]
        + list(BUFFERS)
        + list(SEMS)
    )
    for name, ref in zip(names, refs):
        setattr(r, name, ref)
    alias_late(r)
    me = Place()

    shards = [r.shards.at[m] for m in range(7)]
    pairs = [(getattr(r, f"shard{m}"), shards[m]) for m in range(7)]
    pairs += [
        (r.down_in, r.down.at[me.z, me.x, me.y, me.c]),
        (r.up_in, r.up.at[me.y, me.c, me.z, me.x]),
        (r.tokens_in, r.tokens),
        (r.pool_in, r.pool),
        (r.gains_in, r.gains),
        (r.shifts_in, r.shifts),
        (r.og_in, r.og),
    ]
    loads = [pltpu.make_async_copy(a, b, r.load.at[i]) for i, (a, b) in enumerate(pairs)]
    for cp in loads:
        cp.start()
    greet(me)
    weights = (r.sq, r.up, r.down)
    gat = Gather(me, weights, r.send, r.ag_r)
    sca = Scatter(
        me,
        weights,
        (r.s_sq, r.s_up, r.s_down),
        (r.r1_sq, r.r1_up, r.r1_down),
        (r.r2_sq, r.r2_up, r.r2_down),
        (r.r3_sq, r.r3_up, r.r3_down),
        (r.pz, r.p2, r.p1),
        r.send,
        r.rs_r,
    )

    loads[7].wait()
    gat.start(8)
    gat.go(6, 0, 1)
    for cp in loads[:7]:
        cp.wait()
    place_squares(me, shards, r.sq, r.act, r.swap.at[0], r.swap.at[1])
    for g in (0, 1, 9, 2, 3):
        gat.start(g)
    gat.step0(8)
    gat.step0(6)
    loads[8].wait()
    gat.start(4)
    gat.start(5)
    gat.go(6, 3, 4, 5)
    gat.start(7)
    set_masks(r, r.length[0])
    gat.step0(0)
    gat.step0(1)
    gat.step1(0)
    gat.step0(9)
    gat.step0(2)
    gat.step1(1)
    gat.step1(9)
    gat.step0(3)
    gat.step2(0)
    gat.step1(2)
    gat.step0(4)
    gat.step2(1)
    gat.step2(9)
    gat.step3(0)
    gat.step1(3)
    gat.step0(5)
    gat.step2(2)
    gat.step3(1)
    gat.step4(0)
    gat.step1(4)
    for cp in loads[9:]:
        cp.wait()
    gat.arrived(0)
    project(r, 0, 1)
    gat.step2(3)
    gat.step3(9)
    gat.step3(2)
    gat.step4(1)
    gat.step1(5)
    gat.step0(7)
    gat.step4(9)
    gat.arrived(1)
    project(r, 1, 2)
    gat.step1(6)
    gat.step2(4)
    gat.arrived(9)
    project(r, 2, 3)
    gat.step1(7)
    gat.step1(8)

    def ahead_a():
        gat.step4(2)
        gat.step2(5)

    level_one(r, {2: lambda: gat.step3(3), 4: ahead_a})
    gat.step3(4)
    gat.arrived(2)
    project_pool(r, 0)
    project_pool(r, 1)
    gat.step4(3)
    gat.step2(6)
    gat.arrived(3)

    def ahead_c():
        gat.step4(4)
        gat.step3(5)

    level_two(r, {3: ahead_c, 5: lambda: gat.step2(7)})
    first_norm(r)
    gat.step4(5)
    gat.arrived(4)
    gat.arrived(5)
    ffn_up(r, {1: lambda: gat.step3(6), 2: lambda: gat.step4(8), 3: lambda: gat.step4(6)})
    gat.step3(7)
    gat.arrived(8)
    ffn_down(r, 512, 768, True)
    gat.arrived(6)
    gat.step4(7)
    ffn_down(r, 0, 256, False)
    gat.arrived(7)
    ffn_down(r, 256, 512, False)
    second_norm(r)
    out = pltpu.make_async_copy(r.og, r.out, r.load.at[0])
    out.start()
    for g in range(N_GROUPS):
        gat.sent(g)

    def flush(src, dst):
        cp = pltpu.make_async_copy(src, dst, r.load.at[3 + len(pending)])
        cp.start()
        pending.append(cp)

    pending = []

    def give(g):
        kind, lo, hi = GROUPS[g]
        if kind == "u":
            r.b_up[lo:hi] = sca.finish(g)
            flush(r.b_up.at[lo:hi], r.o_up.at[lo:hi])
        else:
            r.b_down[:, lo:hi] = sca.finish(g)
            flush(r.b_down.at[:, lo:hi], r.o_down.at[:, lo:hi])

    def end_swap(g, incoming=False):
        _, lo, hi = GROUPS[g]
        b = r.b_sq.at[lo:hi, 1 - me.c if incoming else me.c]
        at = SQUARES.index(g)
        return rcopy(b, b, r.ends.at[at], r.endr.at[at], me.sibling())

    def end(g):
        _, lo, hi = GROUPS[g]
        r.b_sq[lo:hi, me.c] = sca.finish(g)
        end_swap(g).start()
        flush(r.b_sq.at[lo:hi, me.c], r.o_sq.at[lo:hi, me.c])

    def close(g):
        _, lo, hi = GROUPS[g]
        end_swap(g, True).wait_recv()
        flush(r.b_sq.at[lo:hi, 1 - me.c], r.o_sq.at[lo:hi, 1 - me.c])

    for g in (6, 8, 7):
        _, lo, hi = GROUPS[g]
        back_down(r, 1 - me.c, lo, hi)
        sca.start(g)
        back_down(r, me.c, lo, hi)
        sca.step1(g)
    sca.step2(6)
    back_hidden(r)
    grad_up(r)
    sca.start(4)
    sca.start(5)
    back_first_norm(r)
    sca.step2(7)
    sca.step3(6)
    back_out(r)
    sca.step1(4)
    sca.step1(5)
    back_level_two(r)
    sca.start(3)
    sca.step3(7)
    back_pool(r, 0)
    sca.step1(3)
    sca.step2(8)
    back_pool(r, 1)
    sca.start(2)
    total = VectorSum(me, r.vec, r.vbuf, r.vs, r.vr)
    total.send_z()

    back_level_one(
        r,
        {
            0: lambda: sca.step2(4),
            2: lambda: sca.step1(2),
            5: lambda: sca.step2(5),
            7: total.send_core,
            9: total.send_beside,
            11: lambda: sca.step3(4),
        },
    )
    finish_projection(r, 1, r.dqkv[1])
    sca.start(1)
    finish_projection(r, 2, r.dqkv[2])
    sca.start(9)
    sca.step1(1)
    sca.step2(3)
    finish_projection(r, 0, r.dqkv[0])
    sca.start(0)
    sca.step1(9)
    sca.step3(5)
    sca.step1(0)
    sca.step3(8)
    r.dlow[...] = r.dr[...].astype(BF)
    din = pltpu.make_async_copy(r.dlow, r.din, r.load.at[1])
    din.start()
    sca.step2(2)
    sca.step3(3)
    for g in (6, 7, 4, 5):
        give(g)
    sca.step2(1)
    sca.step3(2)
    sca.step2(9)
    give(8)
    sca.step3(1)
    sca.step2(0)
    end(3)
    sca.step3(9)
    sca.step3(0)
    end(2)
    close(3)
    close(2)
    total.take()
    vec_out = pltpu.make_async_copy(r.vec, r.o_vec, r.load.at[2])
    vec_out.start()
    end(1)
    end(9)
    end(0)
    for g in range(N_GROUPS):
        sca.sent(g)
    close(1)
    close(9)
    close(0)
    for g in SQUARES:
        end_swap(g).wait_send()
    for cp in [*pending, out, din, vec_out]:
        cp.wait()


def layer(length, tokens, og, gains, shifts, pool, squares, up, down):
    hbm = pl.BlockSpec(memory_space=pl.ANY)
    return pl.pallas_call(
        layer_kernel,
        out_shape=[
            jax.ShapeDtypeStruct((512, 768), BF),
            jax.ShapeDtypeStruct((512, 768), BF),
            jax.ShapeDtypeStruct((16, 768), F32),
            jax.ShapeDtypeStruct((7, 2, 48, 384), F32),
            jax.ShapeDtypeStruct((192, 384), F32),
            jax.ShapeDtypeStruct((96, 768), F32),
        ],
        in_specs=[pl.BlockSpec(memory_space=pltpu.SMEM)] + [hbm] * 14,
        out_specs=[hbm] * 6,
        scratch_shapes=[pltpu.VMEM(*s) for s in BUFFERS.values()]
        + [pltpu.SemaphoreType.DMA(s if isinstance(s, tuple) else (s,)) for s in SEMS.values()],
        compiler_params=pltpu.CompilerParams(
            collective_id=0, has_side_effects=True, vmem_limit_bytes=VMEM_LIMIT
        ),
    )(length, tokens, og, gains, shifts, pool, *squares, up, down)


VMEM_LIMIT = 63 * 2**20


def ending_kernel(*refs):
    o_act, o_din, o_up, o_down = refs[6], refs[7], refs[15], refs[16]
    o_sq = refs[8:15]
    o_gain, o_shift, o_pool, vec, sq, turned, sem = refs[17:]
    copies = [
        pltpu.make_async_copy(a, b, sem.at[i])
        for i, (a, b) in enumerate(zip(refs[:6], (o_act, o_din, vec, sq, o_up, o_down)))
    ]
    for i in (3, 2, 0, 1, 4, 5):
        copies[i].start()
    core = lax.rem(lax.axis_index("dp"), 2)
    mine = pl.ds(pl.multiple_of(core * 192, 8), 192)
    copies[3].wait()
    for m in range(7):
        turned[...] = jnp.transpose(sq[m].reshape(96, 384))
        o_sq[m][...] = turned[mine, :]
    copies[2].wait()
    o_gain[...] = vec[GAIN : GAIN + 2]
    o_shift[...] = vec[SHIFT : SHIFT + 2]
    for t in range(5):
        o_pool[t] = vec[POOL + 2 * t : POOL + 2 * t + 2]
    for i in (0, 1, 4, 5):
        copies[i].wait()


def ending(*parts):
    vmem = pl.BlockSpec(memory_space=pltpu.VMEM)
    shapes = [((512, 768), BF)] * 2 + [((192, 96), F32)] * 7 + [((192, 384), F32), ((96, 768), F32)]
    shapes += [((2, 768), F32)] * 2 + [((5, 2, 768), F32)]
    return pl.pallas_call(
        ending_kernel,
        out_shape=[jax.ShapeDtypeStruct(*s) for s in shapes],
        in_specs=[pl.BlockSpec(memory_space=pl.ANY)] * 6,
        out_specs=[vmem] * len(shapes),
        scratch_shapes=[
            pltpu.VMEM((16, 768), F32),
            pltpu.VMEM((7, 2, 48, 384), F32),
            pltpu.VMEM((384, 96), F32),
            pltpu.SemaphoreType.DMA((6,)),
        ],
        compiler_params=pltpu.CompilerParams(vmem_limit_bytes=VMEM_LIMIT),
    )(*parts)


def local_kernels(
    tokens,
    doc_lengths,
    w_query,
    w_key,
    w_value,
    w_query2,
    w_key2,
    w_value2,
    w_out,
    w_up,
    w_down,
    norm_gains,
    norm_shifts,
    pool_kernels,
    out_grad,
):
    squares = (w_query, w_key, w_value, w_key2, w_value2, w_query2, w_out)
    ends = layer(
        doc_lengths,
        tokens,
        out_grad,
        norm_gains,
        norm_shifts,
        pool_kernels.transpose(1, 0, 2),
        squares,
        w_up,
        w_down.T,
    )
    act, din, g_q, g_k, g_v, g_k2, g_v2, g_q2, g_out, g_up, g_down, gain, shift, pools = ending(*ends)
    return (
        act,
        din,
        g_q,
        g_k,
        g_v,
        g_q2,
        g_k2,
        g_v2,
        g_out,
        g_up,
        g_down.T,
        gain,
        shift,
        pools.transpose(1, 0, 2),
    )


def local(
    tokens,
    doc_lengths,
    w_query,
    w_key,
    w_value,
    w_query2,
    w_key2,
    w_value2,
    w_out,
    w_up,
    w_down,
    norm_gains,
    norm_shifts,
    pool_kernels,
    out_grad,
):
    shards = (w_query, w_key, w_value, w_query2, w_key2, w_value2, w_out, w_up, w_down)
    forward_weights = gather_first(shards)
    (
        full_query,
        full_key,
        full_value,
        full_query2,
        full_key2,
        full_value2,
        full_out,
        full_up,
        full_down,
    ) = forward_weights
    seq_rows = tokens.shape[0]
    length = doc_lengths[0]
    positions = jnp.arange(seq_rows, dtype=jnp.int32)
    padding = positions >= length
    allowed_one = (jnp.abs(positions[:, None] - positions[None, :]) <= WIN) & (
        padding[:, None] == padding[None, :]
    )
    pooled_at = positions[: seq_rows // STRIDE] * STRIDE
    allowed_two = (jnp.abs(positions[:, None] - pooled_at[None, :]) <= PWIN // 2) & (
        padding[:, None] == (pooled_at >= length)[None, :]
    )
    score_scale = 1.0 / math.sqrt(HD)
    query = matmul(tokens, full_query).astype(jnp.bfloat16)
    keys = matmul(tokens, full_key).astype(jnp.bfloat16)
    values = matmul(tokens, full_value).astype(jnp.bfloat16)
    key_two = matmul(tokens, full_key2)
    value_two = matmul(tokens, full_value2)
    key_pool_f, pool_key_back = jax.vjp(pool_rows, key_two, pool_kernels[0])
    value_pool_f, pool_value_back = jax.vjp(pool_rows, value_two, pool_kernels[1])
    key_pool = key_pool_f.astype(jnp.bfloat16)
    value_pool = value_pool_f.astype(jnp.bfloat16)
    first_f, log_one = level_forward(query, keys, values, allowed_one, score_scale)
    first = first_f.astype(jnp.bfloat16)
    query_two = matmul(first, full_query2).astype(jnp.bfloat16)
    second, log_two = level_forward(query_two, key_pool, value_pool, allowed_two, score_scale)
    mixed = (first.astype(jnp.float32) + second).astype(jnp.bfloat16)
    branch = matmul(mixed, full_out)
    hidden, norm_one_back = jax.vjp(
        layer_norm, tokens.astype(jnp.float32) + branch, norm_gains[0], norm_shifts[0]
    )
    hidden_low = hidden.astype(jnp.bfloat16)
    upper = matmul(hidden_low, full_up)
    activated_f, gelu_back = jax.vjp(gelu_tanh, upper)
    activated = activated_f.astype(jnp.bfloat16)
    resid_two = hidden + matmul(activated, full_down)
    result, norm_two_back = jax.vjp(layer_norm, resid_two, norm_gains[1], norm_shifts[1])
    activations = result.astype(jnp.bfloat16)
    back_weights = gather_second(shards)
    (
        back_query,
        back_key,
        back_value,
        back_query2,
        back_key2,
        back_value2,
        back_out,
        back_up,
        back_down,
    ) = back_weights
    d_resid_two, d_gain_two, d_shift_two = norm_two_back(out_grad.astype(jnp.float32))
    d_ffn = d_resid_two.astype(jnp.bfloat16)
    grad_down = inner_rows(activated, d_ffn)
    d_upper = gelu_back(outer_cols(d_ffn, back_down))[0].astype(jnp.bfloat16)
    grad_up = inner_rows(hidden_low, d_upper)
    d_hidden = d_resid_two + outer_cols(d_upper, back_up)
    d_resid_one, d_gain_one, d_shift_one = norm_one_back(d_hidden)
    d_branch = d_resid_one.astype(jnp.bfloat16)
    grad_out = inner_rows(mixed, d_branch)
    d_mixed = outer_cols(d_branch, back_out)
    d_query_two_f, d_key_pool_f, d_value_pool_f = level_backward(
        query_two,
        key_pool,
        value_pool,
        allowed_two,
        score_scale,
        log_two,
        d_mixed.astype(jnp.bfloat16),
    )
    d_query_two = d_query_two_f.astype(jnp.bfloat16)
    d_key_pool = d_key_pool_f.astype(jnp.bfloat16)
    d_value_pool = d_value_pool_f.astype(jnp.bfloat16)
    grad_query2 = inner_rows(first, d_query_two)
    d_first = (d_mixed + outer_cols(d_query_two, back_query2)).astype(jnp.bfloat16)
    d_query_f, d_keys_f, d_values_f = level_backward(
        query, keys, values, allowed_one, score_scale, log_one, d_first
    )
    d_query = d_query_f.astype(jnp.bfloat16)
    d_keys = d_keys_f.astype(jnp.bfloat16)
    d_values = d_values_f.astype(jnp.bfloat16)
    d_key_two_f, d_pool_key = pool_key_back(d_key_pool.astype(jnp.float32))
    d_value_two_f, d_pool_value = pool_value_back(d_value_pool.astype(jnp.float32))
    d_key_two = d_key_two_f.astype(jnp.bfloat16)
    d_value_two = d_value_two_f.astype(jnp.bfloat16)
    grad_query = inner_rows(tokens, d_query)
    grad_key = inner_rows(tokens, d_keys)
    grad_value = inner_rows(tokens, d_values)
    grad_key2 = inner_rows(tokens, d_key_two)
    grad_value2 = inner_rows(tokens, d_value_two)
    d_tokens = (
        d_resid_one
        + outer_cols(d_query, back_query)
        + outer_cols(d_keys, back_key)
        + outer_cols(d_values, back_value)
    )
    d_tokens = d_tokens + outer_cols(d_key_two, back_key2) + outer_cols(d_value_two, back_value2)
    grads_all = (
        grad_query,
        grad_key,
        grad_value,
        grad_query2,
        grad_key2,
        grad_value2,
        grad_out,
        grad_up,
        grad_down,
    )
    owned = reduce_columns_first(grads_all)
    gain_stack = jnp.stack([d_gain_one, d_gain_two])
    shift_stack = jnp.stack([d_shift_one, d_shift_two])
    pool_stack = jnp.stack([d_pool_key, d_pool_value])
    vector_sums = lax.psum((gain_stack, shift_stack, pool_stack), ("dp", "fsdp"))
    return (
        activations,
        d_tokens.astype(jnp.bfloat16),
        owned[0],
        owned[1],
        owned[2],
        owned[3],
        owned[4],
        owned[5],
        owned[6],
        owned[7],
        owned[8],
        vector_sums[0],
        vector_sums[1],
        vector_sums[2],
    )


def solution(mesh):
    fits = mesh.shape["dp"] == 4 and mesh.shape["fsdp"] == 8
    return jax.shard_map(
        local_kernels if fits else local,
        mesh=mesh,
        in_specs=(
            P(("dp", "fsdp"), None),
            P(("dp", "fsdp")),
            P("dp", "fsdp"),
            P("dp", "fsdp"),
            P("dp", "fsdp"),
            P("dp", "fsdp"),
            P("dp", "fsdp"),
            P("dp", "fsdp"),
            P("dp", "fsdp"),
            P("dp", "fsdp"),
            P("dp", "fsdp"),
            P(),
            P(),
            P(),
            P(("dp", "fsdp"), None),
        ),
        out_specs=(
            P(("dp", "fsdp"), None),
            P(("dp", "fsdp"), None),
            P("dp", "fsdp"),
            P("dp", "fsdp"),
            P("dp", "fsdp"),
            P("dp", "fsdp"),
            P("dp", "fsdp"),
            P("dp", "fsdp"),
            P("dp", "fsdp"),
            P("dp", "fsdp"),
            P("dp", "fsdp"),
            P(),
            P(),
            P(),
        ),
        check_vma=False,
    )
```

```python
import math

import jax
import jax.numpy as jnp
from jax import lax
from jax.experimental import pallas as pl
from jax.experimental.pallas import tpu as pltpu
from jax.sharding import PartitionSpec as P

HEADS = 12
HD = 64
WIN = 128
PWIN = 512
STRIDE = 4


def matmul(left_mat, right_mat):
    return jnp.dot(left_mat, right_mat, preferred_element_type=jnp.float32)


def inner_rows(left_mat, right_mat):
    return lax.dot_general(
        left_mat, right_mat, (((0,), (0,)), ((), ())), preferred_element_type=jnp.float32
    )


def outer_cols(left_mat, right_mat):
    return lax.dot_general(
        left_mat, right_mat, (((1,), (1,)), ((), ())), preferred_element_type=jnp.float32
    )


def layer_norm(inputs, norm_gain, norm_shift):
    average = jnp.mean(inputs, axis=-1, keepdims=True)
    centred = inputs - average
    variance = jnp.mean(centred * centred, axis=-1, keepdims=True)
    return centred * lax.rsqrt(variance + 1e-05) * norm_gain + norm_shift


def gelu_tanh(inputs):
    return jax.nn.gelu(inputs, approximate=True)


def pool_rows(inputs, kernel):
    side_rows = (kernel.shape[0] - 1) // 2
    pooled_rows = inputs.shape[0] // STRIDE
    padded = jnp.pad(inputs, ((side_rows, side_rows), (0, 0)))
    summed = jnp.zeros((pooled_rows, inputs.shape[1]), jnp.float32)
    for offset in range(kernel.shape[0]):
        summed = summed + kernel[offset] * padded[offset : offset + inputs.shape[0] : STRIDE]
    return summed


def split_heads(matrix):
    return matrix.reshape(matrix.shape[0], HEADS // 2, 2, HD).transpose(1, 0, 2, 3)


def join_heads(groups):
    return groups.transpose(1, 0, 2, 3).reshape(groups.shape[1], HEADS * HD)


def masked_scores(query, keys, allowed, score_scale):
    raw_scores = (
        jnp.einsum("ihd,jhd->hij", query, keys, preferred_element_type=jnp.float32) * score_scale
    )
    return jnp.where(allowed[None], raw_scores, -1e30)


def attend_forward(query, keys, values, allowed, score_scale):
    scores = masked_scores(query, keys, allowed, score_scale)
    highest = jnp.max(scores, axis=-1, keepdims=True)
    expo_terms = jnp.exp(scores - highest)
    summed = jnp.sum(expo_terms, axis=-1, keepdims=True)
    soft_weights = (expo_terms / summed).astype(jnp.bfloat16)
    result = jnp.einsum("hij,jhd->ihd", soft_weights, values, preferred_element_type=jnp.float32)
    return (result, (highest + jnp.log(summed))[..., 0])


def attend_backward(query, keys, values, allowed, score_scale, log_total, grad_result):
    scores = masked_scores(query, keys, allowed, score_scale)
    soft_weights = jnp.exp(scores - log_total[..., None])
    grad_soft = jnp.einsum("ihd,jhd->hij", grad_result, values, preferred_element_type=jnp.float32)
    grad_values = jnp.einsum(
        "hij,ihd->jhd",
        soft_weights.astype(jnp.bfloat16),
        grad_result,
        preferred_element_type=jnp.float32,
    )
    row_terms = jnp.sum(soft_weights * grad_soft, axis=-1, keepdims=True)
    grad_scores = (soft_weights * (grad_soft - row_terms)).astype(jnp.bfloat16)
    grad_query = (
        jnp.einsum("hij,jhd->ihd", grad_scores, keys, preferred_element_type=jnp.float32)
        * score_scale
    )
    grad_keys = (
        jnp.einsum("hij,ihd->jhd", grad_scores, query, preferred_element_type=jnp.float32)
        * score_scale
    )
    return (grad_query, grad_keys, grad_values)


def level_forward(query, keys, values, allowed, score_scale):

    def one_group(group_parts):
        return attend_forward(group_parts[0], group_parts[1], group_parts[2], allowed, score_scale)

    results, log_totals = lax.map(
        one_group, (split_heads(query), split_heads(keys), split_heads(values))
    )
    return (join_heads(results), log_totals)


def level_backward(query, keys, values, allowed, score_scale, log_totals, grad_result):

    def one_group(group_parts):
        return attend_backward(
            group_parts[0],
            group_parts[1],
            group_parts[2],
            allowed,
            score_scale,
            group_parts[3],
            group_parts[4],
        )

    grad_query, grad_keys, grad_values = lax.map(
        one_group,
        (
            split_heads(query),
            split_heads(keys),
            split_heads(values),
            log_totals,
            split_heads(grad_result),
        ),
    )
    return (join_heads(grad_query), join_heads(grad_keys), join_heads(grad_values))


def gather_first(shards):
    column_parts = (
        lax.all_gather(shards[0], "fsdp", axis=1, tiled=True),
        lax.all_gather(shards[1], "fsdp", axis=1, tiled=True),
        lax.all_gather(shards[2], "fsdp", axis=1, tiled=True),
        lax.all_gather(shards[3], "fsdp", axis=1, tiled=True),
        lax.all_gather(shards[4], "fsdp", axis=1, tiled=True),
        lax.all_gather(shards[5], "fsdp", axis=1, tiled=True),
        lax.all_gather(shards[6], "fsdp", axis=1, tiled=True),
        lax.all_gather(shards[7], "fsdp", axis=1, tiled=True),
        lax.all_gather(shards[8], "fsdp", axis=1, tiled=True),
    )
    return (
        lax.all_gather(column_parts[0], "dp", axis=0, tiled=True),
        lax.all_gather(column_parts[1], "dp", axis=0, tiled=True),
        lax.all_gather(column_parts[2], "dp", axis=0, tiled=True),
        lax.all_gather(column_parts[3], "dp", axis=0, tiled=True),
        lax.all_gather(column_parts[4], "dp", axis=0, tiled=True),
        lax.all_gather(column_parts[5], "dp", axis=0, tiled=True),
        lax.all_gather(column_parts[6], "dp", axis=0, tiled=True),
        lax.all_gather(column_parts[7], "dp", axis=0, tiled=True),
        lax.all_gather(column_parts[8], "dp", axis=0, tiled=True),
    )


def gather_second(shards):
    column_parts = (
        lax.all_gather(shards[0], "fsdp", axis=1, tiled=True),
        lax.all_gather(shards[1], "fsdp", axis=1, tiled=True),
        lax.all_gather(shards[2], "fsdp", axis=1, tiled=True),
        lax.all_gather(shards[3], "fsdp", axis=1, tiled=True),
        lax.all_gather(shards[4], "fsdp", axis=1, tiled=True),
        lax.all_gather(shards[5], "fsdp", axis=1, tiled=True),
        lax.all_gather(shards[6], "fsdp", axis=1, tiled=True),
        lax.all_gather(shards[7], "fsdp", axis=1, tiled=True),
        lax.all_gather(shards[8], "fsdp", axis=1, tiled=True),
    )
    return (
        lax.all_gather(column_parts[0], "dp", axis=0, tiled=True),
        lax.all_gather(column_parts[1], "dp", axis=0, tiled=True),
        lax.all_gather(column_parts[2], "dp", axis=0, tiled=True),
        lax.all_gather(column_parts[3], "dp", axis=0, tiled=True),
        lax.all_gather(column_parts[4], "dp", axis=0, tiled=True),
        lax.all_gather(column_parts[5], "dp", axis=0, tiled=True),
        lax.all_gather(column_parts[6], "dp", axis=0, tiled=True),
        lax.all_gather(column_parts[7], "dp", axis=0, tiled=True),
        lax.all_gather(column_parts[8], "dp", axis=0, tiled=True),
    )


def reduce_columns_first(grads_all):
    column_sums = (
        lax.psum_scatter(
            grads_all[0].astype(jnp.bfloat16), "fsdp", scatter_dimension=1, tiled=True
        ).astype(jnp.float32),
        lax.psum_scatter(
            grads_all[1].astype(jnp.bfloat16), "fsdp", scatter_dimension=1, tiled=True
        ).astype(jnp.float32),
        lax.psum_scatter(
            grads_all[2].astype(jnp.bfloat16), "fsdp", scatter_dimension=1, tiled=True
        ).astype(jnp.float32),
        lax.psum_scatter(
            grads_all[3].astype(jnp.bfloat16), "fsdp", scatter_dimension=1, tiled=True
        ).astype(jnp.float32),
        lax.psum_scatter(
            grads_all[4].astype(jnp.bfloat16), "fsdp", scatter_dimension=1, tiled=True
        ).astype(jnp.float32),
        lax.psum_scatter(
            grads_all[5].astype(jnp.bfloat16), "fsdp", scatter_dimension=1, tiled=True
        ).astype(jnp.float32),
        lax.psum_scatter(
            grads_all[6].astype(jnp.bfloat16), "fsdp", scatter_dimension=1, tiled=True
        ).astype(jnp.float32),
        lax.psum_scatter(
            grads_all[7].astype(jnp.bfloat16), "fsdp", scatter_dimension=1, tiled=True
        ).astype(jnp.float32),
        lax.psum_scatter(
            grads_all[8].astype(jnp.bfloat16), "fsdp", scatter_dimension=1, tiled=True
        ).astype(jnp.float32),
    )
    return (
        lax.psum_scatter(
            column_sums[0].astype(jnp.bfloat16), "dp", scatter_dimension=0, tiled=True
        ).astype(jnp.float32),
        lax.psum_scatter(
            column_sums[1].astype(jnp.bfloat16), "dp", scatter_dimension=0, tiled=True
        ).astype(jnp.float32),
        lax.psum_scatter(
            column_sums[2].astype(jnp.bfloat16), "dp", scatter_dimension=0, tiled=True
        ).astype(jnp.float32),
        lax.psum_scatter(
            column_sums[3].astype(jnp.bfloat16), "dp", scatter_dimension=0, tiled=True
        ).astype(jnp.float32),
        lax.psum_scatter(
            column_sums[4].astype(jnp.bfloat16), "dp", scatter_dimension=0, tiled=True
        ).astype(jnp.float32),
        lax.psum_scatter(
            column_sums[5].astype(jnp.bfloat16), "dp", scatter_dimension=0, tiled=True
        ).astype(jnp.float32),
        lax.psum_scatter(
            column_sums[6].astype(jnp.bfloat16), "dp", scatter_dimension=0, tiled=True
        ).astype(jnp.float32),
        lax.psum_scatter(
            column_sums[7].astype(jnp.bfloat16), "dp", scatter_dimension=0, tiled=True
        ).astype(jnp.float32),
        lax.psum_scatter(
            column_sums[8].astype(jnp.bfloat16), "dp", scatter_dimension=0, tiled=True
        ).astype(jnp.float32),
    )


MESH = pl.DeviceIdType.MESH
BF = jnp.bfloat16
F32 = jnp.float32

GROUPS = (
    ("s", 0, 1),
    ("s", 1, 2),
    ("s", 3, 5),
    ("s", 5, 7),
    ("u", 0, 96),
    ("u", 96, 192),
    ("d", 0, 256),
    ("d", 256, 512),
    ("d", 512, 768),
    ("s", 2, 3),
)
SQUARES = (0, 1, 2, 3, 9)
PLANE = 8
N_GROUPS = len(GROUPS)
SQ = (7, 4, 2, 2, 48, 768)
UP = (2, 2, 4, 2, 192, 384)
DOWN = (4, 2, 2, 2, 96, 768)


class Place:
    def __init__(self):
        dp = lax.axis_index("dp")
        fs = lax.axis_index("fsdp")
        self.y = lax.div(dp, 2)
        self.c = lax.rem(dp, 2)
        self.z = lax.div(fs, 2)
        self.x = lax.rem(fs, 2)
        c, x, y = self.c, self.x, self.y
        self.p1 = ((1 - c) * (1 - x) + c * x, (1 - c) * y + c * (1 - y))
        self.p2 = ((1 - c) * x + c * (1 - x), (1 - c) * (1 - y) + c * y)
        self.own = (x, y)
        self.diag = (1 - x, 1 - y)

    def dev(self, xy, z=None, c=None):
        z = self.z if z is None else z
        c = self.c if c is None else c
        return (xy[1] * 2 + c, z * 2 + xy[0])

    def sibling(self):
        return self.dev(self.own, c=1 - self.c)

    def peer(self, k):
        return lax.rem(self.z + k, 4)

    def everyone(self):
        return [self.sibling(), self.dev(self.p1), self.dev(self.p2), self.dev(self.diag)] + [
            self.dev(self.own, z=self.peer(k)) for k in (1, 2, 3)
        ]


def greet(me):
    bar = pltpu.get_barrier_semaphore()
    for d in me.everyone():
        pl.semaphore_signal(bar, inc=1, device_id=d, device_id_type=MESH)
    pl.semaphore_wait(bar, 7)


def square_lanes(y):
    return pl.ds(pl.multiple_of(y * 384, 128), 384)


def blocks(refs, g, xy, c, z=slice(None)):
    sq, up, down = refs
    x, y = xy
    kind, lo, hi = GROUPS[g]
    if kind == "s":
        return sq.at[lo:hi, z, x, c, :, square_lanes(y)]
    if kind == "u":
        return up.at[y, c, z, x, lo:hi]
    return down.at[z, x, y, c, :, lo:hi]


def half(refs, g, c):
    sq, up, down = refs
    kind, lo, hi = GROUPS[g]
    if kind == "s":
        return sq.at[lo:hi, :, :, c]
    if kind == "u":
        return up.at[:, c, :, :, lo:hi]
    return down.at[:, :, :, c, :, lo:hi]


def plane(down, g, c, z):
    _, lo, hi = GROUPS[g]
    return down.at[z, :, :, c, :, lo:hi]


def rcopy(src, dst, ssem, rsem, dev):
    return pltpu.make_async_remote_copy(
        src_ref=src, dst_ref=dst, send_sem=ssem, recv_sem=rsem, device_id=dev, device_id_type=MESH
    )


class Gather:
    def __init__(self, me, refs, ssem, rsem):
        self.me, self.refs, self.ssem, self.rsem = me, refs, ssem, rsem

    def copy(self, g, i, incoming=False):
        me = self.me
        together = min(i, 6) if i < 10 else (i - 10) // 3
        first = 0 if i in (3, 4, 5) and g != PLANE else together
        ss = self.ssem.at[g, i - 7 if i in (10, 11, 12) else first]
        rs = self.rsem.at[g, i - 3 if i in (10, 11, 12) else together]
        side = 1 if incoming else 0
        c = me.c
        ways = ((me.own, me.p1), (me.own, me.p2), (me.p1, me.diag))
        if i < 3:
            b = blocks(self.refs, g, ways[i][side], c, me.z)
            return rcopy(b, b, ss, rs, me.dev(me.p1 if i == 0 else me.p2))
        if i < 6:
            k = i - 2
            z = lax.rem(me.z + 4 - k, 4) if incoming else me.z
            b = plane(self.refs[2], g, c, z) if g == PLANE else blocks(self.refs, g, me.own, c, z)
            return rcopy(b, b, ss, rs, me.dev(me.own, z=me.peer(k)))
        if i < 10:
            cc = 1 - c if incoming else c
            what = ((me.own, me.own), (me.p1, me.p2), (me.p2, me.p1), (me.diag, me.diag))[i - 6][side]
            if g == PLANE:
                b = plane(self.refs[2], g, cc, lax.rem(me.z + 4 - (i - 6), 4))
            else:
                b = blocks(self.refs, g, what, cc)
            return rcopy(b, b, ss, rs, me.sibling())
        way, k = (i - 10) // 3, (i - 10) % 3 + 1
        b = blocks(self.refs, g, ways[way][side], c, lax.rem(me.z + 4 - k, 4))
        return rcopy(b, b, ss, rs, me.dev(me.p1 if way == 0 else me.p2))

    def go(self, g, *which):
        for i in which:
            self.copy(g, i).start()

    def got(self, g, *which):
        for i in which:
            self.copy(g, i, True).wait_recv()

    def whole(self, g, at, ref):
        return rcopy(ref, ref, self.ssem.at[g, at], self.rsem.at[g, at], self.me.sibling())

    def start(self, g):
        self.go(g, *((0, 1) if g == PLANE else (0, 1, 3, 4, 5)))

    def step0(self, g):
        self.got(g, 0)
        self.go(g, 2)

    def step1(self, g):
        if g == PLANE:
            self.got(g, 1, 2)
            self.go(g, 3, 4, 5, 6)
            return
        for k in range(3):
            self.got(g, 3 + k)
            self.go(g, 13 + k, 10 + k)
        self.go(g, 6)

    def step2(self, g):
        for k in range(3):
            self.got(g, 10 + k)
            self.go(g, 16 + k)
        self.go(g, 7)

    def step3(self, g):
        self.whole(g, 1, blocks(self.refs, g, self.me.p2, self.me.c)).wait_recv()
        self.go(g, 8)

    def step4(self, g):
        if g == PLANE:
            for i in (3, 4, 5):
                self.got(g, i)
                self.go(g, i + 4)
            return
        self.whole(g, 2, blocks(self.refs, g, self.me.diag, self.me.c)).wait_recv()
        self.go(g, 9)

    def arrived(self, g):
        self.whole(g, 6, half(self.refs, g, 1 - self.me.c)).wait_recv()

    def sent(self, g):
        me = self.me
        if g == PLANE:
            for i in range(6):
                self.copy(g, i).wait_send()
        else:
            for at in range(3):
                self.whole(g, at, blocks(self.refs, g, me.own, me.c)).wait_send()
            for i in (10, 11, 12):
                self.copy(g, i).wait_send()
        self.whole(g, 6, half(self.refs, g, me.c)).wait_send()


class Scatter:
    def __init__(self, me, refs, sib, r1, r2, r3, rp, ssem, rsem):
        self.me, self.refs, self.sib = me, refs, sib
        self.r1, self.r2, self.r3 = r1, r2, r3
        self.pz, self.p2, self.p1 = rp
        self.ssem, self.rsem = ssem, rsem

    def sib_view(self, g, xy, z=slice(None)):
        sq, up, down = self.sib
        x, y = xy
        kind, lo, hi = GROUPS[g]
        if kind == "s":
            return sq.at[lo:hi, z, x, :, square_lanes(y)]
        if kind == "u":
            return up.at[y, z, x, lo:hi]
        return down.at[z, x, y, :, lo:hi]

    def plane_of(self, g, c, z):
        return plane(self.refs[2], g, c, z)

    def sib_plane(self, g, z):
        _, lo, hi = GROUPS[g]
        return self.sib[2].at[z, :, :, :, lo:hi]

    def slot(self, bufs, g, i):
        kind, lo, hi = GROUPS[g]
        if kind == "s":
            return bufs[0].at[i, lo:hi]
        buf = bufs[1 if kind == "u" else 2]
        if kind == "d":
            return buf.at[i, :, :, lo:hi] if len(buf.shape) == 4 else buf.at[i, :, lo:hi]
        return buf.at[i, :, lo:hi] if len(buf.shape) == 4 else buf.at[i, lo:hi]

    def copy(self, g, i):
        me = self.me
        c = me.c
        ss, rs = self.ssem.at[g, max(i - 3, 0)], self.rsem.at[g, i]
        if g == PLANE:
            if i < 4:
                z = me.peer(i + 1)
                return rcopy(self.plane_of(g, 1 - c, z), self.sib_plane(g, z), ss, rs, me.sibling())
            if i < 7:
                k = i - 3
                src = self.plane_of(g, c, me.peer(k))
                return rcopy(src, self.pz.at[k - 1], ss, rs, me.dev(me.own, z=me.peer(k)))
            if i < 9:
                src = blocks(self.refs, g, (me.diag, me.p2)[i - 7], c, me.z)
                return rcopy(src, self.p2.at[i - 7], ss, rs, me.dev(me.p2))
            return rcopy(blocks(self.refs, g, me.p1, c, me.z), self.p1, ss, rs, me.dev(me.p1))
        if i < 4:
            what = (me.p1, me.diag, me.p2, me.own)[i]
            return rcopy(blocks(self.refs, g, what, 1 - c), self.sib_view(g, what), ss, rs, me.sibling())
        if i < 6:
            src = blocks(self.refs, g, (me.diag, me.p2)[i - 4], c)
            return rcopy(src, self.slot(self.r1, g, i - 4), ss, rs, me.dev(me.p2))
        if i == 6:
            return rcopy(blocks(self.refs, g, me.p1, c), self.slot(self.r2, g, 0), ss, rs, me.dev(me.p1))
        k = i - 6
        src = blocks(self.refs, g, me.own, c, me.peer(k))
        return rcopy(src, self.slot(self.r3, g, k - 1), ss, rs, me.dev(me.own, z=me.peer(k)))

    def go(self, g, *which):
        for i in which:
            self.copy(g, i).start()

    def got(self, g, i):
        self.copy(g, i).wait_recv()

    def add(self, here, *others):
        total = here[...].astype(F32)
        for other in others:
            total = total + other[...].astype(F32)
        here[...] = total.astype(BF)

    def start(self, g):
        self.go(g, 0, 1, 2, 3)

    def step1(self, g):
        me = self.me
        if g == PLANE:
            for k in (1, 2, 3):
                z = me.peer(k)
                self.got(g, k - 1)
                self.add(self.plane_of(g, me.c, z), self.sib_plane(g, z))
                self.go(g, 3 + k)
            return
        for i, what, out in ((1, me.diag, 4), (0, me.p2, 5)):
            self.got(g, i)
            self.add(blocks(self.refs, g, what, me.c), self.sib_view(g, what))
            self.go(g, out)

    def step2(self, g):
        me = self.me
        if g == PLANE:
            for i in (3, 4, 5, 6):
                self.got(g, i)
            here = self.plane_of(g, me.c, me.z)
            self.add(here, self.sib_plane(g, me.z), *[self.pz.at[k] for k in range(3)])
            self.go(g, 7, 8)
            return
        self.got(g, 2)
        self.got(g, 4)
        here = blocks(self.refs, g, me.p1, me.c)
        self.add(here, self.sib_view(g, me.p1), self.slot(self.r1, g, 0))
        self.go(g, 6)

    def step3(self, g):
        me = self.me
        if g == PLANE:
            self.got(g, 7)
            self.add(blocks(self.refs, g, me.p1, me.c, me.z), self.p2.at[0])
            self.go(g, 9)
            return
        self.got(g, 3)
        self.got(g, 5)
        self.got(g, 6)
        here = blocks(self.refs, g, me.own, me.c)
        self.add(here, self.sib_view(g, me.own), self.slot(self.r1, g, 1), self.slot(self.r2, g, 0))
        self.go(g, 7, 8, 9)

    def finish(self, g):
        me = self.me
        total = blocks(self.refs, g, me.own, me.c, me.z)[...].astype(F32)
        if g == PLANE:
            self.got(g, 8)
            self.got(g, 9)
            return total + self.p2[1].astype(F32) + self.p1[...].astype(F32)
        for k in (1, 2, 3):
            self.got(g, 6 + k)
            total = total + self.slot(self.r3, g, k - 1)[...].astype(F32)
        return total

    def sent(self, g):
        away = half(self.refs, g, 1 - self.me.c)
        rcopy(away, away, self.ssem.at[g, 0], self.rsem.at[g, 0], self.me.sibling()).wait_send()
        for i in range(4, 10):
            self.copy(g, i).wait_send()


class VectorSum:
    def __init__(self, me, vec, buf, ssem, rsem):
        self.me, self.vec, self.buf, self.ssem, self.rsem = me, vec, buf, ssem, rsem

    def copy(self, i, incoming=False):
        me = self.me
        if i < 3:
            z = lax.rem(me.z + 3 - i, 4) if incoming else me.z
            b, d = self.buf.at[z], me.dev(me.own, z=me.peer(i + 1))
        elif i == 3:
            return rcopy(self.buf.at[4], self.buf.at[5], self.ssem.at[i], self.rsem.at[i], me.sibling())
        else:
            x, y = ((1 - me.x, me.y), (me.x, 1 - me.y), me.diag)[i - 4]
            fx, fy = (x, y) if incoming else me.own
            b, d = self.buf.at[6 + fx + 2 * fy], me.dev((x, y))
        return rcopy(b, b, self.ssem.at[i], self.rsem.at[i], d)

    def send(self, first, last):
        for i in range(first, last):
            self.copy(i).start()

    def got(self, first, last):
        for i in range(first, last):
            self.copy(i, True).wait_recv()

    def send_z(self):
        self.buf[self.me.z] = self.vec[...]
        self.send(0, 3)

    def send_core(self):
        self.got(0, 3)
        b = self.buf
        b[4] = (b[0] + b[1]) + (b[2] + b[3])
        self.send(3, 4)

    def send_beside(self):
        self.got(3, 4)
        b = self.buf
        b[6 + self.me.x + 2 * self.me.y] = b[4] + b[5]
        self.send(4, 7)

    def take(self):
        self.got(4, 7)
        b = self.buf
        self.vec[...] = (b[6] + b[7]) + (b[8] + b[9])
        for i in range(7):
            self.copy(i).wait_send()


def place_squares(me, shards, sq, room, ssem, rsem):
    rows = lax.broadcasted_iota(jnp.int32, (192, 384), 0)
    lanes = lax.broadcasted_iota(jnp.int32, (192, 384), 1)
    spot = jnp.where(lanes == rows + me.c * 192, 1.0, 0.0).astype(BF)
    for m in range(7):
        t = dg(shards[m][...], spot, 0, 0).astype(BF)
        for half in range(2):
            room[half, 48 * m : 48 * m + 48, 0:384] = t[48 * half : 48 * half + 48]
    area = (pl.ds(0, 336), pl.ds(0, 384))
    swap = rcopy(room.at[(1 - me.c, *area)], room.at[(2, *area)], ssem, rsem, me.sibling())
    swap.start()
    swap.wait()
    for m in range(7):
        rows = slice(48 * m, 48 * m + 48)
        both = room[me.c, rows, 0:384].astype(F32) + room[2, rows, 0:384].astype(F32)
        sq[m, me.z, me.x, me.c, :, square_lanes(me.y)] = both.astype(BF)


GAIN, SHIFT, POOL = 0, 2, 4


def dg(a, b, ca, cb):
    return lax.dot_general(a, b, (((ca,), (cb,)), ((), ())), preferred_element_type=F32)


def weight(r, m):
    return r.sq[m].reshape(768, 768)


def weight_up(r, j):
    left = r.up[:, :, j, 0].reshape(768, 384)
    right = r.up[:, :, j, 1].reshape(768, 384)
    return jnp.concatenate([left, right], axis=1)


def weight_down(r, y, c, lo, hi):
    return r.down[:, :, y, c, :, lo:hi].reshape(768, hi - lo)


def set_masks(r, length):
    for i in range(2):
        row = lax.broadcasted_iota(jnp.int32, (256, 384), 0) + 256 * i
        col = lax.broadcasted_iota(jnp.int32, (256, 384), 1) + 128 * i
        ok = (jnp.abs(row - col) <= WIN) & ((row >= length) == (col >= length))
        r.bias1[i] = jnp.where(ok, 0.0, -1e30)
    row = lax.broadcasted_iota(jnp.int32, (512, 128), 0)
    col = lax.broadcasted_iota(jnp.int32, (512, 128), 1) * STRIDE
    ok = (jnp.abs(row - col) <= PWIN // 2) & ((row >= length) == (col >= length))
    r.bias2[...] = jnp.where(ok, 0.0, -1e30)


def low_lanes(rows):
    return lax.broadcasted_iota(jnp.int32, (rows, 128), 1) < HD


def two_heads(pair):
    low = low_lanes(pair.shape[0])
    zero = jnp.zeros_like(pair)
    return jnp.concatenate([jnp.where(low, pair, zero), jnp.where(low, zero, pair)], axis=0)


def side_by_side(stacked):
    n = stacked.shape[0] // 2
    return jnp.where(low_lanes(n), stacked[:n], stacked[n:])


def pair_lanes(p):
    return pl.ds(pl.multiple_of(p * 128, 128), 128)


def softmax_out(scores, bias, values, lse_ref, p):
    scores = scores + jnp.concatenate([bias, bias], axis=0)
    highest = jnp.max(scores, axis=-1, keepdims=True)
    terms = jnp.exp(scores - highest)
    summed = jnp.sum(terms, axis=-1, keepdims=True)
    probs = (terms * (1.0 / summed)).astype(BF)
    lane = lax.broadcasted_iota(jnp.int32, lse_ref.shape, 1)
    lse_ref[...] = jnp.where(lane == p, highest + jnp.log(summed), lse_ref[...])
    return side_by_side(dg(probs, values, 1, 0))


def scores_of(query, keys):
    scaled = two_heads(query * jnp.asarray(0.125, BF))
    return scaled, dg(scaled, keys, 1, 1)


def softmax_back(scores, bias, lse_ref, p, grad, values):
    scores = scores + jnp.concatenate([bias, bias], axis=0)
    lane = lax.broadcasted_iota(jnp.int32, lse_ref.shape, 1)
    lse = jnp.sum(jnp.where(lane == p, lse_ref[...], 0.0), axis=-1, keepdims=True)
    probs = jnp.exp(scores - lse)
    grad_probs = dg(grad, values, 1, 1)
    row_terms = jnp.sum(probs * grad_probs, axis=-1, keepdims=True)
    return probs.astype(BF), (probs * (grad_probs - row_terms)).astype(BF)


def project(r, lo, hi):
    @pl.loop(lo, hi)
    def _(m):
        r.qkv[m] = dg(r.tokens[...], weight(r, m), 1, 1).astype(BF)


def project_pool(r, i):
    full = None
    for l in range(6):
        lanes = slice(l * 128, l * 128 + 128)
        if l % 3 == 0:
            full = dg(r.tokens[...], r.sq[3 + i, 2 * (l // 3) : 2 * (l // 3) + 2].reshape(384, 768), 1, 1)
        r.kt[i, l, 0:8] = jnp.zeros((8, 128), F32)
        r.kt[i, l, 520:528] = jnp.zeros((8, 128), F32)
        r.kt[i, l, 8:520] = full[:, (l % 3) * 128 : (l % 3) * 128 + 128]
        total = None
        for t in range(5):
            term = r.pool[t, i : i + 1, lanes] * r.kt[i, l, pl.ds(6 + t, 128, stride=STRIDE), :]
            total = term if total is None else total + term
        r.kp[i, :, lanes] = total.astype(BF)


def at_steps(p, hooks):
    for at, hook in (hooks or {}).items():
        pl.when(p == at)(hook)


def level_one(r, hooks=None):
    @pl.loop(0, HEADS // 2)
    def _(p):
        at_steps(p, hooks)
        lanes = pair_lanes(p)
        for i in range(2):
            rows, cols = pl.ds(256 * i, 256), pl.ds(128 * i, 384)
            _, scores = scores_of(r.qkv[0, rows, lanes], r.qkv[1, cols, lanes])
            out = softmax_out(scores, r.bias1[i], r.qkv[2, cols, lanes], r.lse.at[pl.ds(512 * i, 512)], p)
            r.first[rows, lanes] = out.astype(BF)


def level_two(r, hooks=None):
    r.q2[...] = dg(r.first[...], weight(r, 5), 1, 1).astype(BF)

    @pl.loop(0, HEADS // 2)
    def _(p):
        at_steps(p, hooks)
        lanes = pair_lanes(p)
        _, scores = scores_of(r.q2[:, lanes], r.kp[0, :, lanes])
        out = softmax_out(scores, r.bias2[...], r.kp[1, :, lanes], r.lse, p + HEADS // 2)
        r.mixed[:, lanes] = (r.first[:, lanes].astype(F32) + out).astype(BF)


def norm_parts(x):
    average = jnp.mean(x, axis=-1, keepdims=True)
    centred = x - average
    inverse = lax.rsqrt(jnp.mean(centred * centred, axis=-1, keepdims=True) + 1e-05)
    return centred * inverse, inverse


def norm_back(n, inverse, gain, grad):
    scaled = grad * gain
    return (
        scaled - jnp.mean(scaled, axis=-1, keepdims=True) - n * jnp.mean(scaled * n, axis=-1, keepdims=True)
    ) * inverse


def first_norm(r):
    r.acc[...] = dg(r.mixed[...], weight(r, 6), 1, 1)

    @pl.loop(0, 4)
    def _(i):
        rows = pl.ds(pl.multiple_of(i * 128, 128), 128)
        n, inverse = norm_parts(r.tokens[rows].astype(F32) + r.acc[rows])
        r.n1[rows] = n
        r.inv1[rows] = inverse
        r.hlow[rows] = (n * r.gains[0:1] + r.shifts[0:1]).astype(BF)


def ffn_up(r, hooks=None):
    k = math.sqrt(2.0 / math.pi)

    @pl.loop(0, 4)
    def _(j):
        at_steps(j, hooks)
        for i in range(2):
            rows = pl.ds(256 * i, 256)
            u = dg(r.hlow[rows], weight_up(r, j), 1, 0)
            square = u * u
            half = 0.5 + 0.5 * jnp.tanh(u * (k + (k * 0.044715) * square))
            value = u * half
            r.act[j, rows] = value.astype(BF)
            slope = half + value * (1.0 - half) * (2 * k + (6 * k * 0.044715) * square)
            r.gd[j, rows] = slope.astype(BF)


def ffn_down(r, lo, hi, first):
    @pl.loop(0, 2)
    def _(i):
        rows = pl.ds(pl.multiple_of(256 * i, 256), 256)
        total = None if first else r.acc[rows]
        for j in range(4):
            term = dg(r.act[j, rows, lo:hi], weight_down(r, j // 2, j % 2, lo, hi), 1, 1)
            total = term if total is None else total + term
        r.acc[rows] = total


def second_norm(r):
    r.vec[...] = jnp.zeros_like(r.vec)

    @pl.loop(0, 4)
    def _(i):
        rows = pl.ds(pl.multiple_of(i * 128, 128), 128)
        hidden = r.n1[rows] * r.gains[0:1] + r.shifts[0:1]
        n, inverse = norm_parts(hidden + r.acc[rows])
        grad = r.og[rows].astype(F32)
        r.og[rows] = (n * r.gains[1:2] + r.shifts[1:2]).astype(BF)
        r.vec[GAIN + 1 : GAIN + 2] += jnp.sum(grad * n, axis=0, keepdims=True)
        r.vec[SHIFT + 1 : SHIFT + 2] += jnp.sum(grad, axis=0, keepdims=True)
        d = norm_back(n, inverse, r.gains[1:2], grad)
        r.dr[rows] = d
        r.dlow[rows] = d.astype(BF)


def back_down(r, c, lo, hi):
    @pl.loop(0, 2)
    def _(y):
        j = y * 2 + c
        t = dg(r.dlow[...], weight_down(r, y, c, lo, hi), 1, 0)
        r.gd[j, :, lo:hi] = (r.gd[j, :, lo:hi].astype(F32) * t).astype(BF)
        g = dg(r.dlow[...], r.act[j, :, lo:hi], 0, 0).astype(BF)
        r.down[:, :, y, c, :, lo:hi] = g.reshape(4, 2, 96, hi - lo)


def back_hidden(r):
    @pl.loop(0, 2)
    def _(i):
        rows = pl.ds(pl.multiple_of(256 * i, 256), 256)
        total = r.dr[rows]
        for j in range(4):
            total = total + dg(r.gd[j, rows], weight_up(r, j), 1, 1)
        r.acc[rows] = total


def back_first_norm(r):
    @pl.loop(0, 4)
    def _(i):
        rows = pl.ds(pl.multiple_of(i * 128, 128), 128)
        grad = r.acc[rows]
        n = r.n1[rows]
        r.vec[GAIN : GAIN + 1] += jnp.sum(grad * n, axis=0, keepdims=True)
        r.vec[SHIFT : SHIFT + 1] += jnp.sum(grad, axis=0, keepdims=True)
        d = norm_back(n, r.inv1[rows], r.gains[0:1], grad)
        r.dr[rows] = d
        r.dlow[rows] = d.astype(BF)


def grad_up(r):
    @pl.loop(0, 4)
    def _(j):
        for i in range(2):
            g = dg(r.hlow[:, 384 * i : 384 * i + 384], r.gd[j], 0, 0).astype(BF)
            for x in range(2):
                r.up[i, :, j, x] = g[:, x * 384 : (x + 1) * 384].reshape(2, 192, 384)


def set_grad(r, m, left, right):
    for i in range(2):
        g = dg(left[:, 384 * i : 384 * i + 384], right, 0, 0).astype(BF)
        r.sq[m, 2 * i : 2 * i + 2] = g.reshape(2, 2, 2, 48, 768)


def back_out(r):
    r.acc[...] = dg(r.dlow[...], weight(r, 6), 1, 0)
    set_grad(r, 6, r.dlow[...], r.mixed[...])


def back_level_two(r, hooks=None):
    @pl.loop(0, HEADS // 2)
    def _(p):
        at_steps(p, hooks)
        lanes = pair_lanes(p)
        scaled, scores = scores_of(r.q2[:, lanes], r.kp[0, :, lanes])
        grad = two_heads(r.acc[:, lanes].astype(BF))
        probs, grad_scores = softmax_back(
            scores, r.bias2[...], r.lse, p + HEADS // 2, grad, r.kp[1, :, lanes]
        )
        r.dpool[1][0:128, lanes] = dg(probs, grad, 0, 0).astype(BF).astype(F32)
        r.dpool[0][0:128, lanes] = dg(grad_scores, scaled, 0, 0).astype(BF).astype(F32)
        r.dq2[:, lanes] = (side_by_side(dg(grad_scores, r.kp[0, :, lanes], 1, 0)) * 0.125).astype(BF)

    r.dfirst[...] = (r.acc[...] + dg(r.dq2[...], weight(r, 5), 1, 0)).astype(BF)
    set_grad(r, 5, r.dq2[...], r.first[...])


def back_pool(r, i):
    r.dpool[i][128:136] = jnp.zeros((8, 768), F32)
    for l in range(6):
        lanes = slice(l * 128, l * 128 + 128)
        here = r.dpool[i][0:128, lanes]
        after = r.dpool[i][1:129, lanes]
        for t in range(5):
            term = here * r.kt[i, l, pl.ds(6 + t, 128, stride=STRIDE), :]
            at = POOL + 2 * t + i
            r.vec[at : at + 1, lanes] = jnp.sum(term, axis=0, keepdims=True)
        k = [r.pool[t, i : i + 1, lanes] for t in range(5)]
        r.kt[i, l, pl.ds(8, 128, stride=STRIDE), :] = k[2] * here
        r.kt[i, l, pl.ds(9, 128, stride=STRIDE), :] = k[3] * here
        r.kt[i, l, pl.ds(10, 128, stride=STRIDE), :] = k[4] * here + k[0] * after
        r.kt[i, l, pl.ds(11, 128, stride=STRIDE), :] = k[1] * after
    grad = jnp.concatenate([r.kt[i, l, 8:520].astype(BF) for l in range(6)], axis=1)
    finish_projection(r, 3 + i, grad)


def finish_projection(r, m, grad):
    r.dr[...] = r.dr[...] + dg(grad, weight(r, m), 1, 0)
    set_grad(r, m, grad, r.tokens[...])


def back_level_one(r, hooks=None):
    @pl.loop(0, HEADS)
    def _(step):
        at_steps(step, hooks)
        p, i = lax.div(step, 2), lax.rem(step, 2)
        lanes = pair_lanes(p)
        rows = pl.ds(pl.multiple_of(256 * i, 256), 256)
        cols = pl.ds(pl.multiple_of(128 * i, 128), 384)
        scaled, scores = scores_of(r.qkv[0, rows, lanes], r.qkv[1, cols, lanes])
        grad = two_heads(r.dfirst[rows, lanes])
        stacked = r.lse.at[pl.ds(pl.multiple_of(512 * i, 512), 512)]
        probs, grad_scores = softmax_back(scores, r.bias1[i], stacked, p, grad, r.qkv[2, cols, lanes])

        @pl.when(i == 0)
        def _():
            r.acc[:, 0:256] = jnp.zeros((512, 256), F32)

        r.acc[cols, 0:128] += dg(grad_scores, scaled, 0, 0)
        r.acc[cols, 128:256] += dg(probs, grad, 0, 0)
        dq = side_by_side(dg(grad_scores, r.qkv[1, cols, lanes], 1, 0)) * 0.125
        r.dqkv[0, rows, lanes] = dq.astype(BF)

        @pl.when(i == 1)
        def _():
            r.dqkv[1, :, lanes] = r.acc[:, 0:128].astype(BF)
            r.dqkv[2, :, lanes] = r.acc[:, 128:256].astype(BF)


class Refs:
    pass


ACTIVE = dict(
    qkv=((3, 512, 768), BF),
    kt=((2, 6, 528, 128), F32),
    kp=((2, 128, 768), BF),
    first=((512, 768), BF),
    q2=((512, 768), BF),
    mixed=((512, 768), BF),
    n1=((512, 768), F32),
    inv1=((512, 1), F32),
    hlow=((512, 768), BF),
    act=((4, 512, 768), BF),
    gd=((4, 512, 768), BF),
    dr=((512, 768), F32),
    acc=((512, 768), F32),
    dlow=((512, 768), BF),
    lse=((1024, 128), F32),
    bias1=((2, 256, 384), F32),
    bias2=((512, 128), F32),
)


def alias_late(r):
    r.dq2 = r.act.at[0]
    r.dfirst = r.act.at[1]
    r.dqkv = r.gd
    r.dpool = (r.n1.at[pl.ds(0, 136)], r.n1.at[pl.ds(256, 136)])


def slots(n):
    return dict(
        sq=((n, 7, 4, 48, 384), BF),
        up=((n, 4, 192, 384), BF),
        down=((n, 4, 96, 512), BF),
    )


BUFFERS = dict(
    tokens=((512, 768), BF),
    og=((512, 768), BF),
    gains=((2, 768), F32),
    shifts=((2, 768), F32),
    pool=((5, 2, 768), F32),
    shards=((7, 192, 96), BF),
    sq=(SQ, BF),
    up=(UP, BF),
    down=(DOWN, BF),
    s_sq=((7, 4, 2, 48, 768), BF),
    s_up=((2, 4, 2, 192, 384), BF),
    s_down=((4, 2, 2, 96, 768), BF),
    **{"r1_" + k: v for k, v in slots(2).items()},
    **{"r2_" + k: v for k, v in slots(1).items()},
    r3_sq=((3, 7, 48, 384), BF),
    pz=((3, 2, 2, 96, 256), BF),
    p2=((2, 96, 256), BF),
    p1=((96, 256), BF),
    b_sq=((7, 2, 48, 384), F32),
    b_up=((192, 384), F32),
    b_down=((96, 768), F32),
    vec=((16, 768), F32),
    r3_up=((3, 192, 384), BF),
    r3_down=((3, 96, 512), BF),
    vbuf=((10, 16, 768), F32),
    **ACTIVE,
)
SEMS = dict(
    load=18, swap=2, send=(N_GROUPS, 7), ag_r=(N_GROUPS, 10), rs_r=(N_GROUPS, 10), vs=7, vr=7, ends=5, endr=5
)


def layer_kernel(*refs):
    r = Refs()
    names = (
        ["length", "tokens_in", "og_in", "gains_in", "shifts_in", "pool_in"]
        + [f"shard{m}" for m in range(7)]
        + ["up_in", "down_in", "out", "din", "o_vec", "o_sq", "o_up", "o_down"]
        + list(BUFFERS)
        + list(SEMS)
    )
    for name, ref in zip(names, refs):
        setattr(r, name, ref)
    alias_late(r)
    me = Place()

    shards = [r.shards.at[m] for m in range(7)]
    pairs = [(getattr(r, f"shard{m}"), shards[m]) for m in range(7)]
    pairs += [
        (r.down_in, r.down.at[me.z, me.x, me.y, me.c]),
        (r.up_in, r.up.at[me.y, me.c, me.z, me.x]),
        (r.tokens_in, r.tokens),
        (r.pool_in, r.pool),
        (r.gains_in, r.gains),
        (r.shifts_in, r.shifts),
        (r.og_in, r.og),
    ]
    loads = [pltpu.make_async_copy(a, b, r.load.at[i]) for i, (a, b) in enumerate(pairs)]
    for cp in loads:
        cp.start()
    greet(me)
    weights = (r.sq, r.up, r.down)
    gat = Gather(me, weights, r.send, r.ag_r)
    sca = Scatter(
        me,
        weights,
        (r.s_sq, r.s_up, r.s_down),
        (r.r1_sq, r.r1_up, r.r1_down),
        (r.r2_sq, r.r2_up, r.r2_down),
        (r.r3_sq, r.r3_up, r.r3_down),
        (r.pz, r.p2, r.p1),
        r.send,
        r.rs_r,
    )

    loads[7].wait()
    gat.start(8)
    gat.go(6, 0, 1)
    for cp in loads[:7]:
        cp.wait()
    place_squares(me, shards, r.sq, r.act, r.swap.at[0], r.swap.at[1])
    for g in (0, 1, 9, 2, 3):
        gat.start(g)
    gat.step0(8)
    gat.step0(6)
    loads[8].wait()
    gat.start(4)
    gat.start(5)
    gat.go(6, 3, 4, 5)
    gat.start(7)
    set_masks(r, r.length[0])
    gat.step0(0)
    gat.step0(1)
    gat.step1(0)
    gat.step0(9)
    gat.step0(2)
    gat.step1(1)
    gat.step1(9)
    gat.step0(3)
    gat.step2(0)
    gat.step1(2)
    gat.step0(4)
    gat.step2(1)
    gat.step2(9)
    gat.step3(0)
    gat.step1(3)
    gat.step0(5)
    gat.step2(2)
    gat.step3(1)
    gat.step4(0)
    gat.step1(4)
    for cp in loads[9:]:
        cp.wait()
    gat.arrived(0)
    project(r, 0, 1)
    gat.step2(3)
    gat.step3(9)
    gat.step3(2)
    gat.step4(1)
    gat.step1(5)
    gat.step0(7)
    gat.step4(9)
    gat.arrived(1)
    project(r, 1, 2)
    gat.step1(6)
    gat.step2(4)
    gat.arrived(9)
    project(r, 2, 3)
    gat.step1(7)
    gat.step1(8)

    def ahead_a():
        gat.step4(2)
        gat.step2(5)

    level_one(r, {2: lambda: gat.step3(3), 4: ahead_a})
    gat.step3(4)
    gat.arrived(2)
    project_pool(r, 0)
    project_pool(r, 1)
    gat.step4(3)
    gat.step2(6)
    gat.arrived(3)

    def ahead_c():
        gat.step4(4)
        gat.step3(5)

    level_two(r, {3: ahead_c, 5: lambda: gat.step2(7)})
    gat.step4(5)
    first_norm(r)
    gat.arrived(4)
    gat.arrived(5)
    ffn_up(r, {1: lambda: gat.step3(6), 2: lambda: gat.step4(8), 3: lambda: gat.step4(6)})
    gat.step3(7)
    gat.arrived(8)
    ffn_down(r, 512, 768, True)
    gat.arrived(6)
    gat.step4(7)
    ffn_down(r, 0, 256, False)
    gat.arrived(7)
    ffn_down(r, 256, 512, False)
    second_norm(r)
    out = pltpu.make_async_copy(r.og, r.out, r.load.at[0])
    out.start()
    for g in range(N_GROUPS):
        gat.sent(g)

    def flush(src, dst):
        cp = pltpu.make_async_copy(src, dst, r.load.at[3 + len(pending)])
        cp.start()
        pending.append(cp)

    pending = []

    def give(g):
        kind, lo, hi = GROUPS[g]
        if kind == "u":
            r.b_up[lo:hi] = sca.finish(g)
            flush(r.b_up.at[lo:hi], r.o_up.at[lo:hi])
        else:
            r.b_down[:, lo:hi] = sca.finish(g)
            flush(r.b_down.at[:, lo:hi], r.o_down.at[:, lo:hi])

    def end_swap(g, incoming=False):
        _, lo, hi = GROUPS[g]
        b = r.b_sq.at[lo:hi, 1 - me.c if incoming else me.c]
        at = SQUARES.index(g)
        return rcopy(b, b, r.ends.at[at], r.endr.at[at], me.sibling())

    def end(g):
        _, lo, hi = GROUPS[g]
        r.b_sq[lo:hi, me.c] = sca.finish(g)
        end_swap(g).start()
        flush(r.b_sq.at[lo:hi, me.c], r.o_sq.at[lo:hi, me.c])

    def close(g):
        _, lo, hi = GROUPS[g]
        end_swap(g, True).wait_recv()
        flush(r.b_sq.at[lo:hi, 1 - me.c], r.o_sq.at[lo:hi, 1 - me.c])

    for g in (6, 8, 7):
        _, lo, hi = GROUPS[g]
        back_down(r, 1 - me.c, lo, hi)
        sca.start(g)
        back_down(r, me.c, lo, hi)
        sca.step1(g)
    sca.step2(6)
    back_hidden(r)
    grad_up(r)
    sca.start(4)
    sca.start(5)
    back_first_norm(r)
    sca.step2(7)
    sca.step3(6)
    back_out(r)
    sca.step1(4)
    sca.step1(5)
    back_level_two(r)
    sca.start(3)
    sca.step3(7)
    back_pool(r, 0)
    sca.step1(3)
    sca.step2(8)
    back_pool(r, 1)
    sca.start(2)
    total = VectorSum(me, r.vec, r.vbuf, r.vs, r.vr)
    total.send_z()

    back_level_one(
        r,
        {
            0: lambda: sca.step2(4),
            2: lambda: sca.step1(2),
            5: lambda: sca.step2(5),
            7: total.send_core,
            9: total.send_beside,
            11: lambda: sca.step3(4),
        },
    )
    finish_projection(r, 1, r.dqkv[1])
    sca.start(1)
    finish_projection(r, 2, r.dqkv[2])
    sca.start(9)
    sca.step1(1)
    sca.step2(3)
    finish_projection(r, 0, r.dqkv[0])
    sca.start(0)
    sca.step1(9)
    sca.step3(5)
    sca.step1(0)
    sca.step3(8)
    r.dlow[...] = r.dr[...].astype(BF)
    din = pltpu.make_async_copy(r.dlow, r.din, r.load.at[1])
    din.start()
    sca.step2(2)
    sca.step3(3)
    for g in (6, 7, 4, 5):
        give(g)
    sca.step2(1)
    sca.step3(2)
    sca.step2(9)
    give(8)
    sca.step3(1)
    sca.step2(0)
    end(3)
    sca.step3(9)
    sca.step3(0)
    end(2)
    close(3)
    close(2)
    total.take()
    vec_out = pltpu.make_async_copy(r.vec, r.o_vec, r.load.at[2])
    vec_out.start()
    end(1)
    end(9)
    end(0)
    for g in range(N_GROUPS):
        sca.sent(g)
    close(1)
    close(9)
    close(0)
    for g in SQUARES:
        end_swap(g).wait_send()
    for cp in [*pending, out, din, vec_out]:
        cp.wait()


def layer(length, tokens, og, gains, shifts, pool, squares, up, down):
    hbm = pl.BlockSpec(memory_space=pl.ANY)
    return pl.pallas_call(
        layer_kernel,
        out_shape=[
            jax.ShapeDtypeStruct((512, 768), BF),
            jax.ShapeDtypeStruct((512, 768), BF),
            jax.ShapeDtypeStruct((16, 768), F32),
            jax.ShapeDtypeStruct((7, 2, 48, 384), F32),
            jax.ShapeDtypeStruct((192, 384), F32),
            jax.ShapeDtypeStruct((96, 768), F32),
        ],
        in_specs=[pl.BlockSpec(memory_space=pltpu.SMEM)] + [hbm] * 14,
        out_specs=[hbm] * 6,
        scratch_shapes=[pltpu.VMEM(*s) for s in BUFFERS.values()]
        + [pltpu.SemaphoreType.DMA(s if isinstance(s, tuple) else (s,)) for s in SEMS.values()],
        compiler_params=pltpu.CompilerParams(
            collective_id=0, has_side_effects=True, vmem_limit_bytes=VMEM_LIMIT
        ),
    )(length, tokens, og, gains, shifts, pool, *squares, up, down)


VMEM_LIMIT = 63 * 2**20


def ending_kernel(*refs):
    o_act, o_din, o_up, o_down = refs[6], refs[7], refs[15], refs[16]
    o_sq = refs[8:15]
    o_gain, o_shift, o_pool, vec, sq, turned, sem = refs[17:]
    copies = [
        pltpu.make_async_copy(a, b, sem.at[i])
        for i, (a, b) in enumerate(zip(refs[:6], (o_act, o_din, vec, sq, o_up, o_down)))
    ]
    for i in (3, 2, 0, 1, 4, 5):
        copies[i].start()
    core = lax.rem(lax.axis_index("dp"), 2)
    mine = pl.ds(pl.multiple_of(core * 192, 8), 192)
    copies[3].wait()
    for m in range(7):
        turned[...] = jnp.transpose(sq[m].reshape(96, 384))
        o_sq[m][...] = turned[mine, :]
    copies[2].wait()
    o_gain[...] = vec[GAIN : GAIN + 2]
    o_shift[...] = vec[SHIFT : SHIFT + 2]
    for t in range(5):
        o_pool[t] = vec[POOL + 2 * t : POOL + 2 * t + 2]
    for i in (0, 1, 4, 5):
        copies[i].wait()


def ending(*parts):
    vmem = pl.BlockSpec(memory_space=pltpu.VMEM)
    shapes = [((512, 768), BF)] * 2 + [((192, 96), F32)] * 7 + [((192, 384), F32), ((96, 768), F32)]
    shapes += [((2, 768), F32)] * 2 + [((5, 2, 768), F32)]
    return pl.pallas_call(
        ending_kernel,
        out_shape=[jax.ShapeDtypeStruct(*s) for s in shapes],
        in_specs=[pl.BlockSpec(memory_space=pl.ANY)] * 6,
        out_specs=[vmem] * len(shapes),
        scratch_shapes=[
            pltpu.VMEM((16, 768), F32),
            pltpu.VMEM((7, 2, 48, 384), F32),
            pltpu.VMEM((384, 96), F32),
            pltpu.SemaphoreType.DMA((6,)),
        ],
        compiler_params=pltpu.CompilerParams(vmem_limit_bytes=VMEM_LIMIT),
    )(*parts)


def local_kernels(
    tokens,
    doc_lengths,
    w_query,
    w_key,
    w_value,
    w_query2,
    w_key2,
    w_value2,
    w_out,
    w_up,
    w_down,
    norm_gains,
    norm_shifts,
    pool_kernels,
    out_grad,
):
    squares = (w_query, w_key, w_value, w_key2, w_value2, w_query2, w_out)
    ends = layer(
        doc_lengths,
        tokens,
        out_grad,
        norm_gains,
        norm_shifts,
        pool_kernels.transpose(1, 0, 2),
        squares,
        w_up,
        w_down.T,
    )
    act, din, g_q, g_k, g_v, g_k2, g_v2, g_q2, g_out, g_up, g_down, gain, shift, pools = ending(*ends)
    return (
        act,
        din,
        g_q,
        g_k,
        g_v,
        g_q2,
        g_k2,
        g_v2,
        g_out,
        g_up,
        g_down.T,
        gain,
        shift,
        pools.transpose(1, 0, 2),
    )


def local(
    tokens,
    doc_lengths,
    w_query,
    w_key,
    w_value,
    w_query2,
    w_key2,
    w_value2,
    w_out,
    w_up,
    w_down,
    norm_gains,
    norm_shifts,
    pool_kernels,
    out_grad,
):
    shards = (w_query, w_key, w_value, w_query2, w_key2, w_value2, w_out, w_up, w_down)
    forward_weights = gather_first(shards)
    (
        full_query,
        full_key,
        full_value,
        full_query2,
        full_key2,
        full_value2,
        full_out,
        full_up,
        full_down,
    ) = forward_weights
    seq_rows = tokens.shape[0]
    length = doc_lengths[0]
    positions = jnp.arange(seq_rows, dtype=jnp.int32)
    padding = positions >= length
    allowed_one = (jnp.abs(positions[:, None] - positions[None, :]) <= WIN) & (
        padding[:, None] == padding[None, :]
    )
    pooled_at = positions[: seq_rows // STRIDE] * STRIDE
    allowed_two = (jnp.abs(positions[:, None] - pooled_at[None, :]) <= PWIN // 2) & (
        padding[:, None] == (pooled_at >= length)[None, :]
    )
    score_scale = 1.0 / math.sqrt(HD)
    query = matmul(tokens, full_query).astype(jnp.bfloat16)
    keys = matmul(tokens, full_key).astype(jnp.bfloat16)
    values = matmul(tokens, full_value).astype(jnp.bfloat16)
    key_two = matmul(tokens, full_key2)
    value_two = matmul(tokens, full_value2)
    key_pool_f, pool_key_back = jax.vjp(pool_rows, key_two, pool_kernels[0])
    value_pool_f, pool_value_back = jax.vjp(pool_rows, value_two, pool_kernels[1])
    key_pool = key_pool_f.astype(jnp.bfloat16)
    value_pool = value_pool_f.astype(jnp.bfloat16)
    first_f, log_one = level_forward(query, keys, values, allowed_one, score_scale)
    first = first_f.astype(jnp.bfloat16)
    query_two = matmul(first, full_query2).astype(jnp.bfloat16)
    second, log_two = level_forward(query_two, key_pool, value_pool, allowed_two, score_scale)
    mixed = (first.astype(jnp.float32) + second).astype(jnp.bfloat16)
    branch = matmul(mixed, full_out)
    hidden, norm_one_back = jax.vjp(
        layer_norm, tokens.astype(jnp.float32) + branch, norm_gains[0], norm_shifts[0]
    )
    hidden_low = hidden.astype(jnp.bfloat16)
    upper = matmul(hidden_low, full_up)
    activated_f, gelu_back = jax.vjp(gelu_tanh, upper)
    activated = activated_f.astype(jnp.bfloat16)
    resid_two = hidden + matmul(activated, full_down)
    result, norm_two_back = jax.vjp(layer_norm, resid_two, norm_gains[1], norm_shifts[1])
    activations = result.astype(jnp.bfloat16)
    back_weights = gather_second(shards)
    (
        back_query,
        back_key,
        back_value,
        back_query2,
        back_key2,
        back_value2,
        back_out,
        back_up,
        back_down,
    ) = back_weights
    d_resid_two, d_gain_two, d_shift_two = norm_two_back(out_grad.astype(jnp.float32))
    d_ffn = d_resid_two.astype(jnp.bfloat16)
    grad_down = inner_rows(activated, d_ffn)
    d_upper = gelu_back(outer_cols(d_ffn, back_down))[0].astype(jnp.bfloat16)
    grad_up = inner_rows(hidden_low, d_upper)
    d_hidden = d_resid_two + outer_cols(d_upper, back_up)
    d_resid_one, d_gain_one, d_shift_one = norm_one_back(d_hidden)
    d_branch = d_resid_one.astype(jnp.bfloat16)
    grad_out = inner_rows(mixed, d_branch)
    d_mixed = outer_cols(d_branch, back_out)
    d_query_two_f, d_key_pool_f, d_value_pool_f = level_backward(
        query_two,
        key_pool,
        value_pool,
        allowed_two,
        score_scale,
        log_two,
        d_mixed.astype(jnp.bfloat16),
    )
    d_query_two = d_query_two_f.astype(jnp.bfloat16)
    d_key_pool = d_key_pool_f.astype(jnp.bfloat16)
    d_value_pool = d_value_pool_f.astype(jnp.bfloat16)
    grad_query2 = inner_rows(first, d_query_two)
    d_first = (d_mixed + outer_cols(d_query_two, back_query2)).astype(jnp.bfloat16)
    d_query_f, d_keys_f, d_values_f = level_backward(
        query, keys, values, allowed_one, score_scale, log_one, d_first
    )
    d_query = d_query_f.astype(jnp.bfloat16)
    d_keys = d_keys_f.astype(jnp.bfloat16)
    d_values = d_values_f.astype(jnp.bfloat16)
    d_key_two_f, d_pool_key = pool_key_back(d_key_pool.astype(jnp.float32))
    d_value_two_f, d_pool_value = pool_value_back(d_value_pool.astype(jnp.float32))
    d_key_two = d_key_two_f.astype(jnp.bfloat16)
    d_value_two = d_value_two_f.astype(jnp.bfloat16)
    grad_query = inner_rows(tokens, d_query)
    grad_key = inner_rows(tokens, d_keys)
    grad_value = inner_rows(tokens, d_values)
    grad_key2 = inner_rows(tokens, d_key_two)
    grad_value2 = inner_rows(tokens, d_value_two)
    d_tokens = (
        d_resid_one
        + outer_cols(d_query, back_query)
        + outer_cols(d_keys, back_key)
        + outer_cols(d_values, back_value)
    )
    d_tokens = d_tokens + outer_cols(d_key_two, back_key2) + outer_cols(d_value_two, back_value2)
    grads_all = (
        grad_query,
        grad_key,
        grad_value,
        grad_query2,
        grad_key2,
        grad_value2,
        grad_out,
        grad_up,
        grad_down,
    )
    owned = reduce_columns_first(grads_all)
    gain_stack = jnp.stack([d_gain_one, d_gain_two])
    shift_stack = jnp.stack([d_shift_one, d_shift_two])
    pool_stack = jnp.stack([d_pool_key, d_pool_value])
    vector_sums = lax.psum((gain_stack, shift_stack, pool_stack), ("dp", "fsdp"))
    return (
        activations,
        d_tokens.astype(jnp.bfloat16),
        owned[0],
        owned[1],
        owned[2],
        owned[3],
        owned[4],
        owned[5],
        owned[6],
        owned[7],
        owned[8],
        vector_sums[0],
        vector_sums[1],
        vector_sums[2],
    )


def solution(mesh):
    fits = mesh.shape["dp"] == 4 and mesh.shape["fsdp"] == 8
    return jax.shard_map(
        local_kernels if fits else local,
        mesh=mesh,
        in_specs=(
            P(("dp", "fsdp"), None),
            P(("dp", "fsdp")),
            P("dp", "fsdp"),
            P("dp", "fsdp"),
            P("dp", "fsdp"),
            P("dp", "fsdp"),
            P("dp", "fsdp"),
            P("dp", "fsdp"),
            P("dp", "fsdp"),
            P("dp", "fsdp"),
            P("dp", "fsdp"),
            P(),
            P(),
            P(),
            P(("dp", "fsdp"), None),
        ),
        out_specs=(
            P(("dp", "fsdp"), None),
            P(("dp", "fsdp"), None),
            P("dp", "fsdp"),
            P("dp", "fsdp"),
            P("dp", "fsdp"),
            P("dp", "fsdp"),
            P("dp", "fsdp"),
            P("dp", "fsdp"),
            P("dp", "fsdp"),
            P("dp", "fsdp"),
            P("dp", "fsdp"),
            P(),
            P(),
            P(),
        ),
        check_vma=False,
    )
```
